32 devices in a mesh: dp: 8 (over z, y), mp: 4 (over x, core).
Axes of the slice: x: 2, y: 2, z: 4, core: 2. Of those that a mesh axis runs over, the one named last changes fastest.
Arguments:
- tokens: bfloat16 [8192, 1024], P(('dp', 'mp')), may hold values from -0.1875 to 0.1875
- seq_lengths: int32 [8, 4], P('dp'), may hold values from 1 to 682, as said below
- w_query: bfloat16 [1024, 1024], P(None, 'mp'), may hold values from -0.1875 to 0.1875
- w_key: bfloat16 [1024, 1024], P(None, 'mp'), may hold values from -0.1875 to 0.1875
- w_value: bfloat16 [1024, 1024], P(None, 'mp'), may hold values from -0.1875 to 0.1875
- w_out: bfloat16 [1024, 1024], P('mp'), may hold values from -0.1875 to 0.1875
- qk_scale: float32 [1024], P('mp'), may hold values from 0.7 to 1.6
- attn_rate: float32 [1024], replicated, may hold values from 0.15 to 0.6
- w_up: bfloat16 [1024, 4096], P(None, 'mp'), may hold values from -0.1875 to 0.1875
- w_gate: bfloat16 [1024, 4096], P(None, 'mp'), may hold values from -0.1875 to 0.1875
- up_scale: float32 [4096], P('mp'), may hold values from 0.5 to 2
- gate_scale: float32 [4096], P('mp'), may hold values from 0.5 to 2
- w_down: bfloat16 [4096, 1024], P('mp'), may hold values from -0.09375 to 0.09375
- mlp_rate: float32 [1024], replicated, may hold values from 0.15 to 0.6
- out_grad: bfloat16 [8192, 1024], P(('dp', 'mp')), may hold values from -6 to 6
Outputs:
- block_out: float32 [8192, 1024], P(('dp', 'mp'))
- token_grad: float32 [8192, 1024], P(('dp', 'mp'))
- grad_query: float32 [1024, 1024], P('dp', 'mp')
- grad_key: float32 [1024, 1024], P('dp', 'mp')
- grad_value: float32 [1024, 1024], P('dp', 'mp')
- grad_w_out: float32 [1024, 1024], P('mp', 'dp')
- grad_qk_scale: float32 [1024], P(('mp', 'dp'))
- grad_attn_rate: float32 [1024], P('dp')
- grad_up: float32 [1024, 4096], P('dp', 'mp')
- grad_gate: float32 [1024, 4096], P('dp', 'mp')
- grad_up_scale: float32 [4096], P(('mp', 'dp'))
- grad_gate_scale: float32 [4096], P(('mp', 'dp'))
- grad_down: float32 [4096, 1024], P('mp', 'dp')
- grad_mlp_rate: float32 [1024], P('dp')
The draws below stay inside these ranges and needn't reach their ends.
Inputs may be any that keep to these rules, and one draw needn't show every extreme that they name: `seq_lengths`: in each group the first 3 sequences hold at least one token each and together 7 * 128 - 2 * 1024 // 3 tokens; the last one holds exactly 682 tokens; the remaining slots of the group are padding.
All inputs are finite; a program needn't handle non-finite values.
Results may differ from the reference program's by a relative error of at most 0.015.
Values may be sent and summed in bfloat16 or wider, within the bound.
No kernel may reach another device: no remote copies, remote signals or barrier semaphores. Data moves between devices by JAX's collectives and lax.ppermute only.
A program may use at most 128 MiB of HBM per device.

```python
import math
import jax
import jax.numpy as jnp
from jax import lax

D = 1024
HEADS = 16
HD = 64
FF = 4096
TOK = 1024
SEQS = 4
TOKENS = 8192
N_DP = 8


def draw_seq_lengths(key, part):
    key = jax.random.fold_in(key, 11)
    longest = TOK * 2 // 3
    others = TOK * 7 // 8 - longest
    spare_rows = others - (SEQS - 1)
    cuts = jnp.sort(jax.random.randint(key, (N_DP, SEQS - 2), 0, spare_rows + 1), axis=1)
    edges = jnp.concatenate([jnp.zeros((N_DP, 1), jnp.int32), cuts.astype(jnp.int32), jnp.full((N_DP, 1), spare_rows, jnp.int32)], axis=1)
    leading = edges[:, 1:] - edges[:, :-1] + 1
    return jnp.concatenate([leading, jnp.full((N_DP, 1), longest, jnp.int32)], axis=1).astype(jnp.int32)


def strengthened(values, key, source, target, blocks, factor):
    owner, partner = [(jnp.arange(values.shape[dim]) // (values.shape[dim] // blocks)).reshape([-1 if axis == dim else 1 for axis in range(values.ndim)]) for dim in (source, target)]
    chosen = jax.random.permutation(key, blocks)[partner]
    strong = (owner == chosen) | (owner == (partner + blocks // 2) % blocks)
    return jnp.where(strong, factor * values, values)


def levels(stream_key, shape, split, smallest, largest):
    def one(axis_at, shards_of):
        draws = jax.random.uniform(jax.random.fold_in(jax.random.fold_in(stream_key, 6), axis_at), (shards_of,), jnp.float32, smallest / len(split), largest / len(split))
        return jnp.repeat(jnp.exp(draws), shape[axis_at] // shards_of).reshape((-1,) + (1,) * (len(shape) - axis_at - 1))

    factor_of = one(*split[0])
    for cut in split[1:]:
        factor_of = factor_of * one(*cut)
    return factor_of


def gaussian(key, shape, deviation, most, pieces=(), kind=jnp.bfloat16):
    entries = jax.random.normal(key, shape, jnp.float32) * deviation
    if len(pieces) > 0:
        entries = levels(key, shape, pieces, -0.22, 0.18) * entries
    return jnp.clip(entries, min=-most, max=most).astype(kind)


def bell_draw_with(key, shape, scale, most, cuts, heavy, kind=jnp.bfloat16):
    array = scale * jax.random.normal(key, shape, jnp.float32)
    if cuts:
        array = array * levels(key, shape, cuts, -0.22, 0.18)
    return jnp.clip(strengthened(array, jax.random.fold_in(key, 3), *heavy), -most, most).astype(kind)


def setup_inputs(seed: int = 0) -> dict:
    streams_of = jax.random.split(jax.random.key(seed), 16)
    tokens = gaussian(streams_of[0], (TOKENS, D), D ** -0.5, 0.1875, ((0, 32),))
    seq_lengths = draw_seq_lengths(jax.random.fold_in(streams_of[15], 71), 0)
    w_query = gaussian(streams_of[2], (D, D), D ** -0.5, 0.1875, ((1, 4),))
    w_key = gaussian(streams_of[3], (D, D), D ** -0.5, 0.1875, ((1, 4),))
    w_value = gaussian(streams_of[4], (D, D), D ** -0.5, 0.1875, ((1, 4),))
    w_out = gaussian(streams_of[5], (D, D), D ** -0.5, 0.1875, ((0, 4),))
    qk_scale = jnp.clip(jnp.exp(math.log(1.6) - 0.82667861 * jax.random.uniform(streams_of[6], (D,), jnp.float32) ** levels(streams_of[6], (D,), ((0, 4),), -0.2, 0.2)), 0.7, 1.6)
    attn_rate = jnp.clip(jnp.exp(jax.random.uniform(streams_of[7], (D,), jnp.float32, math.log(0.15), math.log(0.6))), 0.15, 0.6)
    w_up = gaussian(streams_of[8], (D, FF), D ** -0.5, 0.1875, ((1, 4),))
    w_gate = gaussian(streams_of[9], (D, FF), D ** -0.5, 0.1875, ((1, 4),))
    up_scale = jnp.clip(jnp.exp(math.log(2.0) - 1.3862944 * jax.random.uniform(streams_of[10], (FF,), jnp.float32) ** levels(streams_of[10], (FF,), ((0, 4),), -0.2, 0.2)), 0.5, 2.0)
    gate_scale = jnp.clip(jnp.exp(math.log(2.0) - 1.3862944 * jax.random.uniform(streams_of[11], (FF,), jnp.float32) ** levels(streams_of[11], (FF,), ((0, 4),), -0.2, 0.2)), 0.5, 2.0)
    w_down = gaussian(streams_of[12], (FF, D), FF ** -0.5, 0.09375, ((0, 4),))
    mlp_rate = jnp.clip(jnp.exp(jax.random.uniform(streams_of[13], (D,), jnp.float32, math.log(0.15), math.log(0.6))), 0.15, 0.6)
    out_grad = bell_draw_with(streams_of[14], (TOKENS, D), 1.0, 6.0, ((0, 32),), (0, 1, 32, 2.75))
    return {"tokens": tokens, "seq_lengths": seq_lengths, "w_query": w_query, "w_key": w_key, "w_value": w_value, "w_out": w_out, "qk_scale": qk_scale, "attn_rate": attn_rate, "w_up": w_up, "w_gate": w_gate, "up_scale": up_scale, "gate_scale": gate_scale, "w_down": w_down, "mlp_rate": mlp_rate, "out_grad": out_grad}


@jax.custom_vjp
def low(v):
    return lax.optimization_barrier(v.astype(jnp.bfloat16)).astype(jnp.float32)

@jax.custom_vjp
def low_back(v):
    return v

def low_keep(v):
    return (low(v), None)

def low_pass(kept, grad):
    return (grad,)

def back_keep(v):
    return (v, None)

def back_low(kept, grad):
    return (low(grad),)
low.defvjp(low_keep, low_pass)
low_back.defvjp(back_keep, back_low)
eps = 1e-06
highest = lax.Precision.HIGHEST

def unit_rows(values):
    return values * lax.rsqrt(lax.optimization_barrier(jnp.sum(values * values, axis=-1, keepdims=True)) + eps)

def layout(lengths, total_rows):
    seq_ends = jnp.cumsum(lengths).astype(jnp.int32)
    row_ids = jnp.arange(total_rows, dtype=jnp.int32)
    segment = lax.optimization_barrier(jnp.sum((row_ids[:, None] >= seq_ends[None, :]).astype(jnp.int32), axis=1)).astype(jnp.int32)
    starts = jnp.concatenate([jnp.zeros((1,), jnp.int32), seq_ends])
    labels = jnp.arange(starts.shape[0], dtype=jnp.int32)
    first_row = lax.optimization_barrier(jnp.sum(jnp.where(segment[:, None] == labels[None, :], starts[None, :], 0), axis=1)).astype(jnp.int32)
    return (segment, row_ids - first_row)

def rotate(values, position):
    half_dim = values.shape[-1] // 2
    frequency = jnp.exp(jnp.arange(half_dim, dtype=jnp.float32) * (-2.0 * math.log(10000.0) / values.shape[-1]))
    angles = position.astype(jnp.float32)[:, None] * frequency[None, :]
    cosine_table = jnp.cos(angles)[:, None, :]
    sine_table = jnp.sin(angles)[:, None, :]
    first_half = values[..., :half_dim]
    second_half = values[..., half_dim:]
    return jnp.concatenate([first_half * cosine_table - second_half * sine_table, second_half * cosine_table + first_half * sine_table], axis=-1)

def group_block(x_group, segment, position, weights):
    w_q, w_k, w_v, w_o, s_qk, r_attn, w_u, w_g, s_up, s_gate, w_d, r_mlp = weights
    head_shape = (TOK, HEADS, HD)
    q_proj = low_back(jnp.dot(x_group, w_q, precision=highest))
    k_proj = low_back(jnp.dot(x_group, w_k, precision=highest))
    v_round = low_back(low(jnp.dot(x_group, w_v, precision=highest))).reshape(head_shape)
    gain_heads = s_qk.reshape(HEADS, HD)
    q_unit = low(gain_heads * unit_rows(rotate(q_proj.reshape(head_shape), position)))
    k_unit = low(gain_heads * unit_rows(rotate(k_proj.reshape(head_shape), position)))
    row_ids = jnp.arange(TOK, dtype=jnp.int32)
    linked = (segment[:, None] == segment[None, :]) & (segment[:, None] < SEQS) & (row_ids[None, :] <= row_ids[:, None])
    allowed = linked | (row_ids[None, :] == row_ids[:, None])
    scores = math.sqrt(HD) * jnp.einsum('qhd,khd->hqk', q_unit, k_unit, precision=highest)
    scores = low_back(jnp.where(allowed[None], scores, -1e+30))
    shifted = jnp.exp(scores - lax.optimization_barrier(jnp.max(scores, axis=-1, keepdims=True)))
    probs = shifted / lax.optimization_barrier(jnp.sum(shifted, axis=-1, keepdims=True))
    head_out = jnp.einsum('hqk,khd->qhd', low(probs), v_round, precision=highest).reshape(TOK, D)
    head_out = low_back(low(head_out))
    attn_sum = low_back(jnp.dot(head_out, w_o, precision=highest))
    h_attn = unit_rows(attn_sum)
    h_one = unit_rows(x_group + r_attn * (h_attn - x_group))
    mlp_input = low(h_one)
    up_proj = low_back(jnp.dot(mlp_input, w_u, precision=highest))
    gate_proj = low_back(jnp.dot(mlp_input, w_g, precision=highest))
    up_scaled = s_up * up_proj
    gate_scaled = s_gate * math.sqrt(D) * gate_proj
    hidden = low(up_scaled * (gate_scaled * jax.nn.sigmoid(gate_scaled)))
    mlp_sum = low_back(jnp.dot(hidden, w_d, precision=highest))
    h_mlp = unit_rows(mlp_sum)
    return unit_rows(h_one + r_mlp * (h_mlp - h_one))

def reference(tokens, seq_lengths, w_query, w_key, w_value, w_out, qk_scale, attn_rate, w_up, w_gate, up_scale, gate_scale, w_down, mlp_rate, out_grad):
    segments, positions = jax.vmap(lambda lengths: layout(lengths, TOK))(seq_lengths)
    floats = tuple((member.astype(jnp.float32) for member in (tokens, w_query, w_key, w_value, w_out, qk_scale, attn_rate, w_up, w_gate, up_scale, gate_scale, w_down, mlp_rate)))

    def forward(x_all, *weights):
        x_groups = x_all.reshape(N_DP, TOK, D)

        def one_group(items):
            return group_block(items[0], items[1], items[2], weights)
        result = lax.map(jax.checkpoint(one_group), (x_groups, segments, positions))
        return result.reshape(N_DP * TOK, D)
    block_out, pullback = jax.vjp(forward, *floats)
    grads = pullback(out_grad.astype(jnp.float32))
    return (block_out, grads[0], grads[1], grads[2], grads[3], grads[4], grads[5], grads[6], grads[7], grads[8], grads[9], grads[10], grads[11], grads[12])
```

```python
import math

import jax
import jax.numpy as jnp
from jax import lax
from jax.sharding import PartitionSpec as P

HD = 64


eps = 1e-06


def unit_rows(values):
    inverse = lax.rsqrt(jnp.sum(values * values, axis=-1, keepdims=True) + eps)
    return (values * inverse, inverse)


def unit_back(grad_in, normed, inverse):
    return (grad_in - normed * jnp.sum(normed * grad_in, axis=-1, keepdims=True)) * inverse


def layout(lengths, total_rows):
    seq_ends = jnp.cumsum(lengths)
    row_ids = jnp.arange(total_rows, dtype=jnp.int32)
    segment = jnp.sum((row_ids[:, None] >= seq_ends[None, :]).astype(jnp.int32), axis=1)
    starts = jnp.concatenate([jnp.zeros((1,), jnp.int32), seq_ends])
    labels = jnp.arange(starts.shape[0], dtype=jnp.int32)
    first_row = jnp.sum(jnp.where(segment[:, None] == labels[None, :], starts[None, :], 0), axis=1)
    return (segment, row_ids - first_row)


def rope_tables(position, head_size):
    half_dim = head_size // 2
    frequency = jnp.exp(
        jnp.arange(half_dim, dtype=jnp.float32) * (-2.0 * math.log(10000.0) / head_size)
    )
    angles = position.astype(jnp.float32)[:, None] * frequency[None, :]
    return (jnp.cos(angles)[:, None, :], jnp.sin(angles)[:, None, :])


def rotate(values, cosine_table, sine_table):
    half_dim = values.shape[-1] // 2
    first_half = values[..., :half_dim]
    second_half = values[..., half_dim:]
    return jnp.concatenate(
        [
            first_half * cosine_table - second_half * sine_table,
            second_half * cosine_table + first_half * sine_table,
        ],
        axis=-1,
    )


def pair_mask(segment, begin_row, stop_row, seq_count):
    query_ids = jnp.arange(begin_row, stop_row, dtype=jnp.int32)
    key_ids = jnp.arange(stop_row, dtype=jnp.int32)
    query_seg = segment[begin_row:stop_row][:, None]
    linked = (
        (query_seg == segment[None, :stop_row])
        & (query_seg < seq_count)
        & (key_ids[None, :] <= query_ids[:, None])
    )
    return linked | (key_ids[None, :] == query_ids[:, None])


def block_scores(queries, keys_all, segment, seq_count, begin_row, stop_row, score_root):
    scores = score_root * jnp.einsum(
        "qhd,khd->hqk",
        queries[begin_row:stop_row],
        keys_all[:stop_row],
        preferred_element_type=jnp.float32,
    )
    return jnp.where(pair_mask(segment, begin_row, stop_row, seq_count)[None], scores, -1e30)


def attend(queries, keys_all, values_all, segment, seq_count, block_rows, score_root):
    outputs = []
    log_parts = []
    for begin_row in range(0, queries.shape[0], block_rows):
        stop_row = begin_row + block_rows
        scores = block_scores(
            queries, keys_all, segment, seq_count, begin_row, stop_row, score_root
        )
        highest = jnp.max(scores, axis=-1, keepdims=True)
        shifted = jnp.exp(scores - highest)
        summed = jnp.sum(shifted, axis=-1, keepdims=True)
        weights_low = (shifted / summed).astype(jnp.bfloat16)
        outputs.append(
            jnp.einsum(
                "hqk,khd->qhd",
                weights_low,
                values_all[:stop_row],
                preferred_element_type=jnp.float32,
            )
        )
        log_parts.append(highest + jnp.log(summed))
    return (jnp.concatenate(outputs, axis=0), jnp.concatenate(log_parts, axis=1))


def attend_back(
    queries,
    keys_all,
    values_all,
    grad_heads,
    log_totals,
    segment,
    seq_count,
    block_rows,
    score_root,
):
    query_parts = []
    grad_keys = jnp.zeros(keys_all.shape, jnp.float32)
    grad_values = jnp.zeros(values_all.shape, jnp.float32)
    for begin_row in range(0, queries.shape[0], block_rows):
        stop_row = begin_row + block_rows
        scores = block_scores(
            queries, keys_all, segment, seq_count, begin_row, stop_row, score_root
        )
        probs = jnp.exp(scores - log_totals[:, begin_row:stop_row])
        grad_probs = jnp.einsum(
            "qhd,khd->hqk",
            grad_heads[begin_row:stop_row],
            values_all[:stop_row],
            preferred_element_type=jnp.float32,
        )
        row_dot = jnp.sum(probs * grad_probs, axis=-1, keepdims=True)
        grad_scores = (probs * (grad_probs - row_dot)).astype(jnp.bfloat16)
        query_parts.append(
            score_root
            * jnp.einsum(
                "hqk,khd->qhd", grad_scores, keys_all[:stop_row], preferred_element_type=jnp.float32
            )
        )
        grad_keys = grad_keys.at[:stop_row].add(
            score_root
            * jnp.einsum(
                "hqk,qhd->khd",
                grad_scores,
                queries[begin_row:stop_row],
                preferred_element_type=jnp.float32,
            )
        )
        grad_values = grad_values.at[:stop_row].add(
            jnp.einsum(
                "hqk,qhd->khd",
                probs.astype(jnp.bfloat16),
                grad_heads[begin_row:stop_row],
                preferred_element_type=jnp.float32,
            )
        )
    return (jnp.concatenate(query_parts, axis=0), grad_keys, grad_values.astype(jnp.bfloat16))


def contract_rows(left_side, right_side):
    return lax.dot_general(
        left_side, right_side, (((0,), (0,)), ((), ())), preferred_element_type=jnp.float32
    )


def contract_cols(left_side, right_side):
    return lax.dot_general(
        left_side, right_side, (((1,), (1,)), ((), ())), preferred_element_type=jnp.float32
    )


def swap(values, axis, bit):
    size = lax.axis_size(axis)
    return lax.ppermute(values, axis, [(i, i ^ bit) for i in range(size)])


def bits_of(axis):
    size = lax.axis_size(axis)
    out = []
    bit = 1
    while bit < size:
        out.append(bit)
        bit *= 2
    return out


def gather_rows(values):
    slots = {0: values}
    for bit in reversed(bits_of("mp")):
        for slot in list(slots):
            slots[slot ^ bit] = swap(slots[slot], "mp", bit)
    count = len(slots)
    stacked = jnp.stack([slots[i] for i in range(count)])
    order = lax.axis_index("mp") ^ jnp.arange(count, dtype=jnp.int32)
    return stacked[order].reshape((-1,) + values.shape[1:])


def scatter_rows(values):
    count = lax.axis_size("mp")
    parts = values.reshape((count, -1) + values.shape[1:])
    order = lax.axis_index("mp") ^ jnp.arange(count, dtype=jnp.int32)
    parts = parts[order]
    slots = [parts[i] for i in range(count)]
    for bit in bits_of("mp"):
        kept = {}
        sent = jnp.concatenate([slots[i].astype(jnp.bfloat16) for i in range(len(slots)) if i % 2 == 1], axis=0)
        got = jnp.split(swap(sent, "mp", bit), len(slots) // 2, axis=0)
        slots = [slots[2 * i] + got[i].astype(jnp.float32) for i in range(len(slots) // 2)]
    return slots[0]


def scatter_groups(values, dim):
    count = lax.axis_size("dp")
    shape = values.shape
    me = lax.axis_index("dp")
    parts = jnp.moveaxis(
        values.reshape(shape[:dim] + (count, shape[dim] // count) + shape[dim + 1 :]), dim, 0
    )
    for bit in bits_of("dp"):
        mine = (me // bit) % 2
        parts = parts.reshape((parts.shape[0] // 2, 2) + parts.shape[1:])
        sent = lax.dynamic_index_in_dim(parts, 1 - mine, 1, keepdims=False)
        kept = lax.dynamic_index_in_dim(parts, mine, 1, keepdims=False)
        wire = sent.astype(jnp.bfloat16) if values.ndim > 1 else sent
        parts = kept + swap(wire, "dp", bit).astype(jnp.float32)
    return parts[0]


def shards(
    tokens,
    seq_lengths,
    w_query,
    w_key,
    w_value,
    w_out,
    qk_scale,
    attn_rate,
    w_up,
    w_gate,
    up_scale,
    gate_scale,
    w_down,
    mlp_rate,
    out_grad,
):
    local_rows = tokens.shape[0]
    group_rows = local_rows * lax.axis_size("mp")
    model_width = tokens.shape[1]
    head_size = HD
    local_width = w_query.shape[1]
    local_heads = local_width // head_size
    seq_count = seq_lengths.shape[1]
    segment, position = layout(seq_lengths[0], group_rows)
    block_rows = 512
    score_root = math.sqrt(head_size)
    width_root = math.sqrt(model_width)
    cosine_table, sine_table = rope_tables(position, head_size)
    head_shape = (group_rows, local_heads, head_size)
    gathered = gather_rows(tokens)
    w_joined = jnp.concatenate([w_query, w_key, w_value], axis=1)
    projected = jnp.dot(gathered, w_joined, preferred_element_type=jnp.float32)
    q_rot = rotate(projected[:, :local_width].reshape(head_shape), cosine_table, sine_table)
    k_rot = rotate(
        projected[:, local_width : 2 * local_width].reshape(head_shape), cosine_table, sine_table
    )
    v_round = projected[:, 2 * local_width :].astype(jnp.bfloat16).reshape(head_shape)
    gain_heads = qk_scale.reshape(local_heads, head_size)
    q_hat, q_inverse = unit_rows(q_rot)
    k_hat, k_inverse = unit_rows(k_rot)
    q_unit = (gain_heads * q_hat).astype(jnp.bfloat16)
    k_unit = (gain_heads * k_hat).astype(jnp.bfloat16)
    heads_full, log_totals = attend(
        q_unit, k_unit, v_round, segment, seq_count, block_rows, score_root
    )
    head_out = heads_full.astype(jnp.bfloat16).reshape(group_rows, local_width)
    piece = head_out
    attn_sum = scatter_rows(jnp.dot(piece, w_out, preferred_element_type=jnp.float32))
    residual = tokens.astype(jnp.float32)
    h_attn, attn_inverse = unit_rows(attn_sum)
    h_one, one_inverse = unit_rows(residual + attn_rate * (h_attn - residual))
    normed_low = h_one.astype(jnp.bfloat16)
    mlp_input = gather_rows(normed_low)
    up_proj = jnp.dot(mlp_input, w_up, preferred_element_type=jnp.float32)
    gate_proj = jnp.dot(mlp_input, w_gate, preferred_element_type=jnp.float32)
    gate_factor = gate_scale * width_root
    up_scaled = up_scale * up_proj
    gate_scaled = gate_factor * gate_proj
    sigmoid_gate = jax.nn.sigmoid(gate_scaled)
    activated = gate_scaled * sigmoid_gate
    hidden = (up_scaled * activated).astype(jnp.bfloat16)
    piece = hidden
    mlp_sum = scatter_rows(jnp.dot(piece, w_down, preferred_element_type=jnp.float32))
    h_mlp, mlp_inverse = unit_rows(mlp_sum)
    block_out, out_inverse = unit_rows(h_one + mlp_rate * (h_mlp - h_one))
    cotangent = out_grad.astype(jnp.float32)
    d_mix_two = unit_back(cotangent, block_out, out_inverse)
    rate_mlp_part = jnp.sum(d_mix_two * (h_mlp - h_one), axis=0)
    d_mlp = unit_back(mlp_rate * d_mix_two, h_mlp, mlp_inverse).astype(jnp.bfloat16)
    d_mlp_all = gather_rows(d_mlp)
    d_hidden = contract_cols(d_mlp_all, w_down)
    grad_down = contract_rows(hidden, d_mlp_all)
    silu_grad = sigmoid_gate * (1.0 + gate_scaled * (1.0 - sigmoid_gate))
    d_up_scaled = d_hidden * activated
    d_gate_scaled = d_hidden * up_scaled * silu_grad
    d_up = (d_up_scaled * up_scale).astype(jnp.bfloat16)
    d_gate = (d_gate_scaled * gate_factor).astype(jnp.bfloat16)
    grad_up_scale = jnp.sum(d_up_scaled * up_proj, axis=0)
    grad_gate_scale = jnp.sum(d_gate_scaled * gate_proj, axis=0) * width_root
    grad_up = contract_rows(mlp_input, d_up)
    grad_gate = contract_rows(mlp_input, d_gate)
    d_feed = scatter_rows(contract_cols(d_up, w_up) + contract_cols(d_gate, w_gate))
    d_one = (1.0 - mlp_rate) * d_mix_two + d_feed
    d_mix = unit_back(d_one, h_one, one_inverse)
    rate_attn_part = jnp.sum(d_mix * (h_attn - residual), axis=0)
    d_attn = unit_back(attn_rate * d_mix, h_attn, attn_inverse).astype(jnp.bfloat16)
    d_attn_all = gather_rows(d_attn)
    grad_w_out = contract_rows(head_out, d_attn_all)
    d_head = contract_cols(d_attn_all, w_out).astype(jnp.bfloat16).reshape(head_shape)
    d_q_unit, d_k_unit, d_value = attend_back(
        q_unit, k_unit, v_round, d_head, log_totals, segment, seq_count, block_rows, score_root
    )
    grad_qk_scale = jnp.sum(q_hat * d_q_unit + k_hat * d_k_unit, axis=0).reshape(local_width)
    d_query = rotate(unit_back(gain_heads * d_q_unit, q_hat, q_inverse), cosine_table, -sine_table)
    d_key = rotate(unit_back(gain_heads * d_k_unit, k_hat, k_inverse), cosine_table, -sine_table)
    d_joined = jnp.concatenate(
        [
            d_query.astype(jnp.bfloat16).reshape(group_rows, local_width),
            d_key.astype(jnp.bfloat16).reshape(group_rows, local_width),
            d_value.reshape(group_rows, local_width),
        ],
        axis=1,
    )
    grad_joined = contract_rows(gathered, d_joined)
    piece = d_joined
    d_input = scatter_rows(contract_cols(piece, w_joined))
    residual_grad = (1.0 - attn_rate) * d_mix
    rates = jnp.stack([rate_attn_part, rate_mlp_part])
    for bit in bits_of("mp"):
        rates = rates + swap(rates, "mp", bit)
    rate_attn, rate_mlp = rates[0], rates[1]
    token_grad = residual_grad + d_input
    reduced = (
        scatter_groups(grad_joined, 0),
        scatter_groups(grad_w_out, 1),
        scatter_groups(grad_up, 0),
        scatter_groups(grad_gate, 0),
        scatter_groups(grad_down, 1),
        scatter_groups(grad_qk_scale, 0),
        scatter_groups(grad_up_scale, 0),
        scatter_groups(grad_gate_scale, 0),
        scatter_groups(rate_attn, 0),
        scatter_groups(rate_mlp, 0),
    )
    joined_part = reduced[0]
    return (
        block_out,
        token_grad,
        joined_part[:, :local_width],
        joined_part[:, local_width : 2 * local_width],
        joined_part[:, 2 * local_width :],
        reduced[1],
        reduced[5],
        reduced[8],
        reduced[2],
        reduced[3],
        reduced[6],
        reduced[7],
        reduced[4],
        reduced[9],
    )


def solution(mesh):
    in_specs = (
        P(("dp", "mp"), None),
        P("dp", None),
        P(None, "mp"),
        P(None, "mp"),
        P(None, "mp"),
        P("mp", None),
        P("mp"),
        P(),
        P(None, "mp"),
        P(None, "mp"),
        P("mp"),
        P("mp"),
        P("mp", None),
        P(),
        P(("dp", "mp"), None),
    )
    out_specs = (
        P(("dp", "mp"), None),
        P(("dp", "mp"), None),
        P("dp", "mp"),
        P("dp", "mp"),
        P("dp", "mp"),
        P("mp", "dp"),
        P(("mp", "dp")),
        P("dp"),
        P("dp", "mp"),
        P("dp", "mp"),
        P(("mp", "dp")),
        P(("mp", "dp")),
        P("mp", "dp"),
        P("dp"),
    )
    return jax.shard_map(shards, mesh=mesh, in_specs=in_specs, out_specs=out_specs, check_vma=False)
```

```python
import functools
import math

import jax
import jax.numpy as jnp
from jax import lax
from jax.experimental import pallas as pl
from jax.experimental.pallas import tpu as pltpu
from jax.sharding import PartitionSpec as P

HD = 64
HALF = HD // 2
EPS = 1e-06
F32 = jnp.float32
BF16 = jnp.bfloat16
SCORE_ROOT = math.sqrt(HD)
EXP_SCALE = SCORE_ROOT * math.log2(math.e)
MIB = 1 << 20
PARTS = 2


def dot(left, right):
    return lax.dot_general(left, right, (((1,), (0,)), ((), ())), preferred_element_type=F32)


def dot_nt(left, right):
    return lax.dot_general(left, right, (((1,), (1,)), ((), ())), preferred_element_type=F32)


def dot_tn(left, right):
    return lax.dot_general(left, right, (((0,), (0,)), ((), ())), preferred_element_type=F32)


def iota(shape, dim):
    return lax.broadcasted_iota(jnp.int32, shape, dim)


def struct(shape, dtype):
    return jax.ShapeDtypeStruct(shape, dtype)


def in_vmem():
    return pl.BlockSpec(memory_space=pltpu.VMEM)


def in_smem():
    return pl.BlockSpec(memory_space=pltpu.SMEM)


def cost(flops, args, outs, transcendentals=0):
    moved = sum(a.size * a.dtype.itemsize for a in args)
    moved += sum(math.prod(o.shape) * jnp.dtype(o.dtype).itemsize for o in outs)
    return pl.CostEstimate(flops=int(flops), bytes_accessed=int(moved), transcendentals=int(transcendentals))


def run_whole(body, outs, args, flops, scratch=(), vmem=32, smem=0, transcendentals=0):
    specs = [in_smem() if i < smem else in_vmem() for i in range(len(args))]
    return pl.pallas_call(
        body,
        out_shape=outs,
        in_specs=specs,
        out_specs=[in_vmem() for _ in outs],
        scratch_shapes=list(scratch),
        compiler_params=pltpu.CompilerParams(vmem_limit_bytes=vmem * MIB),
        cost_estimate=cost(flops, args, outs, transcendentals),
    )(*args)


def swap(values, axis, bit):
    size = lax.axis_size(axis)
    return lax.ppermute(values, axis, [(i, i ^ bit) for i in range(size)])


def bits_of(axis):
    size = lax.axis_size(axis)
    return [1 << i for i in range(size.bit_length() - 1)]


def head_order(width):
    half = width // 2
    source = iota((width, width), 0)
    target = iota((width, width), 1)
    wanted = (target % half) // HALF * HD + target // half * HALF + target % HALF
    return (source == wanted).astype(BF16)


def same_head(lanes):
    return (iota((lanes, lanes), 0) // HALF == iota((lanes, lanes), 1) // HALF).astype(BF16)


def head_total(values, ones):
    high = values.astype(BF16)
    low = (values - high.astype(F32)).astype(BF16)
    return dot(high, ones) + dot(low, ones)


def rope_head(lanes):
    half = lanes // 2
    return iota((1, lanes), 1) % half // HALF


def value_head(lanes):
    return iota((1, lanes), 1) // HD


def project_kernel(xa, xb, wq, wk, wv, gain, cos, sin, q_out, k_out, v_out, qi_out, ki_out, wq_s, wk_s):
    width = wq.shape[1]
    half = width // 2
    order = head_order(width)
    ones = same_head(half)
    wq_s[...] = dot(wq[...], order).astype(BF16)
    wk_s[...] = dot(wk[...], order).astype(BF16)
    for index, source in enumerate((xa, xb)):
        rows = source[...]
        c, s = cos[index], sin[index]
        for weights, unit_out, inverse_out in ((wq_s, q_out, qi_out), (wk_s, k_out, ki_out)):
            full = dot(rows, weights[...])
            a, b = full[:, :half], full[:, half:]
            inverse = lax.rsqrt(head_total(a * a + b * b, ones) + EPS)
            inverse_out[index] = inverse
            unit_out[index, :, :half] = ((a * c - b * s) * inverse * gain[:, :half]).astype(BF16)
            unit_out[index, :, half:] = ((b * c + a * s) * inverse * gain[:, half:]).astype(BF16)
        v_out[index] = dot(rows, wv[...]).astype(BF16)


def project(xa, xb, wq, wk, wv, gain, cos, sin):
    rows, depth = xa.shape
    width = wq.shape[1]
    outs = [struct((2, rows, width), BF16)] * 3 + [struct((2, rows, width // 2), F32)] * 2
    args = (xa, xb, wq, wk, wv, gain, cos, sin)
    scratch = [pltpu.VMEM((depth, width), BF16)] * 2
    return run_whole(project_kernel, outs, args, 2 * 2 * rows * depth * width * 3, scratch)


def attend_kernel(
    slots, heads, me, q, k01, k23, v01, v23, seg_col, seg_row, w_out,
    head_out, inv_out, p_first, p_second, kbuf, vbuf, qm, acc, total,
):
    rows, width = kbuf.shape[1:]
    mine = me[0, 0]
    kbuf[0:2] = k01[...]
    kbuf[2:4] = k23[...]
    vbuf[0:2] = v01[...]
    vbuf[2:4] = v23[...]
    q_head = rope_head(width)
    v_head = value_head(width)
    for index, slot in enumerate(slots):
        block = jnp.bitwise_xor(mine, slot)
        queries = q[slot % 2]
        for h in range(heads):
            qm[h] = jnp.where(q_head == h, queries, jnp.zeros_like(queries))
        acc[...] = jnp.zeros_like(acc)
        total[...] = jnp.zeros_like(total)
        seg_q = seg_col[slot]

        def step(key_block, carry):
            other = jnp.bitwise_xor(key_block, mine)
            keys = kbuf[other]
            values = vbuf[other]
            key_id = iota((rows, rows), 1) + key_block * rows
            query_id = iota((rows, rows), 0) + block * rows
            allowed = ((seg_q == seg_row[other]) & (key_id <= query_id)) | (key_id == query_id)
            for h in range(heads):
                scores = dot_nt(qm[h], keys)
                weight = jnp.where(allowed, jnp.exp2(scores * EXP_SCALE), 0.0)
                total[h] += jnp.sum(weight, axis=1, keepdims=True)
                acc[h] += dot(weight.astype(BF16), values)
            return carry

        lax.fori_loop(0, block + 1, step, 0)
        inverse = jnp.zeros((rows, width), F32)
        mixed = jnp.zeros((rows, width), F32)
        for h in range(heads):
            inverse = jnp.where(v_head == h, 1.0 / total[h], inverse)
            mixed = jnp.where(v_head == h, acc[h], mixed)
        inv_out[index] = inverse
        out = (mixed * inverse).astype(BF16)
        head_out[index] = out
        target = p_first if index == 0 else p_second
        target[...] = dot(out, w_out[...]).astype(target.dtype)


def attend(slots, me, q, k01, k23, v01, v23, seg_col, seg_row, w_out, first_type, second_type):
    _, rows, width = q.shape
    heads = width // HD
    depth = w_out.shape[1]
    outs = [
        struct((2, rows, width), BF16),
        struct((2, rows, width), F32),
        struct((rows, depth), first_type),
        struct((rows, depth), second_type),
    ]
    args = (me, q, k01, k23, v01, v23, seg_col, seg_row, w_out)
    scratch = [
        pltpu.VMEM((4, rows, width), BF16),
        pltpu.VMEM((4, rows, width), BF16),
        pltpu.VMEM((heads, rows, width), BF16),
        pltpu.VMEM((heads, rows, width), F32),
        pltpu.VMEM((heads, rows, 1), F32),
    ]
    return run_whole(
        functools.partial(attend_kernel, slots, heads), outs, args,
        2 * 2 * rows * depth * width + 5 * heads * 2 * 2 * rows * rows * width,
        scratch, smem=1,
    )


def attend_back_kernel(
    heads, me, a0c0, a2c0, a13c0, a0c1, a2c1, a13c1, w_out, q01, q23, k01, k23, v01, v23,
    heads10, heads32, inv10, inv32, qi01, qi23, ki01, ki23, seg_col, seg_row, gain, cos, sin,
    wq, wk, wv, joined, p3, p2, scale_out,
    qm, kbuf, qbuf, vm, dhm, dhn, dq, dk, dv,
):
    rows, width = kbuf.shape[1:]
    half = width // 2
    part = rows // PARTS
    mine = me[0, 0]
    q_head = rope_head(width)
    v_head = value_head(width)
    lane = iota((1, width), 1)
    for pair, (q_ref, k_ref) in enumerate(((q01, k01), (q23, k23))):
        for i in range(2):
            qbuf[2 * pair + i] = q_ref[i]
            kbuf[2 * pair + i] = k_ref[i]
    dk[...] = jnp.zeros_like(dk)
    dv[...] = jnp.zeros_like(dv)
    sources = {
        0: (lambda c: (a0c0, a0c1)[c][...]),
        2: (lambda c: (a2c0, a2c1)[c][...]),
        1: (lambda c: (a13c0, a13c1)[c][0]),
        3: (lambda c: (a13c0, a13c1)[c][1]),
    }
    for slot in range(4):
        for c in range(PARTS):
            span = pl.ds(c * part, part)
            grads = dot_nt(sources[slot](c), w_out[...])
            at = (1 - slot) if slot < 2 else (3 - slot)
            inverse = (inv10 if slot < 2 else inv32)[at, c * part : (c + 1) * part]
            outs = (heads10 if slot < 2 else heads32)[at, c * part : (c + 1) * part]
            scaled = (grads * inverse).astype(BF16)
            dhn[slot, span] = scaled
            product = scaled.astype(F32) * outs.astype(F32)
            for h in range(heads):
                row_dot = jnp.sum(jnp.where(v_head == h, product, 0.0), axis=1, keepdims=True)
                high = (-row_dot).astype(BF16)
                low = (-row_dot - high.astype(F32)).astype(BF16)
                first = (h + 1) % heads * HD
                dhm[slot, h, span] = jnp.where(
                    v_head == h,
                    scaled,
                    jnp.where(lane == first, high, jnp.where(lane == first + 1, low, jnp.zeros_like(scaled))),
                )
        values = (v01 if slot < 2 else v23)[slot % 2]
        for h in range(heads):
            first = (h + 1) % heads * HD
            vm[slot, h] = jnp.where((lane == first) | (lane == first + 1), jnp.ones_like(values), values)
    for slot in range(4):
        block = jnp.bitwise_xor(mine, slot)
        queries = qbuf[slot]
        for h in range(heads):
            qm[h] = jnp.where(q_head == h, queries, jnp.zeros_like(queries))
        seg_q = seg_row[slot]
        dq[slot] = jnp.zeros((rows, width), F32)

        def step(key_block, carry):
            other = jnp.bitwise_xor(key_block, mine)
            keys = kbuf[other]
            key_id = iota((rows, rows), 0) + key_block * rows
            query_id = iota((rows, rows), 1) + block * rows
            allowed = ((seg_q == seg_col[other]) & (key_id <= query_id)) | (key_id == query_id)
            for h in range(heads):
                scores = dot_nt(keys, qm[h])
                weight = jnp.where(allowed, jnp.exp2(scores * EXP_SCALE), 0.0)
                grad = weight * dot_nt(vm[other, h], dhm[slot, h])
                low = grad.astype(BF16)
                dv[other] += jnp.where(v_head == h, dot(weight.astype(BF16), dhn[slot]), 0.0)
                dk[other] += jnp.where(q_head == h, dot(low, qbuf[slot]), 0.0)
                dq[slot] += jnp.where(q_head == h, dot_tn(low, keys), 0.0)
            return carry

        lax.fori_loop(0, block + 1, step, 0)
    order = head_order(width)
    ones = same_head(half)
    scale_sum = jnp.zeros((1, width), F32)
    for slot in range(4):
        c, s = cos[slot], sin[slot]
        for place, (grad_ref, unit_ref, inv_ref) in enumerate(
            ((dq, qbuf, (qi01, qi23)), (dk, kbuf, (ki01, ki23)))
        ):
            inverse = inv_ref[slot // 2][slot % 2]
            grads = grad_ref[slot] * SCORE_ROOT
            normed = unit_ref[slot].astype(F32) / gain[...]
            scale_sum = scale_sum + jnp.sum(normed * grads, axis=0, keepdims=True)
            grads = grads * gain[...]
            product = normed * grads
            along = head_total(product[:, :half] + product[:, half:], ones)
            a = (grads[:, :half] - normed[:, :half] * along) * inverse
            b = (grads[:, half:] - normed[:, half:] * along) * inverse
            turned = jnp.concatenate([(a * c + b * s).astype(BF16), (b * c - a * s).astype(BF16)], axis=1)
            joined[slot, :, place * width : (place + 1) * width] = dot_nt(turned, order).astype(BF16)
        joined[slot, :, 2 * width : 3 * width] = dv[slot].astype(BF16)
    scale_out[...] = scale_sum
    for slot, target in ((3, p3), (2, p2)):
        target[...] = input_grad(joined, slot, wq, wk, wv).astype(target.dtype)


def input_grad(joined, slot, wq, wk, wv):
    width = wq.shape[1]
    out = dot_nt(joined[slot, :, :width], wq[...])
    out += dot_nt(joined[slot, :, width : 2 * width], wk[...])
    return out + dot_nt(joined[slot, :, 2 * width :], wv[...])


def attend_back(me, grads, w_out, q01, q23, k01, k23, v01, v23, heads10, heads32, inv10, inv32,
                qi01, qi23, ki01, ki23, seg_col, seg_row, gain, cos, sin, wq, wk, wv):
    _, rows, width = q01.shape
    heads = width // HD
    depth = w_out.shape[1]
    outs = [
        struct((4, rows, 3 * width), BF16),
        struct((rows, depth), BF16),
        struct((rows, depth), F32),
        struct((1, width), F32),
    ]
    flat = [piece for chunk in grads for piece in chunk]
    args = (me, *flat, w_out, q01, q23, k01, k23, v01, v23, heads10, heads32, inv10, inv32,
            qi01, qi23, ki01, ki23, seg_col, seg_row, gain, cos, sin, wq, wk, wv)
    scratch = [
        pltpu.VMEM((heads, rows, width), BF16),
        pltpu.VMEM((4, rows, width), BF16),
        pltpu.VMEM((4, rows, width), BF16),
        pltpu.VMEM((4, heads, rows, width), BF16),
        pltpu.VMEM((4, heads, rows, width), BF16),
        pltpu.VMEM((4, rows, width), BF16),
        pltpu.VMEM((4, rows, width), F32),
        pltpu.VMEM((4, rows, width), F32),
        pltpu.VMEM((4, rows, width), F32),
    ]
    return run_whole(
        functools.partial(attend_back_kernel, heads), outs, args,
        2 * 6 * rows * depth * width * 2 + 10 * heads * 5 * 2 * rows * rows * width,
        scratch, vmem=48, smem=1,
    )


def input_tail_kernel(joined, wq, wk, wv, p1, p0):
    for slot, target in ((1, p1), (0, p0)):
        target[...] = input_grad(joined, slot, wq, wk, wv).astype(target.dtype)


def input_tail(joined, wq, wk, wv):
    rows = joined.shape[1]
    depth, width = wq.shape
    outs = [struct((rows, depth), BF16), struct((rows, depth), F32)]
    return run_whole(input_tail_kernel, outs, (joined, wq, wk, wv), 2 * 2 * rows * depth * width * 3)


def unit_rows(values):
    inverse = lax.rsqrt(jnp.sum(values * values, axis=-1, keepdims=True) + EPS)
    return values * inverse, inverse


def unit_back(grad_in, normed, inverse):
    return (grad_in - normed * jnp.sum(normed * grad_in, axis=-1, keepdims=True)) * inverse


def mix_attn_kernel(own, core, far, tokens, rate, low_out, one_out, sum_out):
    total = own[...] + core[...].astype(F32) + far[...].astype(F32)
    sum_out[...] = total
    h_attn, _ = unit_rows(total)
    residual = tokens[...].astype(F32)
    h_one, _ = unit_rows(residual + rate[...] * (h_attn - residual))
    one_out[...] = h_one
    low_out[...] = h_one.astype(BF16)


def mix_mlp_kernel(own, core, far, h_one, rate, cotangent, out, low_out, mix_out, rate_out):
    total = own[...] + core[...].astype(F32) + far[...].astype(F32)
    h_mlp, mlp_inverse = unit_rows(total)
    first = h_one[...]
    away = h_mlp - first
    block_out, out_inverse = unit_rows(first + rate[...] * away)
    out[...] = block_out
    d_mix = unit_back(cotangent[...].astype(F32), block_out, out_inverse)
    mix_out[...] = d_mix
    rate_out[...] = jnp.sum(d_mix * away, axis=0, keepdims=True)
    low_out[...] = unit_back(rate[...] * d_mix, h_mlp, mlp_inverse).astype(BF16)


def mix_back_kernel(own, core, far, d_mix_two, attn_sum, h_one, tokens, rate, mlp_rate, low_out, rest_out, rate_out):
    d_one = own[...] + core[...].astype(F32) + far[...].astype(F32)
    d_one = d_one + (1.0 - mlp_rate[...]) * d_mix_two[...]
    h_attn, attn_inverse = unit_rows(attn_sum[...])
    residual = tokens[...].astype(F32)
    away = h_attn - residual
    _, one_inverse = unit_rows(residual + rate[...] * away)
    d_mix = unit_back(d_one, h_one[...], one_inverse)
    rest_out[...] = (1.0 - rate[...]) * d_mix
    rate_out[...] = jnp.sum(d_mix * away, axis=0, keepdims=True)
    low_out[...] = unit_back(rate[...] * d_mix, h_attn, attn_inverse).astype(BF16)


def silu_parts(gate):
    sig = 1.0 / (1.0 + jnp.exp(-gate))
    return sig, gate * sig


def fill_rows(buffer, near, far, cores):
    part = near.shape[0]
    buffer[0:part] = near[...]
    buffer[part : 2 * part] = far[...]
    buffer[2 * part : 3 * part] = cores[0]
    buffer[3 * part : 4 * part] = cores[1]


def spread_rows(total, own, far, cores):
    part = own.shape[0]
    own[...] = total[0:part]
    far[...] = total[part : 2 * part]
    cores[0] = total[2 * part : 3 * part].astype(BF16)
    cores[1] = total[3 * part : 4 * part].astype(BF16)


def feed_kernel(near, far, cores, w_up, w_gate, w_down, up_scale, gate_scale,
                up_out, gate_out, hid_out, p0, p2, p13, rows, total):
    step = pl.program_id(0)

    @pl.when(step == 0)
    def _():
        fill_rows(rows, near, far, cores)

    up = dot(rows[...], w_up[...])
    gate = dot(rows[...], w_gate[...])
    up_out[...] = up
    gate_out[...] = gate
    _, active = silu_parts(gate_scale[...] * gate)
    hidden = (up_scale[...] * up * active).astype(BF16)
    hid_out[...] = hidden
    product = dot(hidden, w_down[...])

    @pl.when(step == 0)
    def _():
        total[...] = product

    @pl.when(step > 0)
    def _():
        total[...] += product

    @pl.when(step == pl.num_programs(0) - 1)
    def _():
        spread_rows(total, p0, p2, p13)


def feed(near, far, cores, w_up, w_gate, w_down, up_scale, gate_scale, tile=256):
    part, depth = near.shape
    rows = 4 * part
    width = w_up.shape[1]
    whole2 = pl.BlockSpec((part, depth), lambda j: (0, 0))
    whole3 = pl.BlockSpec((2, part, depth), lambda j: (0, 0, 0))
    column = pl.BlockSpec((depth, tile), lambda j: (0, j))
    scale = pl.BlockSpec((1, tile), lambda j: (0, j))
    hidden = pl.BlockSpec((rows, tile), lambda j: (0, j))
    outs = [
        struct((rows, width), F32), struct((rows, width), F32), struct((rows, width), BF16),
        struct((part, depth), F32), struct((part, depth), F32), struct((2, part, depth), BF16),
    ]
    args = (near, far, cores, w_up, w_gate, w_down, up_scale, gate_scale)
    return pl.pallas_call(
        feed_kernel,
        grid=(width // tile,),
        out_shape=outs,
        in_specs=[whole2, whole2, whole3, column, column, pl.BlockSpec((tile, depth), lambda j: (j, 0)), scale, scale],
        out_specs=[hidden, hidden, hidden, whole2, whole2, whole3],
        scratch_shapes=[pltpu.VMEM((rows, depth), BF16), pltpu.VMEM((rows, depth), F32)],
        compiler_params=pltpu.CompilerParams(vmem_limit_bytes=32 * MIB),
        cost_estimate=cost(6 * rows * depth * width, args, outs),
    )(*args)


def feed_back_kernel(near, far, cores, up, gate, w_up, w_gate, w_down, up_scale, gate_scale,
                     d_up_out, d_gate_out, sums_out, p0, p2, p13, rows, total):
    step = pl.program_id(0)

    @pl.when(step == 0)
    def _():
        fill_rows(rows, near, far, cores)

    d_hidden = dot_nt(rows[...], w_down[...])
    u = up[...]
    g = gate[...]
    scaled = gate_scale[...] * g
    sig, active = silu_parts(scaled)
    d_up_scaled = d_hidden * active
    d_gate_scaled = d_hidden * (up_scale[...] * u) * (sig * (1.0 + scaled * (1.0 - sig)))
    d_up = (d_up_scaled * up_scale[...]).astype(BF16)
    d_gate = (d_gate_scaled * gate_scale[...]).astype(BF16)
    d_up_out[...] = d_up
    d_gate_out[...] = d_gate
    sums_out[0:1] = jnp.sum(d_up_scaled * u, axis=0, keepdims=True)
    sums_out[1:2] = jnp.sum(d_gate_scaled * g, axis=0, keepdims=True)
    product = dot_nt(d_up, w_up[...]) + dot_nt(d_gate, w_gate[...])

    @pl.when(step == 0)
    def _():
        total[...] = product

    @pl.when(step > 0)
    def _():
        total[...] += product

    @pl.when(step == pl.num_programs(0) - 1)
    def _():
        spread_rows(total, p0, p2, p13)


def feed_back(near, far, cores, up, gate, w_up, w_gate, w_down, up_scale, gate_scale, tile=256):
    part, depth = near.shape
    rows = 4 * part
    width = w_up.shape[1]
    whole2 = pl.BlockSpec((part, depth), lambda j: (0, 0))
    whole3 = pl.BlockSpec((2, part, depth), lambda j: (0, 0, 0))
    column = pl.BlockSpec((depth, tile), lambda j: (0, j))
    scale = pl.BlockSpec((1, tile), lambda j: (0, j))
    hidden = pl.BlockSpec((rows, tile), lambda j: (0, j))
    outs = [
        struct((rows, width), BF16), struct((rows, width), BF16), struct((2, width), F32),
        struct((part, depth), F32), struct((part, depth), F32), struct((2, part, depth), BF16),
    ]
    args = (near, far, cores, up, gate, w_up, w_gate, w_down, up_scale, gate_scale)
    return pl.pallas_call(
        feed_back_kernel,
        grid=(width // tile,),
        out_shape=outs,
        in_specs=[whole2, whole2, whole3, hidden, hidden, column, column,
                  pl.BlockSpec((tile, depth), lambda j: (j, 0)), scale, scale],
        out_specs=[hidden, hidden, pl.BlockSpec((2, tile), lambda j: (0, j)), whole2, whole2, whole3],
        scratch_shapes=[pltpu.VMEM((rows, depth), BF16), pltpu.VMEM((rows, depth), F32)],
        compiler_params=pltpu.CompilerParams(vmem_limit_bytes=32 * MIB),
        cost_estimate=cost(6 * rows * depth * width, args, outs),
    )(*args)


def weight_kernel(n_left, n_right, me, *refs):
    left = refs[:n_left]
    right = refs[n_left : n_left + n_right]
    sent, kept, turned = refs[n_left + n_right :]
    half = sent.shape[0]
    pieces = half // turned_piece(turned)
    piece = turned_piece(turned)

    @pl.when(pl.program_id(0) == 0)
    def _():
        mine = me[0, 0]
        for side in range(2):
            for i in range(pieces):
                at = jnp.bitwise_xor(mine, 2 * i + 1 - side) * piece
                start = 0
                for ref in left:
                    columns = ref[:, pl.ds(pl.multiple_of(at, piece), piece)]
                    turned[side, i * piece : (i + 1) * piece, start : start + ref.shape[0]] = columns.T
                    start += ref.shape[0]

    for side, target in enumerate((sent, kept)):
        start = 0
        product = None
        for ref in right:
            part = dot(turned[side, :, start : start + ref.shape[0]], ref[...])
            product = part if product is None else product + part
            start += ref.shape[0]
        target[...] = product.astype(target.dtype)


def turned_piece(turned):
    return 128


def weight_halves(me, left, right, n_groups, tile=256):
    depth = left[0].shape[1]
    rows = sum(a.shape[0] for a in left)
    width = right[0].shape[1]
    half = depth // 2
    piece = depth // n_groups
    outs = [struct((half, width), BF16), struct((half, width), F32)]
    args = (me, *left, *right)
    out_spec = pl.BlockSpec((half, tile), lambda j: (0, j))
    sent, kept = pl.pallas_call(
        functools.partial(weight_kernel, len(left), len(right)),
        grid=(width // tile,),
        out_shape=outs,
        in_specs=[in_smem()]
        + [pl.BlockSpec(a.shape, lambda j: (0, 0)) for a in left]
        + [pl.BlockSpec((a.shape[0], tile), lambda j: (0, j)) for a in right],
        out_specs=[out_spec, out_spec],
        scratch_shapes=[pltpu.VMEM((2, half, rows), BF16)],
        compiler_params=pltpu.CompilerParams(vmem_limit_bytes=32 * MIB),
        cost_estimate=cost(2 * rows * depth * width, args, outs),
    )(*args)
    return sent.reshape(n_groups // 2, piece, width), kept.reshape(n_groups // 2, piece, width)


def weight_halves_plain(me, left, right, n_groups):
    product = dot_tn(jnp.concatenate(left, axis=0), jnp.concatenate(right, axis=0))
    parts = product.reshape(n_groups, product.shape[0] // n_groups, product.shape[1])
    order = jnp.bitwise_xor(me[0, 0], jnp.arange(n_groups, dtype=jnp.int32))
    parts = parts[order].reshape((n_groups // 2, 2) + parts.shape[1:])
    return parts[:, 1].astype(BF16), parts[:, 0]


def scatter_halves(sent, kept, bits):
    first = True
    for bit in bits:
        if not first:
            count = kept.shape[0] // 2
            parts = kept.reshape((count, 2) + kept.shape[1:])
            sent, kept = parts[:, 1].astype(BF16), parts[:, 0]
        kept = kept + swap(sent, "dp", bit).astype(F32)
        first = False
    return kept[0]


def shards(
    tokens,
    seq_lengths,
    w_query,
    w_key,
    w_value,
    w_out,
    qk_scale,
    attn_rate,
    w_up,
    w_gate,
    up_scale,
    gate_scale,
    w_down,
    mlp_rate,
    out_grad,
):
    local_rows, depth = tokens.shape
    n_mp = lax.axis_size("mp")
    n_dp = lax.axis_size("dp")
    assert n_mp == 4
    width = w_query.shape[1]
    heads = width // HD
    part = local_rows // PARTS
    me = lax.axis_index("mp").astype(jnp.int32)
    me_ref = me.reshape(1, 1)
    group = lax.axis_index("dp").astype(jnp.int32)
    group_ref = group.reshape(1, 1)
    dp_bits = bits_of("dp")
    seq_count = seq_lengths.shape[1]

    far_tokens = swap(tokens, "mp", 2)
    core_tokens = swap(tokens, "mp", 1)
    ends = jnp.cumsum(seq_lengths[0])
    starts = jnp.concatenate([jnp.zeros((1,), jnp.int32), ends])
    owner = jnp.bitwise_xor(me, jnp.arange(n_mp, dtype=jnp.int32))
    row_ids = owner[:, None] * local_rows + jnp.arange(local_rows, dtype=jnp.int32)[None]
    segment = jnp.sum((row_ids[:, :, None] >= ends).astype(jnp.int32), axis=2)
    first = jnp.sum(
        jnp.where(segment[:, :, None] == jnp.arange(seq_count + 1, dtype=jnp.int32), starts, 0), axis=2
    )
    position = (row_ids - first).astype(F32)
    frequency = jnp.exp(jnp.arange(HALF, dtype=F32) * (-2.0 * math.log(10000.0) / HD))
    angles = position[:, :, None] * jnp.tile(frequency, heads)[None, None]
    cos, sin = jnp.cos(angles), jnp.sin(angles)
    seg_q = jnp.where(segment < seq_count, segment, -1)
    seg_k = jnp.where(segment < seq_count, segment, -2)
    gain = qk_scale.reshape(heads, 2, HALF).transpose(1, 0, 2).reshape(1, width)

    weights = (w_query, w_key, w_value)
    q01, k01, v01, qi01, ki01 = project(tokens, core_tokens, *weights, gain, cos[0:2], sin[0:2])
    cross_tokens = swap(far_tokens, "mp", 1)
    q23, k23, v23, qi23, ki23 = project(far_tokens, cross_tokens, *weights, gain, cos[2:4], sin[2:4])
    seg_col, seg_row = seg_q[:, :, None], seg_k[:, None, :]
    heads32, inv32, p3, p2 = attend(
        (3, 2), me_ref, q23, k01, k23, v01, v23, seg_col, seg_row, w_out, BF16, F32
    )
    r3 = swap(p3, "mp", 1)
    far_sum = (p2 + r3.astype(F32)).astype(BF16)
    far_parts = [swap(far_sum[c * part : (c + 1) * part], "mp", 2) for c in range(PARTS)]
    heads10, inv10, p1, p0 = attend(
        (1, 0), me_ref, q01, k01, k23, v01, v23, seg_col, seg_row, w_out, BF16, F32
    )
    r1 = swap(p1, "mp", 1)

    attn_row = attn_rate.reshape(1, depth)
    mlp_row = mlp_rate.reshape(1, depth)
    up_row = up_scale.reshape(1, -1)
    gate_row = (gate_scale * math.sqrt(depth)).reshape(1, -1)

    def rows_of(values, c):
        return values[c * part : (c + 1) * part]

    def spread(low):
        far = swap(low, "mp", 2)
        cores = swap(jnp.stack([low, far]), "mp", 1)
        return low, far, cores

    def gather_sums(own, far, cores):
        got = swap(cores, "mp", 1)
        return own, got[0], swap((far + got[1].astype(F32)).astype(BF16), "mp", 2)

    full, lowered, vector = struct((part, depth), F32), struct((part, depth), BF16), struct((1, depth), F32)
    inputs, ones, sums = [], [], []
    for c in range(PARTS):
        low, h_one, attn_sum = run_whole(
            mix_attn_kernel, [lowered, full, full],
            (rows_of(p0, c), rows_of(r1, c), far_parts[c], rows_of(tokens, c), attn_row), 20 * part * depth,
        )
        inputs.append(spread(low))
        ones.append(h_one)
        sums.append(attn_sum)
    ups, gates, hiddens, outs, d_mixes, rate_parts, d_mlps = [], [], [], [], [], [], []
    for c in range(PARTS):
        up, gate, hidden, own, far, cores = feed(*inputs[c], w_up, w_gate, w_down, up_row, gate_row)
        ups.append(up)
        gates.append(gate)
        hiddens.append(hidden)
        block_out, low, d_mix, rate_part = run_whole(
            mix_mlp_kernel, [full, lowered, full, vector],
            (*gather_sums(own, far, cores), ones[c], mlp_row, rows_of(out_grad, c)), 30 * part * depth,
        )
        outs.append(block_out)
        d_mixes.append(d_mix)
        rate_parts.append(rate_part)
        d_mlps.append(spread(low))
    d_ups, d_gates, d_attns, rests, rate_attns, scale_sums = [], [], [], [], [], []
    for c in range(PARTS):
        d_up, d_gate, scale_sum, own, far, cores = feed_back(
            *d_mlps[c], ups[c], gates[c], w_up, w_gate, w_down, up_row, gate_row
        )
        d_ups.append(d_up)
        d_gates.append(d_gate)
        scale_sums.append(scale_sum)
        low, rest, rate_part = run_whole(
            mix_back_kernel, [lowered, full, vector],
            (*gather_sums(own, far, cores), d_mixes[c], sums[c], ones[c], rows_of(tokens, c), attn_row, mlp_row),
            40 * part * depth,
        )
        rests.append(rest)
        rate_attns.append(rate_part)
        d_attns.append(spread(low))

    def row_list(pieces):
        return [p for near, far, cores in pieces for p in (near, far, cores.reshape(2 * part, depth))]

    fast = depth // n_dp == 128

    def weight_grad(left, right):
        if fast:
            return weight_halves(group_ref, left, right, n_dp)
        return weight_halves_plain(group_ref, left, right, n_dp)

    down = scatter_halves(*weight_grad(row_list(d_mlps), hiddens), dp_bits)
    grad_up = scatter_halves(*weight_grad(row_list(inputs), d_ups), dp_bits)
    grad_gate = scatter_halves(*weight_grad(row_list(inputs), d_gates), dp_bits)

    joined, b3, b2, qk_sum = attend_back(
        me_ref, d_attns, w_out, q01, q23, k01, k23, v01, v23, heads10, heads32, inv10, inv32,
        qi01, qi23, ki01, ki23, seg_k[:, :, None], seg_q[:, None, :], gain, cos, sin, *weights,
    )
    b3_got = swap(b3, "mp", 1)
    far_grad = swap((b2 + b3_got.astype(F32)).astype(BF16), "mp", 2)
    b1, b0 = input_tail(joined, *weights)
    b1_got = swap(b1, "mp", 1)
    token_rows = [tokens, core_tokens, far_tokens, cross_tokens]
    grad_joined = scatter_halves(
        *weight_grad(token_rows, [joined.reshape(4 * local_rows, 3 * width)]), dp_bits
    )
    token_grad = jnp.concatenate(rests, axis=0) + (b0 + b1_got.astype(F32) + far_grad.astype(F32))

    def head_rows(slot, c):
        source = heads10 if slot < 2 else heads32
        return source[(1 - slot) if slot < 2 else (3 - slot), c * part : (c + 1) * part]

    head_list = [head_rows(slot, c) for c in range(PARTS) for slot in (0, 2, 1, 3)]
    grad_out = scatter_halves(*weight_grad(row_list(d_attns), [jnp.concatenate(head_list, axis=0)]), dp_bits)

    rates = jnp.concatenate([sum(rate_attns), sum(rate_parts)], axis=0)
    for bit in bits_of("mp"):
        rates = rates + swap(rates, "mp", bit)
    scale_total = sum(scale_sums)
    gate_total = scale_total[1:2] * math.sqrt(depth)
    qk_total = qk_sum.reshape(2, heads, HALF).transpose(1, 0, 2).reshape(1, width)
    vectors = jnp.concatenate([rates.reshape(-1), scale_total[0], gate_total[0], qk_total[0]])
    sizes = [depth // n_dp] * 2 + [w_up.shape[1] // n_dp] * 2 + [width // n_dp]
    columns, start = [], 0
    for size in sizes:
        columns.append(vectors[start : start + size * n_dp].reshape(n_dp, size))
        start += size * n_dp
    table = jnp.concatenate(columns, axis=1)
    for bit in dp_bits:
        mine = (group // bit) % 2
        table = table.reshape(table.shape[0] // 2, 2, table.shape[-1])
        sent = lax.dynamic_index_in_dim(table, 1 - mine, 1, keepdims=False)
        kept = lax.dynamic_index_in_dim(table, mine, 1, keepdims=False)
        table = kept + swap(sent, "dp", bit)
    vector_outs, start = [], 0
    for size in sizes:
        vector_outs.append(table[0, start : start + size])
        start += size
    return (
        jnp.concatenate(outs, axis=0),
        token_grad,
        grad_joined[:, :width],
        grad_joined[:, width : 2 * width],
        grad_joined[:, 2 * width :],
        grad_out.T,
        vector_outs[4],
        vector_outs[0],
        grad_up,
        grad_gate,
        vector_outs[2],
        vector_outs[3],
        down.T,
        vector_outs[1],
    )


def solution(mesh):
    in_specs = (
        P(("dp", "mp"), None),
        P("dp", None),
        P(None, "mp"),
        P(None, "mp"),
        P(None, "mp"),
        P("mp", None),
        P("mp"),
        P(),
        P(None, "mp"),
        P(None, "mp"),
        P("mp"),
        P("mp"),
        P("mp", None),
        P(),
        P(("dp", "mp"), None),
    )
    out_specs = (
        P(("dp", "mp"), None),
        P(("dp", "mp"), None),
        P("dp", "mp"),
        P("dp", "mp"),
        P("dp", "mp"),
        P("mp", "dp"),
        P(("mp", "dp")),
        P("dp"),
        P("dp", "mp"),
        P("dp", "mp"),
        P(("mp", "dp")),
        P(("mp", "dp")),
        P("mp", "dp"),
        P("dp"),
    )
    return jax.shard_map(shards, mesh=mesh, in_specs=in_specs, out_specs=out_specs, check_vma=False)
```

```python
import functools
import math

import jax
import jax.numpy as jnp
from jax import lax
from jax.experimental import pallas as pl
from jax.experimental.pallas import tpu as pltpu
from jax.sharding import PartitionSpec as P

HD = 64
HALF = HD // 2
EPS = 1e-06
F32 = jnp.float32
BF16 = jnp.bfloat16
SCORE_ROOT = math.sqrt(HD)
EXP_SCALE = SCORE_ROOT * math.log2(math.e)
MIB = 1 << 20
PARTS = 2
FEED_VMEM = 32
VECTOR_ROWS = 16


def dot(left, right):
    return lax.dot_general(left, right, (((1,), (0,)), ((), ())), preferred_element_type=F32)


def dot_nt(left, right):
    return lax.dot_general(left, right, (((1,), (1,)), ((), ())), preferred_element_type=F32)


def dot_tn(left, right):
    return lax.dot_general(left, right, (((0,), (0,)), ((), ())), preferred_element_type=F32)


def iota(shape, dim):
    return lax.broadcasted_iota(jnp.int32, shape, dim)


def struct(shape, dtype):
    return jax.ShapeDtypeStruct(shape, dtype)


def in_vmem():
    return pl.BlockSpec(memory_space=pltpu.VMEM)


def in_smem():
    return pl.BlockSpec(memory_space=pltpu.SMEM)


def cost(flops, args, outs, transcendentals=0):
    moved = sum(a.size * a.dtype.itemsize for a in args)
    moved += sum(math.prod(o.shape) * jnp.dtype(o.dtype).itemsize for o in outs)
    return pl.CostEstimate(flops=int(flops), bytes_accessed=int(moved), transcendentals=int(transcendentals))


class Fetched:
    def __init__(self, copies, buffer):
        self.copies = copies
        self.buffer = buffer
        self.shape = buffer.shape
        self.waited = set()

    def start(self):
        for copy in self.copies:
            copy.start()

    def get(self, *parts):
        for n in parts or range(len(self.copies)):
            if n not in self.waited:
                self.copies[n].wait()
                self.waited.add(n)
        return self.buffer


class Stored:
    def __init__(self, copies, buffer):
        self.copies = copies
        self.buffer = buffer
        self.shape = buffer.shape
        self.sent = set()

    def send(self, *parts):
        for n in parts or range(len(self.copies)):
            if n not in self.sent:
                self.copies[n].start()
                self.sent.add(n)


def run_whole(
    body, outs, args, flops, scratch=(), vmem=32, smem=0, transcendentals=0, after=(), fetch=None, store=None,
    far_in=(), far_out=(), far_after=()
):
    fetch, store = fetch or {}, store or {}
    after = (*after, *[pltpu.with_memory_space_constraint(a, pltpu.HBM) for a in far_after])
    count, extra, n_out = len(args), len(after), len(outs)
    fetch = {i: [()] if places is None else places for i, places in fetch.items()}
    store = {i: [()] if places is None else places for i, places in store.items()}
    n_copies = sum(len(places) for places in (*fetch.values(), *store.values()))

    def kernel(*refs):
        ins = list(refs[:count])
        results = list(refs[count + extra : count + extra + n_out])
        rest = refs[count + extra + n_out :]
        own, rest = rest[: len(scratch)], list(rest[len(scratch) :])
        semaphores = rest.pop() if n_copies else None
        used = 0
        for i, places in fetch.items():
            buffer = rest.pop(0)
            copies = []
            for place in places:
                source, target = (ins[i].at[place], buffer.at[place]) if place else (ins[i], buffer)
                copies.append(pltpu.make_async_copy(source, target, semaphores.at[used]))
                used += 1
            ins[i] = Fetched(copies, buffer)
            ins[i].start()
        for i, places in store.items():
            buffer = rest.pop(0)
            copies = []
            for place in places:
                source, target = (buffer.at[place], results[i].at[place]) if place else (buffer, results[i])
                copies.append(pltpu.make_async_copy(source, target, semaphores.at[used]))
                used += 1
            results[i] = Stored(copies, buffer)
        body(*ins, *results, *own)
        for i in fetch:
            ins[i].get()
        for i in store:
            results[i].send()
        for i in store:
            for copy in results[i].copies:
                copy.wait()

    estimate = cost(flops, args, outs, transcendentals)
    buffers = [pltpu.VMEM(args[i].shape, args[i].dtype) for i in fetch]
    buffers += [pltpu.VMEM(outs[i].shape, outs[i].dtype) for i in store]
    if n_copies:
        buffers.append(pltpu.SemaphoreType.DMA((n_copies,)))
    args = [pltpu.with_memory_space_constraint(a, pltpu.HBM) if i in far_in else a for i, a in enumerate(args)]
    outs = [pltpu.HBM(o.shape, o.dtype) if i in store or i in far_out else o for i, o in enumerate(outs)]
    anywhere = pl.BlockSpec(memory_space=pl.ANY)
    specs = [in_smem() if i < smem else anywhere if i in fetch else in_vmem() for i in range(count)]
    return pl.pallas_call(
        kernel,
        out_shape=outs,
        in_specs=specs + [anywhere] * extra,
        out_specs=[anywhere if i in store else in_vmem() for i in range(n_out)],
        scratch_shapes=list(scratch) + buffers,
        compiler_params=pltpu.CompilerParams(vmem_limit_bytes=vmem * MIB),
        cost_estimate=estimate,
    )(*args, *after)


def hold(arrays, after):
    count = len(arrays)

    def kernel(*refs):
        for source, target in zip(refs[:count], refs[count + len(after) :]):
            target[...] = source[...]
        token = refs[-1]
        token[...] = jnp.zeros_like(token)

    anywhere = pl.BlockSpec(memory_space=pl.ANY)
    return pl.pallas_call(
        kernel,
        out_shape=[struct(a.shape, a.dtype) for a in arrays] + [struct((8, 128), F32)],
        in_specs=[in_vmem()] * count + [anywhere] * len(after),
        out_specs=[in_vmem()] * (count + 1),
        compiler_params=pltpu.CompilerParams(vmem_limit_bytes=16 * MIB),
        cost_estimate=pl.CostEstimate(flops=0, bytes_accessed=0, transcendentals=0),
    )(*arrays, *after)


def swap(values, axis, bit):
    size = lax.axis_size(axis)
    return lax.ppermute(values, axis, [(i, i ^ bit) for i in range(size)])


def bits_of(axis):
    size = lax.axis_size(axis)
    return [1 << i for i in range(size.bit_length() - 1)]


def head_order(width):
    half = width // 2
    source = iota((width, width), 0)
    target = iota((width, width), 1)
    wanted = (target % half) // HALF * HD + target // half * HALF + target % HALF
    return (source == wanted).astype(BF16)


def same_head(lanes):
    return (iota((lanes, lanes), 0) // HALF == iota((lanes, lanes), 1) // HALF).astype(BF16)


def head_total(values, ones):
    high = values.astype(BF16)
    low = (values - high.astype(F32)).astype(BF16)
    return dot(high, ones) + dot(low, ones)


def rope_head(lanes):
    half = lanes // 2
    return iota((1, lanes), 1) % half // HALF


def value_head(lanes):
    return iota((1, lanes), 1) // HD


def project_kernel(first, xa, xb, wq, wk, wv, gain, cos, sin, *refs):
    fars, (wq_s, wk_s) = refs[:7], refs[-2:]
    nears = refs[7:10] if len(refs) > 9 else None
    qi_out, ki_out, cos_far, sin_far = fars[:4]
    width = wq.shape[1]
    half = width // 2
    order = head_order(width)
    ones = same_head(half)
    wq_s[...] = dot(wq.get()[...], order).astype(BF16)
    wk_s[...] = dot(wk.get()[...], order).astype(BF16)
    cos_far.buffer[...] = cos[first : first + 2]
    sin_far.buffer[...] = sin[first : first + 2]
    cos_far.send()
    sin_far.send()
    for index, source in enumerate((xa, xb)):
        rows = source.get()[...] if isinstance(source, Fetched) else source[...]
        c, s = cos[first + index], sin[first + index]
        for weights, unit_out, inverse_out in ((wq_s, fars[4], qi_out), (wk_s, fars[5], ki_out)):
            full = dot(rows, weights[...])
            a, b = full[:, :half], full[:, half:]
            inverse = lax.rsqrt(head_total(a * a + b * b, ones) + EPS)
            inverse_out.buffer[index] = inverse
            unit_out.buffer[index, :, :half] = ((a * c - b * s) * inverse * gain[:, :half]).astype(BF16)
            unit_out.buffer[index, :, half:] = ((b * c + a * s) * inverse * gain[:, half:]).astype(BF16)
            inverse_out.send(index)
            unit_out.send(index)
        fars[6].buffer[index] = dot(rows, wv.get()[...]).astype(BF16)
        fars[6].send(index)
    if nears:
        for near, far in zip(nears, fars[4:]):
            near[...] = far.buffer[...]


def project(first, xa, xb, wq, wk, wv, gain, cos, sin):
    rows, depth = xa.shape
    width = wq.shape[1]
    low = [struct((2, rows, width), BF16)] * 3
    outs = [struct((2, rows, width // 2), F32)] * 4 + low
    args = (xa, xb, wq, wk, wv, gain, cos, sin)
    early = first == 0
    by_row = [(0,), (1,)]
    results = run_whole(
        functools.partial(project_kernel, first), outs if early else outs + low, args,
        2 * 2 * rows * depth * width * 3, [pltpu.VMEM((depth, width), BF16)] * 2, vmem=24,
        far_in=(0, 2, 3, 4) if early else (2, 3, 4),
        fetch={2: None, 3: None, 0: None, 4: None} if early else {2: None, 3: None, 4: None},
        store={0: by_row, 1: by_row, 2: None, 3: None, 4: by_row, 5: by_row, 6: by_row},
    )
    return [*results[:7], *results[-3:]]


def pair_mask(seg_query, seg_key, query_block, key_block, query_dim, rows):
    allowed = seg_query == seg_key
    if query_block == key_block:
        query_id = iota((rows, rows), query_dim)
        key_id = iota((rows, rows), 1 - query_dim)
        allowed = (allowed & (key_id <= query_id)) | (key_id == query_id)
    return allowed


def column(row):
    return jnp.broadcast_to(row, (8, row.shape[1])).T[:, :1]


def join_pairs(buffer, first, second):
    buffer[0:2] = first[...]
    buffer[2:4] = second[...]


def attend_kernel(
    heads, me, q01, q23, k01, k23, v01, v23, seg_col, seg_row, head_out, inv_out, give_out, q, k, v, kbuf, vbuf
):
    blocks, rows, width = kbuf.shape
    join_pairs(q, q01, q23)
    join_pairs(k, k01, k23)
    join_pairs(v, v01, v23)
    mine = me[0, 0]
    q_head = rope_head(width)
    v_head = value_head(width)
    for block in range(blocks):
        slot = jnp.bitwise_xor(mine, block)
        kbuf[block] = k[slot]
        vbuf[block] = v[slot]
    for block in range(blocks):
        slot = jnp.bitwise_xor(mine, block)
        queries = q[slot]
        seg_q = column(seg_col[slot])
        count = block + 1
        allowed = jnp.concatenate(
            [
                pair_mask(seg_q, seg_row[jnp.bitwise_xor(mine, other)], block, other, 0, rows)
                for other in range(count)
            ],
            axis=1,
        )
        keys = kbuf[0:count].reshape(count * rows, width)
        values = vbuf[0:count].reshape(count * rows, width)
        inverse = jnp.zeros((rows, width), F32)
        mixed = jnp.zeros((rows, width), F32)
        for h in range(heads):
            scores = dot_nt(jnp.where(q_head == h, queries, jnp.zeros_like(queries)), keys)
            weight = jnp.where(allowed, jnp.exp2(scores * EXP_SCALE), 0.0)
            total = jnp.sum(weight, axis=1, keepdims=True)
            inverse = jnp.where(v_head == h, 1.0 / total, inverse)
            mixed = jnp.where(v_head == h, dot(weight.astype(BF16), values), mixed)
        inv_out[slot] = inverse
        head_out[slot] = (mixed * inverse).astype(BF16)
    give_out[0] = head_out[1]
    give_out[1] = head_out[3]


def attend(me, q, k, v, seg_col, seg_row, after):
    _, rows, width = q[0].shape
    blocks = 4
    heads = width // HD
    outs = [
        struct((blocks, rows, width), BF16),
        struct((blocks, rows, width), F32),
        struct((2, rows, width), BF16),
    ]
    args = (me, *q, *k, *v, seg_col, seg_row)
    scratch = [pltpu.VMEM((blocks, rows, width), BF16)] * 5
    return run_whole(
        functools.partial(attend_kernel, heads), outs, args,
        10 * heads * 2 * 2 * rows * rows * width, scratch, vmem=24, smem=1, after=after, far_out=(1,), far_in=(1, 3, 5),
    )


def out_project_kernel(heads, got, w_out, w_core, own, far):
    far[...] = (dot(heads[2], w_out[...]) + dot(got[1], w_core[...])).astype(BF16)
    own[...] = dot(heads[0], w_out[...]) + dot(got[0], w_core[...])


def out_project(heads, got, w_out, w_core):
    _, rows, width = heads.shape
    depth = w_out.shape[1]
    outs = [struct((rows, depth), F32), struct((rows, depth), BF16)]
    return run_whole(
        out_project_kernel, outs, (heads, got, w_out, w_core), 2 * 4 * rows * width * depth, vmem=16, far_in=(2,),
    )


def head_back_kernel(near, far, w_out, w_core, mine, give):
    part, depth = near.shape
    for i, source in enumerate((near, far)):
        span = slice(i * part, (i + 1) * part)
        rows = source[...]
        mine[span] = dot_nt(rows, w_out[...]).astype(BF16)
        give[span, :depth] = rows
        give[span, depth:] = dot_nt(rows, w_core[...]).astype(BF16)


def head_back(near, far, w_out, w_core, after):
    part, depth = near.shape
    width = w_out.shape[0]
    outs = [struct((2 * part, width), BF16), struct((2 * part, depth + width), BF16)]
    return run_whole(
        head_back_kernel, outs, (near, far, w_out, w_core), 2 * 4 * part * width * depth, vmem=16, after=after, far_in=(2,),
    )


def attend_back_kernel(
    heads, me, mine0, mine1, got0, got1, q01, q23, k01, k23, v01, v23, head_out, inv, qi01, qi23, ki01, ki23,
    seg_col, seg_row, gain, cos01, cos23, sin01, sin23, joined, scale_out, q, k, v, qm, km, dm, row_dot, dq, dk, dv,
):
    blocks, rows, width = q.shape
    inv = inv.get()
    join_pairs(q, q01.get(), q23.get())
    join_pairs(k, k01.get(), k23.get())
    join_pairs(v, v01.get(), v23.get())
    half = width // 2
    part = rows // PARTS
    depth = got0.shape[1] - width
    self_id = me[0, 0]
    q_head = rope_head(width)
    v_head = value_head(width)
    picks = (iota((8, width), 0) == iota((8, width), 1) // HD).astype(BF16)
    for slot in range(blocks):
        for c in range(PARTS):
            span = slice(c * part, (c + 1) * part)
            at = slice(slot // 2 * part, (slot // 2 + 1) * part)
            grads = (mine0, mine1)[c][at] if slot % 2 == 0 else (got0, got1)[c][at, depth:]
            scaled = (grads.astype(F32) * inv[slot, span]).astype(BF16)
            product = scaled.astype(F32) * head_out[slot, span].astype(F32)
            high = product.astype(BF16)
            low = (product - high.astype(F32)).astype(BF16)
            dots = dot_nt(picks, high) + dot_nt(picks, low)
            for h in range(heads):
                start = h * rows + c * part
                dm[slot, start : start + part] = jnp.where(v_head == h, scaled, jnp.zeros_like(scaled))
                row_dot[slot, :, start : start + part] = dots[h : h + 1]
        queries, keys = q[slot], k[slot]
        for h in range(heads):
            at = slice(h * rows, (h + 1) * rows)
            qm[slot, at] = jnp.where(q_head == h, queries, jnp.zeros_like(queries))
            km[slot, at] = jnp.where(q_head == h, keys, jnp.zeros_like(keys))
    for block in range(blocks):
        slot = jnp.bitwise_xor(self_id, block)
        for other in range(block + 1):
            there = jnp.bitwise_xor(self_id, other)
            allowed = pair_mask(seg_row[slot], column(seg_col[there]), block, other, 1, rows)
            allowed = jnp.concatenate([allowed] * heads, axis=1)
            scores = dot_nt(k[there], qm[slot])
            weight = jnp.where(allowed, jnp.exp2(scores * EXP_SCALE), 0.0)
            grad = (weight * (dot_nt(v[there], dm[slot]) - row_dot[slot])).astype(BF16)
            d_value = dot(weight.astype(BF16), dm[slot])
            d_key = dot(grad, qm[slot])
            stacked = jnp.concatenate([grad[:, h * rows : (h + 1) * rows] for h in range(heads)], axis=0)
            d_query = dot_tn(stacked, km[there])
            if other == block:
                dv[there] = d_value
                dk[there] = d_key
            else:
                dv[there] += d_value
                dk[there] += d_key
            if other == 0:
                dq[slot] = d_query
            else:
                dq[slot] += d_query
    order = head_order(width)
    ones = same_head(half)
    scale_sum = jnp.zeros((1, width), F32)
    for slot in range(blocks):
        c, s = [pair[slot // 2].get()[slot % 2] for pair in ((cos01, cos23), (sin01, sin23))]
        for place, (grad_ref, unit_ref, inv_ref) in enumerate(
            ((dq, q, (qi01, qi23)), (dk, k, (ki01, ki23)))
        ):
            inverse = inv_ref[slot // 2].get()[slot % 2]
            grads = grad_ref[slot] * SCORE_ROOT
            normed = unit_ref[slot].astype(F32) / gain[...]
            scale_sum = scale_sum + jnp.sum(normed * grads, axis=0, keepdims=True)
            grads = grads * gain[...]
            product = normed * grads
            along = head_total(product[:, :half] + product[:, half:], ones)
            a = (grads[:, :half] - normed[:, :half] * along) * inverse
            b = (grads[:, half:] - normed[:, half:] * along) * inverse
            turned = jnp.concatenate([(a * c + b * s).astype(BF16), (b * c - a * s).astype(BF16)], axis=1)
            joined[slot, :, place * width : (place + 1) * width] = dot_nt(turned, order).astype(BF16)
        joined[slot, :, 2 * width : 3 * width] = dv[slot].astype(BF16)
    scale_out[...] = jnp.zeros_like(scale_out)
    for h in range(heads):
        for side in range(2):
            at = side * half + h * HALF
            scale_out[2 * h + side : 2 * h + side + 1, :HALF] = scale_sum[:, at : at + HALF]


def attend_back(me, mine, got, q, k, v, head_out, inv, qi, ki, seg_col, seg_row, gain, cos, sin, after):
    blocks = 4
    _, rows, width = q[0].shape
    heads = width // HD
    outs = [struct((blocks, rows, 3 * width), BF16), struct((2 * heads, 128), F32)]
    args = (me, *mine, *got, *q, *k, *v, head_out, inv, *qi, *ki, seg_col, seg_row, gain, *cos, *sin)
    scratch = (
        [pltpu.VMEM((blocks, rows, width), BF16)] * 3
        + [pltpu.VMEM((blocks, heads * rows, width), BF16)] * 3
        + [pltpu.VMEM((blocks, 1, heads * rows), F32)]
        + [pltpu.VMEM((blocks, rows, width), F32)] * 3
    )
    return run_whole(
        functools.partial(attend_back_kernel, heads), outs, args,
        10 * heads * 5 * 2 * rows * rows * width, scratch, vmem=40, smem=1,
        fetch={i: None for i in (12, 5, 6, 7, 8, 9, 10, 13, 14, 15, 16, 20, 21, 22, 23)},
        far_in=(5, 6, 7, 8, 9, 10, 12, 13, 14, 15, 16, 20, 21, 22, 23), far_after=after,
    )


def input_grad_kernel(joined, wq, wk, wv, give_far, far, give, own):
    width = wq.shape[1]

    def rows_of(slot):
        out = dot_nt(joined[slot, :, :width], wq[...])
        out += dot_nt(joined[slot, :, width : 2 * width], wk[...])
        return out + dot_nt(joined[slot, :, 2 * width :], wv[...])

    give_far[...] = rows_of(3).astype(BF16)
    far[...] = rows_of(2)
    give[...] = rows_of(1).astype(BF16)
    own[...] = rows_of(0)


def input_grad(joined, wq, wk, wv, after, far_after):
    rows = joined.shape[1]
    depth, width = wq.shape
    outs = [struct((rows, depth), BF16), struct((rows, depth), F32)] * 2
    return run_whole(
        input_grad_kernel, outs, (joined, wq, wk, wv), 2 * 4 * rows * depth * width * 3, vmem=24, after=after, far_after=far_after, far_in=(1, 2, 3),
    )


def unit_rows(values):
    inverse = lax.rsqrt(jnp.sum(values * values, axis=-1, keepdims=True) + EPS)
    return values * inverse, inverse


def unit_back(grad_in, normed, inverse):
    return (grad_in - normed * jnp.sum(normed * grad_in, axis=-1, keepdims=True)) * inverse


def mix_attn_kernel(c, own, far, tokens, rate, *refs):
    low_out, sum_out, both_out = refs[-3:]
    part = sum_out.shape[0]
    span = slice(c * part, (c + 1) * part)
    total = own[span] + far[span].astype(F32)
    sum_out.buffer[...] = total.astype(BF16)
    sum_out.send()
    h_attn, _ = unit_rows(total)
    residual = tokens.get()[span].astype(F32)
    h_one, _ = unit_rows(residual + rate[...] * (h_attn - residual))
    low = h_one.astype(BF16)
    low_out[...] = low
    if c > 0:
        both_out = both_out.buffer
        both_out[: c * part] = refs[0][...]
    both_out[span] = low


def mix_mlp_kernel(c, own, far, h_one, rate, cotangent, *refs):
    out, low_out, mix_out, rate_out, both_out = refs[-5:]
    part = far.shape[0]
    span = slice(c * part, (c + 1) * part)
    total = far[...].astype(F32) + (own.get()[...] if c > 0 else own[...])
    h_mlp, mlp_inverse = unit_rows(total)
    first = h_one[...].astype(F32)
    away = h_mlp - first
    block_out, out_inverse = unit_rows(first + rate[...] * away)
    out.buffer[...] = block_out
    out.send()
    d_mix = unit_back(cotangent.get()[span].astype(F32), block_out, out_inverse)
    mix_out.buffer[...] = d_mix.astype(BF16)
    mix_out.send()
    rate_out[...] = jnp.sum(d_mix * away, axis=0, keepdims=True)
    low = unit_back(rate[...] * d_mix, h_mlp, mlp_inverse).astype(BF16)
    low_out[...] = low
    if c > 0:
        both_out = both_out.buffer
        both_out[: c * part] = refs[0][...]
    both_out[span] = low


def mix_back_kernel(c, own, far, d_mix_two, attn_sum, h_one, tokens, rate, mlp_rate, low_out, rest_out, rate_out):
    part = far.shape[0]
    span = slice(c * part, (c + 1) * part)
    h_attn, attn_inverse = unit_rows(attn_sum.get()[...].astype(F32))
    residual = tokens.get()[span].astype(F32)
    away = h_attn - residual
    _, one_inverse = unit_rows(residual + rate[...] * away)
    d_one = far[...].astype(F32) + (own.get()[...] if c == 0 else own[...])
    d_one = d_one + (1.0 - mlp_rate[...]) * d_mix_two.get()[...].astype(F32)
    d_mix = unit_back(d_one, h_one[...].astype(F32), one_inverse)
    rest_out.buffer[...] = (1.0 - rate[...]) * d_mix
    rest_out.send()
    rate_out[...] = jnp.sum(d_mix * away, axis=0, keepdims=True)
    low_out[...] = unit_back(rate[...] * d_mix, h_attn, attn_inverse).astype(BF16)


def silu_parts(gate):
    sig = 0.5 * jnp.tanh(0.5 * gate) + 0.5
    return sig, gate * sig


def load_kernel(*refs):
    sources, target, semaphores = refs[:-2], refs[-2], refs[-1]
    copies = [pltpu.make_async_copy(s, target.at[i], semaphores.at[i]) for i, s in enumerate(sources)]
    for copy in copies:
        copy.start()
    for copy in copies:
        copy.wait()


def load_weights(arrays, after):
    count = len(arrays)

    def kernel(*refs):
        load_kernel(*refs[:count], *refs[count + len(after) :])

    shape = (count,) + arrays[0].shape
    return pl.pallas_call(
        kernel,
        out_shape=struct(shape, BF16),
        in_specs=[pl.BlockSpec(memory_space=pl.ANY)] * (count + len(after)),
        out_specs=in_vmem(),
        scratch_shapes=[pltpu.SemaphoreType.DMA((count,))],
        compiler_params=pltpu.CompilerParams(vmem_limit_bytes=20 * MIB),
        cost_estimate=pl.CostEstimate(flops=0, bytes_accessed=0, transcendentals=0),
    )(*[pltpu.with_memory_space_constraint(a, pltpu.HBM) for a in arrays], *after)


def column_tiles(width, tile=512):
    return [(slice(None), slice(start, start + tile)) for start in range(0, width, tile)]


def feed_kernel(near, far, weights, scales, up_out, gate_out, hid_out, give, own, sent, rows):
    up_all, gate_all, hid = up_out.buffer, gate_out.buffer, hid_out.buffer
    part, depth = near.shape
    tile = 512
    width = hid.shape[1]
    rows[:part] = near[...]
    rows[part:] = far[...]
    for i in range(2):
        for n, start in enumerate(range(0, width, tile)):
            span = slice(start, start + tile)
            at = slice(i * width + start, i * width + start + tile)
            up = dot(rows[...], weights[3 * i, :, span])
            gate = dot(rows[...], weights[3 * i + 1, :, span])
            up_all[:, at] = up.astype(BF16)
            gate_all[:, at] = gate.astype(BF16)
            up_out.send(2 * i + n)
            gate_out.send(2 * i + n)
            _, active = silu_parts(scales[2 * i + 1 : 2 * i + 2, span] * gate)
            hidden = (scales[2 * i : 2 * i + 1, span] * up * active).astype(BF16)
            if i == 0:
                hid[:, span] = hidden
                hid_out.send(n)
            else:
                give[:, span] = hidden
    total = dot(hid[...], weights[2]) + dot(give[...], weights[5])
    own[...] = total[:part]
    sent[...] = total[part:].astype(BF16)


def feed(near, far, weights, scales, after, keep_own=False):
    part, depth = near.shape
    rows = 2 * part
    width = weights.shape[2]
    outs = [
        struct((rows, 2 * width), BF16), struct((rows, 2 * width), BF16), struct((rows, width), BF16),
        struct((rows, width), BF16), struct((part, depth), F32), struct((part, depth), BF16),
    ]
    return run_whole(
        feed_kernel, outs, (near, far, weights, scales), 12 * rows * depth * width,
        scratch=[pltpu.VMEM((rows, depth), BF16)], vmem=FEED_VMEM, after=after,
        store={0: column_tiles(2 * width), 1: column_tiles(2 * width), 2: column_tiles(width)},
        far_out=(4,) if keep_own else (),
    )


def feed_back_kernel(near, far, up_in, gate_in, weights, scales, d_up_out, d_gate_out, sums_out, give, own, sent, rows):
    d_up_all, d_gate_all = d_up_out.buffer, d_gate_out.buffer
    part, depth = near.shape
    tile = 512
    width = d_up_all.shape[1]
    rows[:part] = near[...]
    rows[part:] = far[...]
    for i in range(2):
        for n, start in enumerate(range(0, width, tile)):
            span = slice(start, start + tile)
            at = slice(i * width + start, i * width + start + tile)
            d_hidden = dot_nt(rows[...], weights[3 * i + 2, span])
            up_scale = scales[2 * i : 2 * i + 1, span]
            gate_scale = scales[2 * i + 1 : 2 * i + 2, span]
            up = up_in.get(2 * i + n)[:, at].astype(F32)
            gate = gate_in.get(2 * i + n)[:, at].astype(F32)
            scaled = gate_scale * gate
            sig, active = silu_parts(scaled)
            d_up_scaled = d_hidden * active
            d_gate_scaled = d_hidden * (up_scale * up) * (sig + active * (1.0 - sig))
            d_up = (d_up_scaled * up_scale).astype(BF16)
            d_gate = (d_gate_scaled * gate_scale).astype(BF16)
            sums_out[0:1, at] = jnp.sum(d_up_scaled * up, axis=0, keepdims=True)
            sums_out[1:2, at] = jnp.sum(d_gate_scaled * gate, axis=0, keepdims=True)
            if i == 0:
                d_up_all[:, span] = d_up
                d_gate_all[:, span] = d_gate
                d_up_out.send(n)
                d_gate_out.send(n)
            else:
                give[0, :, span] = d_up
                give[1, :, span] = d_gate
    total = dot_nt(d_up_all[...], weights[0]) + dot_nt(d_gate_all[...], weights[1])
    total += dot_nt(give[0], weights[3]) + dot_nt(give[1], weights[4])
    own[...] = total[:part]
    sent[...] = total[part:].astype(BF16)


def feed_back(near, far, up, gate, weights, scales, after, keep_own=False):
    part, depth = near.shape
    rows = 2 * part
    width = weights.shape[2]
    outs = [
        struct((rows, width), BF16), struct((rows, width), BF16), struct((2, 2 * width), F32),
        struct((2, rows, depth), BF16), struct((part, depth), F32), struct((part, depth), BF16),
    ]
    return run_whole(
        feed_back_kernel, outs, (near, far, up, gate, weights, scales), 12 * rows * depth * width,
        scratch=[pltpu.VMEM((rows, depth), BF16)], vmem=FEED_VMEM, after=after, fetch={2: column_tiles(2 * width), 3: column_tiles(2 * width)},
        far_in=(2, 3), store={0: column_tiles(width), 1: column_tiles(width)}, far_out=(4,) if keep_own else (),
    )


def view(ref, place):
    return ref.at[place] if place else ref


def piece_place(piece, bits):
    flags = [piece // bit % 2 for bit in bits]
    return flags[0], flags[1] + 2 * flags[2]


def weight_kernel(groups, orders, vectors, me, *refs):
    n_in = sum(len(left) + len(right) for left, right in groups) + (2 if vectors else 0)
    inputs = list(refs[:n_in])
    results = refs[n_in : n_in + 2 * len(orders)]
    targets = [r.buffer if isinstance(r, Stored) else r for r in results]
    turned = refs[-1]
    piece = 128
    count, half = turned.shape[0] // piece, turned.shape[0] // 2
    mine = me[0, 0]
    pieces = sorted(range(count), key=lambda j: (1 - piece_place(j, orders[0][0])[0], piece_place(j, orders[0][0])[1]))
    if vectors:
        table, short = inputs.pop(0), inputs.pop(0)
        for j in pieces:
            sent, position = piece_place(j, orders[0][0])
            target = targets[1 - sent]
            rows = target.shape[1] - piece
            owner = jnp.bitwise_xor(mine, j)
            line = table[pl.ds(owner, 1), :]
            extra = jnp.concatenate([short[pl.ds(owner, 1), :], jnp.zeros((1, line.shape[1] - 128), F32)], axis=1)
            row = iota((rows, line.shape[1]), 0)
            block = jnp.where(row == 0, line, jnp.where(row == 1, extra, 0.0))
            target[position, piece:] = block.astype(BF16)
    base = 0
    for left_places, right_places in groups:
        left = [(inputs.pop(0), place) for place in left_places]
        right = [(inputs.pop(0), place) for place in right_places]
        start = 0
        for source, place in left:
            ref = view(source.get(), place)
            for n, j in enumerate(pieces):
                at = jnp.bitwise_xor(mine, j) * piece
                columns = ref[:, pl.ds(pl.multiple_of(at, piece), piece)]
                turned[n * piece : (n + 1) * piece, start : start + ref.shape[0]] = columns.T
            start += ref.shape[0]
        for side in range(2):
            start = 0
            product = None
            for source, place in right:
                ref = view(source.get(), place)
                rows = ref.shape[0]
                part = dot(turned[side * half : (side + 1) * half, start : start + rows], ref[...])
                product = part if product is None else product + part
                start += rows
            product = product.astype(BF16)
            width = product.shape[1]
            begin = 0
            for n, (bits, columns) in enumerate(orders):
                first, last = max(base, begin), min(base + width, begin + columns)
                if first < last:
                    for i, j in enumerate(pieces[side * count // 2 : (side + 1) * count // 2]):
                        sent, position = piece_place(j, bits)
                        targets[2 * n + 1 - sent][position, :piece, first - begin : last - begin] = product[
                            i * piece : (i + 1) * piece, first - base : last - base
                        ]
                begin += columns
            if side == 1 and len(orders) == 1 and len(groups) == 1:
                results[1].send()
        base += width


def weight_halves(me, groups, n_groups, orders, after=(), far_after=(), vectors=()):
    depth = shape_at(groups[0][0][0])[1]
    rows = sum(shape_at(entry)[0] for entry in groups[0][0])
    piece = depth // n_groups
    outs = [
        struct((n_groups // 2, piece + (VECTOR_ROWS if vectors and n == 0 else 0), columns), BF16)
        for n, (_, columns) in enumerate(orders) for _ in range(2)
    ]
    entries = [entry for left, right in groups for entry in (*left, *right)]
    args = (me, *vectors, *[a for a, _, _ in entries])
    places = [([p for _, p, _ in left], [p for _, p, _ in right]) for left, right in groups]
    total = sum(columns for _, columns in orders)
    skip = 1 + len(vectors)
    results = run_whole(
        functools.partial(weight_kernel, places, orders, bool(vectors)), outs, args, 2 * rows * depth * total,
        [pltpu.VMEM((depth, rows), BF16)], vmem=40, smem=1, after=after,
        fetch={skip + i: [p] if p else None for i, (_, p, _) in enumerate(entries)},
        far_in=tuple(skip + i for i, (_, _, far) in enumerate(entries) if far), far_after=far_after,
        store={i: None for i in range(1, len(outs), 2)},
    )
    return [results[2 * n : 2 * n + 2] for n in range(len(orders))]


def merge_kernel(kept, got, *outs):
    count = kept.shape[0]
    kept, got = kept.get(), got.get()
    if count == 1:
        outs[0][...] = kept[0].astype(F32) + got[0].astype(F32)
        return
    for i in range(count // 2):
        outs[0][i] = (kept[2 * i + 1].astype(F32) + got[2 * i + 1].astype(F32)).astype(BF16)
    for i in range(count // 2):
        outs[1].buffer[i] = (kept[2 * i].astype(F32) + got[2 * i].astype(F32)).astype(BF16)


def merge(kept, got, after=(), far_after=()):
    count, rows, columns = kept.shape
    if count == 1:
        outs, store = [struct((rows, columns), F32)], {}
    else:
        outs, store = [struct((count // 2, rows, columns), BF16)] * 2, {1: None}
    return run_whole(
        merge_kernel, outs, (kept, got), kept.size, vmem=16, after=after, far_after=far_after, far_in=(0,),
        fetch={0: None, 1: None}, store=store,
    )


def shape_at(entry):
    array, place, _ = entry
    return jax.eval_shape(lambda x: x[place], array).shape if place else array.shape


def block_of(entry):
    array, place, _ = entry
    return array[place] if place else array


def weight_halves_plain(me, groups, n_groups, orders, after=(), far_after=(), vectors=()):
    products = [
        dot_tn(jnp.concatenate([block_of(e) for e in left], axis=0), jnp.concatenate([block_of(e) for e in right], axis=0))
        for left, right in groups
    ]
    product = jnp.concatenate(products, axis=1)
    parts = product.reshape(n_groups, product.shape[0] // n_groups, product.shape[1])
    order = jnp.bitwise_xor(me[0, 0], jnp.arange(n_groups, dtype=jnp.int32))
    parts = parts[order]
    results, start = [], 0
    for n, (_, columns) in enumerate(orders):
        chosen = parts[:, :, start : start + columns]
        if vectors and n == 0:
            table, short = [jnp.pad(v[order], ((0, 0), (0, columns - v.shape[1]))) for v in vectors]
            chosen = jnp.concatenate([chosen, table[:, None], short[:, None]], axis=1)
            chosen = jnp.pad(chosen, ((0, 0), (0, VECTOR_ROWS - 2), (0, 0)))
        chosen = chosen.reshape((n_groups // 2, 2) + chosen.shape[1:]).astype(BF16)
        results.append((chosen[:, 1], chosen[:, 0]))
        start += columns
    return results


def stage(pair, bit, after=(), far_after=()):
    kept, got = pair
    if kept.shape[1] >= 128:
        sent, kept = merge(kept, got, after, far_after)
    else:
        total = kept.astype(F32) + got.astype(F32)
        parts = total.reshape((kept.shape[0] // 2, 2) + kept.shape[1:]).astype(BF16)
        kept, sent = parts[:, 0], parts[:, 1]
    return kept, swap(sent, "dp", bit)


def last_stage(pair, bits):
    for bit in bits:
        pair = stage(pair, bit)
    kept, got = pair
    return (kept.astype(F32) + got.astype(F32))[0]


def shards(
    tokens,
    seq_lengths,
    w_query,
    w_key,
    w_value,
    w_out,
    qk_scale,
    attn_rate,
    w_up,
    w_gate,
    up_scale,
    gate_scale,
    w_down,
    mlp_rate,
    out_grad,
):
    local_rows, depth = tokens.shape
    n_mp = lax.axis_size("mp")
    n_dp = lax.axis_size("dp")
    assert n_mp == 4
    width = w_query.shape[1]
    hidden_width = w_up.shape[1]
    heads = width // HD
    part = local_rows // PARTS
    me = lax.axis_index("mp").astype(jnp.int32)
    me_ref = me.reshape(1, 1)
    group = lax.axis_index("dp").astype(jnp.int32)
    group_ref = group.reshape(1, 1)
    dp_bits = bits_of("dp")
    seq_count = seq_lengths.shape[1]

    far_tokens = swap(tokens, "mp", 2)
    core_tokens = swap(tokens, "mp", 1)
    ends = jnp.cumsum(seq_lengths[0])
    starts = jnp.concatenate([jnp.zeros((1,), jnp.int32), ends])
    owner = jnp.bitwise_xor(me, jnp.arange(n_mp, dtype=jnp.int32))
    row_ids = owner[:, None] * local_rows + jnp.arange(local_rows, dtype=jnp.int32)[None]
    segment = jnp.sum((row_ids[:, :, None] >= ends).astype(jnp.int32), axis=2)
    first = jnp.sum(
        jnp.where(segment[:, :, None] == jnp.arange(seq_count + 1, dtype=jnp.int32), starts, 0), axis=2
    )
    position = (row_ids - first).astype(F32)
    frequency = jnp.exp(jnp.arange(HALF, dtype=F32) * (-2.0 * math.log(10000.0) / HD))
    angles = position[:, :, None] * jnp.tile(frequency, heads)[None, None]
    cos, sin = jnp.cos(angles), jnp.sin(angles)
    seg_q = jnp.where(segment < seq_count, segment, -1).astype(F32)[:, None, :]
    seg_k = jnp.where(segment < seq_count, segment, -2).astype(F32)[:, None, :]
    gain = qk_scale.reshape(heads, 2, HALF).transpose(1, 0, 2).reshape(1, width)

    scale_rows = jnp.stack([up_scale, gate_scale * math.sqrt(depth)])
    core_out = swap(w_out, "mp", 1)
    core_rows = swap(scale_rows, "mp", 1)
    core_up = swap(w_up, "mp", 1)
    core_gate = swap(w_gate, "mp", 1)
    core_down = swap(w_down, "mp", 1)
    scales = jnp.concatenate([scale_rows, core_rows], axis=0)

    weights = (w_query, w_key, w_value)
    early = project(0, tokens, core_tokens, *weights, gain, cos, sin)
    far_tokens, _ = hold([far_tokens], (early[0], seg_q, seg_k))
    cross_tokens = swap(far_tokens, "mp", 1)
    late = project(2, far_tokens, cross_tokens, *weights, gain, cos, sin)
    qi, ki, cos_far, sin_far, q_far, k_far, v_far, q, k, v = zip(early, late)
    head_out, inv, give = attend(
        me_ref, q, k, v, seg_q, seg_k, (core_up, core_gate, core_down, core_out, core_rows)
    )
    attn_own, attn_far = out_project(head_out, swap(give, "mp", 1), w_out, core_out)
    feed_weights = load_weights([w_up, w_gate, w_down, core_up, core_gate, core_down], (attn_own,))
    attn_far = swap(attn_far, "mp", 2)

    attn_row = attn_rate.reshape(1, depth)
    mlp_row = mlp_rate.reshape(1, depth)
    full, lowered, vector = struct((part, depth), F32), struct((part, depth), BF16), struct((1, depth), F32)
    both = struct((2 * part, depth), BF16)

    def rows_place(c):
        return [(slice(c * part, (c + 1) * part),)]

    def mix_attn(c, after, *before):
        return run_whole(
            functools.partial(mix_attn_kernel, c), [lowered, lowered, both],
            (attn_own, attn_far, tokens, attn_row, *before), 20 * part * depth, vmem=16, after=after,
            far_in=(2,), fetch={2: rows_place(c)}, store={1: None} if c == 0 else {1: None, 2: None},
        )

    def mix_mlp(c, own, far, h_one, after, *before):
        return run_whole(
            functools.partial(mix_mlp_kernel, c), [full, lowered, lowered, vector, both],
            (own, far, h_one, mlp_row, out_grad, *before), 30 * part * depth, vmem=16, after=after,
            far_in=(4,) if c == 0 else (0, 4), fetch={4: rows_place(c)} if c == 0 else {0: None, 4: rows_place(c)},
            store={0: None, 2: None} if c == 0 else {0: None, 2: None, 4: None},
        )

    def mix_back(c, own, far, after):
        return run_whole(
            functools.partial(mix_back_kernel, c), [lowered, full, vector],
            (own, far, mlp_mixes[c][2], attn_mixes[c][1], attn_mixes[c][0], tokens, attn_row, mlp_row),
            40 * part * depth, vmem=16, after=after, far_in=(2, 3, 5) if c else (0, 2, 3, 5), store={1: None},
            fetch={3: None, 5: rows_place(c), 2: None, **({} if c else {0: None})},
        )

    fast = depth // n_dp == 128 and len(dp_bits) == 3
    later_bits = [dp_bits[1], dp_bits[0], dp_bits[2]] if fast else dp_bits

    def weight_grad(groups, orders, after=(), far_after=(), vectors=()):
        run = weight_halves if fast else weight_halves_plain
        return run(group_ref, groups, n_dp, orders, after, far_after, vectors)

    def whole(array, far=False):
        return (array, (), far)

    def layer(array, i, far=False):
        return (array, (i,), far)

    def rows_of(array, c, far=False):
        return (array, (slice(c * part, (c + 1) * part),), far)

    def cross(array):
        return swap(array, "mp", 2)

    def core(array):
        return swap(array, "mp", 1)

    mix = mix_attn(0, (feed_weights,))
    near_a = mix[0]
    far_a = cross(near_a)
    attn_mixes = [mix, mix_attn(1, (near_a,), near_a)]

    near_rows = attn_mixes[1][2]
    near_b, token = hold([attn_mixes[1][0]], (far_a,))
    far_b = cross(near_b)
    core_near = core(near_rows)
    core_far_a = core(far_a)
    feed_a = feed(near_a, far_a, feed_weights, scales, (token,))

    sent, hidden, token = hold([feed_a[5], feed_a[3]], (far_b,))
    got = cross(sent)
    core_hid_a = core(hidden)
    core_far_b = core(far_b)
    feed_b = feed(near_b, far_b, feed_weights, scales, (token,), True)

    sent, hidden, token = hold([feed_b[5], feed_b[3]], (got, core_near, core_far_a, core_far_b))
    got_b = cross(sent)
    core_hid_b = core(hidden)
    mlp_mixes = [mix_mlp(0, feed_a[4], got, near_a, (token,))]
    d_near_a = mlp_mixes[0][1]
    d_far_a = cross(d_near_a)

    back_weights = load_weights([w_up, w_gate, w_down, core_up, core_gate, core_down], (d_near_a,))
    mix = mix_mlp(1, feed_b[4], got_b, near_b, (d_far_a, core_hid_a, back_weights), d_near_a)
    mlp_mixes.append(mix)
    d_near_b, d_near_rows = mix[1], mix[4]
    d_far_b = cross(d_near_b)
    core_d_near = core(d_near_rows)
    core_d_far_a = core(d_far_a)
    back_a = feed_back(d_near_a, d_far_a, *feed_a[:2], back_weights, scales, (d_near_b,), True)

    sent, give_a, token = hold([back_a[5], back_a[3]], (d_far_b, core_hid_b))
    got_a = cross(sent)
    core_give_a = core(give_a)
    core_d_far_b = core(d_far_b)
    back_b = feed_back(d_near_b, d_far_b, *feed_b[:2], back_weights, scales, (token,))
    (down,) = weight_grad(
        [(
            [rows_of(d_near_rows, 0, True), whole(d_far_a), rows_of(d_near_rows, 1, True), whole(d_far_b),
             rows_of(core_d_near, 0), whole(core_d_far_a), rows_of(core_d_near, 1), whole(core_d_far_b)],
            [whole(feed_a[2], True), whole(feed_b[2], True), whole(core_hid_a), whole(core_hid_b)],
        )],
        [(dp_bits, hidden_width)], (back_b[2],),
    )

    sent, give_b, down_sent, token = hold([back_b[5], back_b[3], down[0]], (got_a,))
    got_b = cross(sent)
    core_give_b = core(give_b)
    down = (down[1], swap(down_sent, "dp", dp_bits[0]))
    mix = mix_back(0, back_a[4], got_a, (token,))
    back_mixes = [mix]
    a_near_a = mix[0]
    a_far_a = cross(a_near_a)
    rows_in = [
        rows_of(near_rows, 0, True), whole(far_a), rows_of(near_rows, 1, True), whole(far_b),
        rows_of(core_near, 0, True), whole(core_far_a, True), rows_of(core_near, 1, True), whole(core_far_b, True),
    ]
    (grad_up,) = weight_grad(
        [(rows_in, [whole(back_a[0], True), whole(back_b[0], True), layer(core_give_a, 0), layer(core_give_b, 0)])],
        [(later_bits, hidden_width)], (a_near_a,),
    )

    up_sent, token = hold([grad_up[0]], (got_b, a_far_a))
    grad_up = (grad_up[1], swap(up_sent, "dp", later_bits[0]))
    mix = mix_back(1, back_b[4], got_b, (token,))
    back_mixes.append(mix)
    a_near_b = mix[0]
    a_far_b = cross(a_near_b)
    head_a = head_back(a_near_a, a_far_a, w_out, core_out, (a_near_b,))
    (grad_gate,) = weight_grad(
        [(rows_in, [whole(back_a[1], True), whole(back_b[1], True), layer(core_give_a, 1), layer(core_give_b, 1)])],
        [(dp_bits, hidden_width)], (head_a[0],),
    )

    gate_sent, head_give, token = hold([grad_gate[0], head_a[1]], (a_far_b, down[1]))
    grad_gate = (grad_gate[1], swap(gate_sent, "dp", dp_bits[0]))
    core_head_a = core(head_give)
    head_b = head_back(a_near_b, a_far_b, w_out, core_out, (token,))
    core_head_b = core(head_b[1])

    def pack_kernel(part_a, part_b, rate_a, rate_b, rate_c, rate_d, own_ref, core_ref):
        total = part_a[...] + part_b[...]
        own_ref[0:2] = total[:, :hidden_width]
        own_ref[2:3] = rate_a[...] + rate_b[...]
        own_ref[3:4] = rate_c[...] + rate_d[...]
        core_ref[0:2] = total[:, hidden_width:]
        core_ref[2:4] = own_ref[2:4]

    def pair_kernel(own_ref, got_ref, sum_ref, rate_ref):
        sum_ref[...] = own_ref[...] + got_ref[...]
        rate_ref[...] = own_ref[2:4] + got_ref[2:4]

    def table_kernel(sum_ref, got_ref, table_ref):
        size = depth // n_dp
        rates = sum_ref[2:4] + got_ref[...]
        lines = [sum_ref[0:1], sum_ref[1:2] * math.sqrt(depth), rates[0:1], rates[1:2]]
        for n, line in enumerate(lines):
            for p in range(n_dp):
                table_ref[p : p + 1, n * size : (n + 1) * size] = line[:, p * size : (p + 1) * size]

    four = struct((4, depth), F32)
    assert hidden_width == depth
    own_sums, core_sums = run_whole(
        pack_kernel, [four, four],
        (back_a[2], back_b[2], *[m[2] for m in back_mixes], *[m[3] for m in mlp_mixes]),
        0, vmem=8, after=(head_b[0],),
    )
    core_sums = core(core_sums)
    down = stage(down, dp_bits[1], (own_sums,))
    joined, qk_rows = attend_back(
        me_ref, [head_a[0], head_b[0]], [core_head_a, core_head_b], q_far, k_far, v_far, head_out, inv, qi, ki,
        seg_k, seg_q, gain, cos_far, sin_far, down[:1],
    )

    def attn_rows(array, half):
        return (array, (slice(half * part, (half + 1) * part), slice(0, depth)), False)

    pair_sums, rates = run_whole(pair_kernel, [four, struct((2, depth), F32)], (own_sums, core_sums), 0, vmem=8,
                                 after=(qk_rows,))
    rates = cross(rates)
    grad_up = stage(grad_up, later_bits[1], (pair_sums,))
    if fast:
        (table,) = run_whole(
            table_kernel, [struct((n_dp, 4 * depth // n_dp), F32)], (pair_sums, rates), 0, vmem=8,
            far_after=grad_up[:1],
        )
    else:
        rates = pair_sums[2:4] + rates
        lines = [pair_sums[0], pair_sums[1] * math.sqrt(depth), rates[0], rates[1]]
        table = jnp.concatenate([line.reshape(n_dp, -1) for line in lines], axis=1)
        qk_rows = qk_rows[:, :HALF].reshape(n_dp, -1)
    token_rows = [whole(tokens, True), whole(core_tokens), whole(far_tokens), whole(cross_tokens)]
    first, second = weight_grad(
        [
            (
                [attn_rows(x, half) for pair in ((head_give, head_b[1]), (core_head_a, core_head_b))
                 for half in range(2) for x in pair],
                [layer(head_out, slot) for slot in (0, 2, 1, 3)],
            ),
            (token_rows, [layer(joined, slot) for slot in range(4)]),
        ],
        [(dp_bits, 2 * width), (later_bits, 2 * width)], vectors=(table, qk_rows),
    )
    chain = first[0]
    first = (first[1], swap(first[0], "dp", dp_bits[0]))
    second = (second[1], swap(second[0], "dp", later_bits[0]))
    grad_gate = stage(grad_gate, dp_bits[1], (chain,))
    down = stage(down, dp_bits[2], (), grad_gate[:1])
    give_far, far, give, own = input_grad(joined, *weights, (), down[:1])
    far_grad = cross((far + core(give_far).astype(F32)).astype(BF16))
    got = core(give)
    grad_up = stage(grad_up, later_bits[2], (own,))
    grad_gate = stage(grad_gate, dp_bits[2], (), grad_up[:1])
    first = stage(first, dp_bits[1], (), grad_gate[:1])
    second = stage(second, later_bits[1], (), first[:1])
    first = stage(first, dp_bits[2], (), second[:1])
    second = stage(second, later_bits[2], (), first[:1])
    down, grad_up, grad_gate, first, second = [
        last_stage(pair, dp_bits[3:]) for pair in (down, grad_up, grad_gate, first, second)
    ]
    block_out = jnp.concatenate([m[0] for m in mlp_mixes], axis=0)
    rests = jnp.concatenate([m[1] for m in back_mixes], axis=0)
    token_grad = rests + (own + got.astype(F32) + far_grad.astype(F32))
    size = depth // n_dp
    line = first[size]
    return (
        block_out,
        token_grad,
        first[:size, width:],
        second[:, :width],
        second[:, width:],
        first[:size, :width].T,
        first[size + 1, : width // n_dp],
        line[2 * size : 3 * size],
        grad_up,
        grad_gate,
        line[:size],
        line[size : 2 * size],
        down.T,
        line[3 * size : 4 * size],
    )


def solution(mesh):
    in_specs = (
        P(("dp", "mp"), None),
        P("dp", None),
        P(None, "mp"),
        P(None, "mp"),
        P(None, "mp"),
        P("mp", None),
        P("mp"),
        P(),
        P(None, "mp"),
        P(None, "mp"),
        P("mp"),
        P("mp"),
        P("mp", None),
        P(),
        P(("dp", "mp"), None),
    )
    out_specs = (
        P(("dp", "mp"), None),
        P(("dp", "mp"), None),
        P("dp", "mp"),
        P("dp", "mp"),
        P("dp", "mp"),
        P("mp", "dp"),
        P(("mp", "dp")),
        P("dp"),
        P("dp", "mp"),
        P("dp", "mp"),
        P(("mp", "dp")),
        P(("mp", "dp")),
        P("mp", "dp"),
        P("dp"),
    )
    return jax.shard_map(shards, mesh=mesh, in_specs=in_specs, out_specs=out_specs, check_vma=False)
```

```python
import functools
import math

import jax
import jax.numpy as jnp
from jax import lax
from jax.experimental import pallas as pl
from jax.experimental.pallas import tpu as pltpu
from jax.sharding import PartitionSpec as P

HD = 64
HALF = HD // 2
EPS = 1e-06
F32 = jnp.float32
BF16 = jnp.bfloat16
SCORE_ROOT = math.sqrt(HD)
EXP_SCALE = SCORE_ROOT * math.log2(math.e)
MIB = 1 << 20
PARTS = 2
FEED_VMEM = 24
VECTOR_ROWS = 16


def dot(left, right):
    return lax.dot_general(left, right, (((1,), (0,)), ((), ())), preferred_element_type=F32)


def dot_nt(left, right):
    return lax.dot_general(left, right, (((1,), (1,)), ((), ())), preferred_element_type=F32)


def dot_tn(left, right):
    return lax.dot_general(left, right, (((0,), (0,)), ((), ())), preferred_element_type=F32)


def iota(shape, dim):
    return lax.broadcasted_iota(jnp.int32, shape, dim)


def struct(shape, dtype):
    return jax.ShapeDtypeStruct(shape, dtype)


def in_vmem():
    return pl.BlockSpec(memory_space=pltpu.VMEM)


def in_smem():
    return pl.BlockSpec(memory_space=pltpu.SMEM)


def cost(flops, args, outs, transcendentals=0):
    moved = sum(a.size * a.dtype.itemsize for a in args)
    moved += sum(math.prod(o.shape) * jnp.dtype(o.dtype).itemsize for o in outs)
    return pl.CostEstimate(flops=int(flops), bytes_accessed=int(moved), transcendentals=int(transcendentals))


class Fetched:
    def __init__(self, copies, buffer):
        self.copies = copies
        self.buffer = buffer
        self.shape = buffer.shape
        self.waited = set()

    def start(self):
        for copy in self.copies:
            copy.start()

    def get(self, *parts):
        for n in parts or range(len(self.copies)):
            if n not in self.waited:
                self.copies[n].wait()
                self.waited.add(n)
        return self.buffer


class Stored:
    def __init__(self, copies, buffer):
        self.copies = copies
        self.buffer = buffer
        self.shape = buffer.shape
        self.sent = set()

    def send(self, *parts):
        for n in parts or range(len(self.copies)):
            if n not in self.sent:
                self.copies[n].start()
                self.sent.add(n)


def run_whole(
    body, outs, args, flops, scratch=(), vmem=32, smem=0, transcendentals=0, after=(), fetch=None, store=None,
    far_in=(), far_out=(), far_after=(), raw=(), load=(), save=(), carry=(), pile=()
):
    fetch, store = fetch or {}, store or {}
    after = (*after, *[pltpu.with_memory_space_constraint(a, pltpu.HBM) for a in far_after])
    count, extra, n_out = len(args), len(after), len(outs)
    fetch = {i: [()] if places is None else places for i, places in fetch.items()}
    store = {i: [()] if places is None else places for i, places in store.items()}
    n_copies = sum(len(places) for places in (*fetch.values(), *store.values()))
    n_copies += len(load) + len(save) + len(pile)
    sides = len(load) + len(save) + len(carry)

    def kernel(*refs):
        ins, refs = list(refs[:count]), refs[count + extra :]
        side_in, refs = refs[:sides], refs[sides:]
        heap, refs = refs[: len(pile)], refs[len(pile) :]
        results, refs = list(refs[:n_out]), refs[n_out:]
        side_out, rest = refs[:sides], refs[sides:]
        if pile:
            heap_out, rest = rest[0], rest[1:]
        own, rest = rest[: len(scratch)], list(rest[len(scratch) :])
        semaphores = rest.pop() if n_copies else None
        used = 0
        for i, places in fetch.items():
            buffer = rest.pop(0)
            copies = []
            for place in places:
                source, target = (ins[i].at[place], buffer.at[place]) if place else (ins[i], buffer)
                copies.append(pltpu.make_async_copy(source, target, semaphores.at[used]))
                used += 1
            ins[i] = Fetched(copies, buffer)
            ins[i].start()
        for i, places in store.items():
            buffer = rest.pop(0)
            copies = []
            for place in places:
                source, target = (buffer.at[place], results[i].at[place]) if place else (buffer, results[i])
                copies.append(pltpu.make_async_copy(source, target, semaphores.at[used]))
                used += 1
            results[i] = Stored(copies, buffer)
        moves = []
        for n in range(len(load) + len(save)):
            source = side_in[n]
            if n < len(load) and load[n][1]:
                source = source.at[load[n][1]]
            moves.append(pltpu.make_async_copy(source, side_out[n], semaphores.at[used]))
            used += 1
        start = 0
        for ref in heap:
            target = heap_out.at[start : start + ref.shape[0]]
            moves.append(pltpu.make_async_copy(ref, target, semaphores.at[used]))
            start += ref.shape[0]
            used += 1
        for move in moves:
            move.start()
        for n in range(len(load) + len(save), sides):
            side_out[n][...] = side_in[n][...]
        body(*ins, *results, *own)
        for i in fetch:
            ins[i].get()
        for i in store:
            results[i].send()
        for i in store:
            for copy in results[i].copies:
                copy.wait()
        for move in moves:
            move.wait()

    def in_hbm(array):
        return pltpu.with_memory_space_constraint(array, pltpu.HBM)

    estimate = cost(flops, args, outs, transcendentals)
    buffers = [pltpu.VMEM(args[i].shape, args[i].dtype) for i in fetch]
    buffers += [pltpu.VMEM(outs[i].shape, outs[i].dtype) for i in store]
    if n_copies:
        buffers.append(pltpu.SemaphoreType.DMA((n_copies,)))
    args = [in_hbm(a) if i in far_in else a for i, a in enumerate(args)]
    outs = [pltpu.HBM(o.shape, o.dtype) if i in store or i in far_out else o for i, o in enumerate(outs)]
    anywhere = pl.BlockSpec(memory_space=pl.ANY)
    specs = [
        in_smem() if i < smem else anywhere if i in fetch or i in raw else in_vmem() for i in range(count)
    ]
    side_args = [in_hbm(a) for a, _ in load] + [*save, *carry]
    side_outs = [struct(shape_at(entry), entry[0].dtype) for entry in load]
    side_outs += [pltpu.HBM(a.shape, a.dtype) for a in save] + [struct(a.shape, a.dtype) for a in carry]
    heap_shape = [pltpu.HBM((sum(a.shape[0] for a in pile), *pile[0].shape[1:]), pile[0].dtype)] if pile else []
    return pl.pallas_call(
        kernel,
        out_shape=outs + side_outs + heap_shape,
        in_specs=specs
        + [anywhere] * (extra + len(load)) + [in_vmem()] * (len(save) + len(carry)) + [anywhere] * len(pile),
        out_specs=[anywhere if i in store else in_vmem() for i in range(n_out)]
        + [in_vmem()] * len(load) + [anywhere] * len(save) + [in_vmem()] * len(carry) + [anywhere] * len(heap_shape),
        scratch_shapes=list(scratch) + buffers,
        compiler_params=pltpu.CompilerParams(vmem_limit_bytes=vmem * MIB),
        cost_estimate=estimate,
    )(*args, *after, *side_args, *pile)


def shape_at(entry):
    array, place = entry[:2]
    return jax.eval_shape(lambda x: x[place], array).shape if place else array.shape


def hold(arrays, after):
    count = len(arrays)

    def kernel(*refs):
        for source, target in zip(refs[:count], refs[count + len(after) :]):
            target[...] = source[...]
        token = refs[-1]
        token[...] = jnp.zeros_like(token)

    anywhere = pl.BlockSpec(memory_space=pl.ANY)
    return pl.pallas_call(
        kernel,
        out_shape=[struct(a.shape, a.dtype) for a in arrays] + [struct((8, 128), F32)],
        in_specs=[in_vmem()] * count + [anywhere] * len(after),
        out_specs=[in_vmem()] * (count + 1),
        compiler_params=pltpu.CompilerParams(vmem_limit_bytes=16 * MIB),
        cost_estimate=pl.CostEstimate(flops=0, bytes_accessed=0, transcendentals=0),
    )(*arrays, *after)


def swap(values, axis, bit):
    size = lax.axis_size(axis)
    return lax.ppermute(values, axis, [(i, i ^ bit) for i in range(size)])


def bits_of(axis):
    size = lax.axis_size(axis)
    return [1 << i for i in range(size.bit_length() - 1)]


def head_order(width):
    half = width // 2
    source = iota((width, width), 0)
    target = iota((width, width), 1)
    wanted = (target % half) // HALF * HD + target // half * HALF + target % HALF
    return (source == wanted).astype(BF16)


def same_head(lanes):
    return (iota((lanes, lanes), 0) // HALF == iota((lanes, lanes), 1) // HALF).astype(BF16)


def head_total(values, ones):
    high = values.astype(BF16)
    low = (values - high.astype(F32)).astype(BF16)
    return dot(high, ones) + dot(low, ones)


def rope_head(lanes):
    half = lanes // 2
    return iota((1, lanes), 1) % half // HALF


def value_head(lanes):
    return iota((1, lanes), 1) // HD


def project_kernel(first, xa, xb, wq, wk, wv, gain, cos, sin, *refs):
    fars, more = refs[:7], refs[7:10]
    qi_out, ki_out, cos_far, sin_far = fars[:4]
    width = wq.shape[1]
    half = width // 2
    ones = same_head(half)
    if first == 0:
        order = head_order(width)
        more[0][...] = dot(wq.get()[...], order).astype(BF16)
        more[1][...] = dot(wk.get()[...], order).astype(BF16)
        wq, wk = more[0], more[1]
        wv = wv.get()
        more[2][...] = wv[...]
    cos_far.buffer[...] = cos[first : first + 2]
    sin_far.buffer[...] = sin[first : first + 2]
    cos_far.send()
    sin_far.send()
    for index, source in enumerate((xa, xb)):
        rows = source.get()[...] if isinstance(source, Fetched) else source[...]
        c, s = cos[first + index], sin[first + index]
        for weights, unit_out, inverse_out in ((wq, fars[4], qi_out), (wk, fars[5], ki_out)):
            full = dot(rows, weights[...])
            a, b = full[:, :half], full[:, half:]
            inverse = lax.rsqrt(head_total(a * a + b * b, ones) + EPS)
            inverse_out.buffer[index] = inverse
            unit_out.buffer[index, :, :half] = ((a * c - b * s) * inverse * gain[:, :half]).astype(BF16)
            unit_out.buffer[index, :, half:] = ((b * c + a * s) * inverse * gain[:, half:]).astype(BF16)
            inverse_out.send(index)
            unit_out.send(index)
        fars[6].buffer[index] = dot(rows, wv[...]).astype(BF16)
        fars[6].send(index)
    if first > 0:
        for near, far in zip(more, fars[4:]):
            near[...] = far.buffer[...]


def project(first, xa, xb, wq, wk, wv, gain, cos, sin, **sides):
    rows, depth = xa.shape
    width = wq.shape[1]
    low = [struct((2, rows, width), BF16)] * 3
    outs = [struct((2, rows, width // 2), F32)] * 4 + low
    args = (xa, xb, wq, wk, wv, gain, cos, sin)
    early = first == 0
    outs = outs + ([struct((depth, width), BF16)] * 3 if early else low)
    by_row = [(0,), (1,)]
    return run_whole(
        functools.partial(project_kernel, first), outs, args, 2 * 2 * rows * depth * width * 3, vmem=24,
        far_in=(0, 2, 3, 4) if early else (), fetch={2: None, 3: None, 0: None, 4: None} if early else {},
        store={0: by_row, 1: by_row, 2: None, 3: None, 4: by_row, 5: by_row, 6: by_row}, **sides,
    )


def pair_mask(seg_query, seg_key, query_block, key_block, query_dim, rows):
    allowed = seg_query == seg_key
    if query_block == key_block:
        query_id = iota((rows, rows), query_dim)
        key_id = iota((rows, rows), 1 - query_dim)
        allowed = (allowed & (key_id <= query_id)) | (key_id == query_id)
    return allowed


def column(row):
    return jnp.broadcast_to(row, (8, row.shape[1])).T[:, :1]


def join_pairs(buffer, first, second):
    buffer[0:2] = first[...]
    buffer[2:4] = second[...]


def attend_kernel(
    heads, me, q01, q23, k01, k23, v01, v23, seg_col, seg_row, head_out, inv_out, give_out, q, k, v, kbuf, vbuf
):
    blocks, rows, width = kbuf.shape
    join_pairs(q, q01, q23)
    join_pairs(k, k01, k23)
    join_pairs(v, v01, v23)
    mine = me[0, 0]
    q_head = rope_head(width)
    v_head = value_head(width)
    for block in range(blocks):
        slot = jnp.bitwise_xor(mine, block)
        kbuf[block] = k[slot]
        vbuf[block] = v[slot]
    for block in range(blocks):
        slot = jnp.bitwise_xor(mine, block)
        queries = q[slot]
        seg_q = column(seg_col[slot])
        count = block + 1
        allowed = jnp.concatenate(
            [
                pair_mask(seg_q, seg_row[jnp.bitwise_xor(mine, other)], block, other, 0, rows)
                for other in range(count)
            ],
            axis=1,
        )
        keys = kbuf[0:count].reshape(count * rows, width)
        values = vbuf[0:count].reshape(count * rows, width)
        inverse = jnp.zeros((rows, width), F32)
        mixed = jnp.zeros((rows, width), F32)
        for h in range(heads):
            scores = dot_nt(jnp.where(q_head == h, queries, jnp.zeros_like(queries)), keys)
            weight = jnp.where(allowed, jnp.exp2(scores * EXP_SCALE), 0.0)
            total = jnp.sum(weight, axis=1, keepdims=True)
            inverse = jnp.where(v_head == h, 1.0 / total, inverse)
            mixed = jnp.where(v_head == h, dot(weight.astype(BF16), values), mixed)
        inv_out[slot] = inverse
        head_out[slot] = (mixed * inverse).astype(BF16)
    give_out[0] = head_out[1]
    give_out[1] = head_out[3]


def attend(me, q, k, v, seg_col, seg_row, after, **sides):
    _, rows, width = q[0].shape
    blocks = 4
    heads = width // HD
    outs = [
        struct((blocks, rows, width), BF16),
        struct((blocks, rows, width), F32),
        struct((2, rows, width), BF16),
    ]
    args = (me, *q, *k, *v, seg_col, seg_row)
    scratch = [pltpu.VMEM((blocks, rows, width), BF16)] * 5
    return run_whole(
        functools.partial(attend_kernel, heads), outs, args,
        10 * heads * 2 * 2 * rows * rows * width, scratch, vmem=24, smem=1, after=after, far_out=(1,), far_in=(1, 3, 5), **sides,
    )


def out_project_kernel(heads, got, w_out, w_core, own, far):
    far[...] = (dot(heads[2], w_out[...]) + dot(got[1], w_core[...])).astype(BF16)
    own[...] = dot(heads[0], w_out[...]) + dot(got[0], w_core[...])


def out_project(heads, got, w_out, w_core):
    _, rows, width = heads.shape
    depth = w_out.shape[1]
    outs = [struct((rows, depth), F32), struct((rows, depth), BF16)]
    return run_whole(
        out_project_kernel, outs, (heads, got, w_out, w_core), 2 * 4 * rows * width * depth, vmem=16,
    )


def head_back_kernel(near, far, w_out, w_core, mine, give):
    part, depth = near.shape
    for i, source in enumerate((near, far)):
        span = slice(i * part, (i + 1) * part)
        rows = source[...]
        mine[span] = dot_nt(rows, w_out[...]).astype(BF16)
        give[span, :depth] = rows
        give[span, depth:] = dot_nt(rows, w_core[...]).astype(BF16)


def head_back(near, far, w_out, w_core, after):
    part, depth = near.shape
    width = w_out.shape[0]
    outs = [struct((2 * part, width), BF16), struct((2 * part, depth + width), BF16)]
    return run_whole(
        head_back_kernel, outs, (near, far, w_out, w_core), 2 * 4 * part * width * depth, vmem=16, after=after,
    )


def attend_back_kernel(
    heads, me, mine0, mine1, got0, got1, q01, q23, k01, k23, v01, v23, head_out, inv, qi01, qi23, ki01, ki23,
    seg_col, seg_row, gain, cos01, cos23, sin01, sin23, joined, scale_out, q, k, v, qm, km, dm, row_dot, dq, dk, dv,
):
    blocks, rows, width = q.shape
    inv = inv.get()
    join_pairs(q, q01.get(), q23.get())
    join_pairs(k, k01.get(), k23.get())
    join_pairs(v, v01.get(), v23.get())
    half = width // 2
    part = rows // PARTS
    depth = got0.shape[1] - width
    self_id = me[0, 0]
    q_head = rope_head(width)
    v_head = value_head(width)
    picks = (iota((8, width), 0) == iota((8, width), 1) // HD).astype(BF16)
    for slot in range(blocks):
        for c in range(PARTS):
            span = slice(c * part, (c + 1) * part)
            at = slice(slot // 2 * part, (slot // 2 + 1) * part)
            grads = (mine0, mine1)[c][at] if slot % 2 == 0 else (got0, got1)[c][at, depth:]
            scaled = (grads.astype(F32) * inv[slot, span]).astype(BF16)
            product = scaled.astype(F32) * head_out[slot, span].astype(F32)
            high = product.astype(BF16)
            low = (product - high.astype(F32)).astype(BF16)
            dots = dot_nt(picks, high) + dot_nt(picks, low)
            for h in range(heads):
                start = h * rows + c * part
                dm[slot, start : start + part] = jnp.where(v_head == h, scaled, jnp.zeros_like(scaled))
                row_dot[slot, :, start : start + part] = dots[h : h + 1]
        queries, keys = q[slot], k[slot]
        for h in range(heads):
            at = slice(h * rows, (h + 1) * rows)
            qm[slot, at] = jnp.where(q_head == h, queries, jnp.zeros_like(queries))
            km[slot, at] = jnp.where(q_head == h, keys, jnp.zeros_like(keys))
    for block in range(blocks):
        slot = jnp.bitwise_xor(self_id, block)
        for other in range(block + 1):
            there = jnp.bitwise_xor(self_id, other)
            allowed = pair_mask(seg_row[slot], column(seg_col[there]), block, other, 1, rows)
            allowed = jnp.concatenate([allowed] * heads, axis=1)
            scores = dot_nt(k[there], qm[slot])
            weight = jnp.where(allowed, jnp.exp2(scores * EXP_SCALE), 0.0)
            grad = (weight * (dot_nt(v[there], dm[slot]) - row_dot[slot])).astype(BF16)
            d_value = dot(weight.astype(BF16), dm[slot])
            d_key = dot(grad, qm[slot])
            stacked = jnp.concatenate([grad[:, h * rows : (h + 1) * rows] for h in range(heads)], axis=0)
            d_query = dot_tn(stacked, km[there])
            if other == block:
                dv[there] = d_value
                dk[there] = d_key
            else:
                dv[there] += d_value
                dk[there] += d_key
            if other == 0:
                dq[slot] = d_query
            else:
                dq[slot] += d_query
    order = head_order(width)
    ones = same_head(half)
    scale_sum = jnp.zeros((1, width), F32)
    for slot in range(blocks):
        c, s = [pair[slot // 2].get()[slot % 2] for pair in ((cos01, cos23), (sin01, sin23))]
        for place, (grad_ref, unit_ref, inv_ref) in enumerate(
            ((dq, q, (qi01, qi23)), (dk, k, (ki01, ki23)))
        ):
            inverse = inv_ref[slot // 2].get()[slot % 2]
            grads = grad_ref[slot] * SCORE_ROOT
            normed = unit_ref[slot].astype(F32) / gain[...]
            scale_sum = scale_sum + jnp.sum(normed * grads, axis=0, keepdims=True)
            grads = grads * gain[...]
            product = normed * grads
            along = head_total(product[:, :half] + product[:, half:], ones)
            a = (grads[:, :half] - normed[:, :half] * along) * inverse
            b = (grads[:, half:] - normed[:, half:] * along) * inverse
            turned = jnp.concatenate([(a * c + b * s).astype(BF16), (b * c - a * s).astype(BF16)], axis=1)
            joined[slot, :, place * width : (place + 1) * width] = dot_nt(turned, order).astype(BF16)
        joined[slot, :, 2 * width : 3 * width] = dv[slot].astype(BF16)
    scale_out[...] = jnp.zeros_like(scale_out)
    for h in range(heads):
        for side in range(2):
            at = side * half + h * HALF
            scale_out[2 * h + side : 2 * h + side + 1, :HALF] = scale_sum[:, at : at + HALF]


def attend_back(me, mine, got, q, k, v, head_out, inv, qi, ki, seg_col, seg_row, gain, cos, sin, **sides):
    blocks = 4
    _, rows, width = q[0].shape
    heads = width // HD
    outs = [struct((blocks, rows, 3 * width), BF16), struct((2 * heads, 128), F32)]
    args = (me, *mine, *got, *q, *k, *v, head_out, inv, *qi, *ki, seg_col, seg_row, gain, *cos, *sin)
    scratch = (
        [pltpu.VMEM((blocks, rows, width), BF16)] * 3
        + [pltpu.VMEM((blocks, heads * rows, width), BF16)] * 3
        + [pltpu.VMEM((blocks, 1, heads * rows), F32)]
        + [pltpu.VMEM((blocks, rows, width), F32)] * 3
    )
    return run_whole(
        functools.partial(attend_back_kernel, heads), outs, args,
        10 * heads * 5 * 2 * rows * rows * width, scratch, vmem=40, smem=1,
        fetch={i: None for i in (12, 5, 6, 7, 8, 9, 10, 13, 14, 15, 16, 20, 21, 22, 23)},
        far_in=(5, 6, 7, 8, 9, 10, 12, 13, 14, 15, 16, 20, 21, 22, 23), **sides,
    )


def input_grad_kernel(joined, wq, wk, wv, give_far, far, give, own):
    width = wq.shape[1]

    def rows_of(slot):
        out = dot_nt(joined[slot, :, :width], wq[...])
        out += dot_nt(joined[slot, :, width : 2 * width], wk[...])
        return out + dot_nt(joined[slot, :, 2 * width :], wv[...])

    give_far[...] = rows_of(3).astype(BF16)
    far[...] = rows_of(2)
    give[...] = rows_of(1).astype(BF16)
    own[...] = rows_of(0)


def input_grad(joined, wq, wk, wv, after, far_after):
    rows = joined.shape[1]
    depth, width = wq.shape
    outs = [struct((rows, depth), BF16), struct((rows, depth), F32)] * 2
    return run_whole(
        input_grad_kernel, outs, (joined, wq, wk, wv), 2 * 4 * rows * depth * width * 3, vmem=24, after=after, far_after=far_after, far_in=(1, 2, 3),
    )


def add_far_kernel(far, got, sum_out):
    sum_out[...] = (far[...] + got[...].astype(F32)).astype(BF16)


def add_far(far, got, after):
    return run_whole(add_far_kernel, [struct(far.shape, BF16)], (far, got), far.size, vmem=16, after=after)[0]


def unit_rows(values):
    inverse = lax.rsqrt(jnp.sum(values * values, axis=-1, keepdims=True) + EPS)
    return values * inverse, inverse


def unit_back(grad_in, normed, inverse):
    return (grad_in - normed * jnp.sum(normed * grad_in, axis=-1, keepdims=True)) * inverse


def mix_attn_kernel(c, own, far, tokens, rate, *refs):
    part = refs[-3].shape[0]
    span = slice(c * part, (c + 1) * part)
    total = own[span] + far[span].astype(F32)
    h_attn, _ = unit_rows(total)
    residual = tokens[span].astype(F32)
    h_one, _ = unit_rows(residual + rate[...] * (h_attn - residual))
    low = h_one.astype(BF16)
    low_out, sum_out, both_out = refs[-3:]
    low_out[...] = low
    if c > 0:
        sum_out[: c * part] = refs[0][...]
        both_out[: c * part] = refs[1][...]
        sum_out[span] = total.astype(BF16)
        both_out[span] = low
    else:
        sum_out[...] = total.astype(BF16)
        both_out[...] = jnp.zeros_like(both_out)


def mix_mlp_kernel(c, own, far, h_one, rate, cotangent, *refs):
    out, low_out, mix_out, rate_out, both_out = refs[-5:]
    part = far.shape[0]
    total = own[...] + far[...].astype(F32)
    h_mlp, mlp_inverse = unit_rows(total)
    first = h_one[...].astype(F32)
    away = h_mlp - first
    block_out, out_inverse = unit_rows(first + rate[...] * away)
    (out if c > 0 else out.buffer)[...] = block_out
    d_mix = unit_back(cotangent[...].astype(F32), block_out, out_inverse)
    (mix_out if c > 0 else mix_out.buffer)[...] = d_mix.astype(BF16)
    if c == 0:
        out.send()
        mix_out.send()
    rate_out[...] = jnp.sum(d_mix * away, axis=0, keepdims=True)
    low = unit_back(rate[...] * d_mix, h_mlp, mlp_inverse).astype(BF16)
    low_out[...] = low
    if c > 0:
        both_out[: c * part] = refs[0][...]
        both_out[c * part :] = low
    else:
        both_out[...] = jnp.zeros_like(both_out)


def mix_back_kernel(own, far, d_mix_two, attn_sum, h_one, tokens, rate, mlp_rate, low_out, rest_out, rate_out):
    h_attn, attn_inverse = unit_rows(attn_sum[...].astype(F32))
    residual = tokens[...].astype(F32)
    away = h_attn - residual
    _, one_inverse = unit_rows(residual + rate[...] * away)
    d_one = own[...] + far[...].astype(F32)
    d_one = d_one + (1.0 - mlp_rate[...]) * d_mix_two[...].astype(F32)
    d_mix = unit_back(d_one, h_one[...].astype(F32), one_inverse)
    rest_out[...] = (1.0 - rate[...]) * d_mix
    rate_out[...] = jnp.sum(d_mix * away, axis=0, keepdims=True)
    low_out[...] = unit_back(rate[...] * d_mix, h_attn, attn_inverse).astype(BF16)


def silu_parts(gate):
    sig = 0.5 * jnp.tanh(0.5 * gate) + 0.5
    return sig, gate * sig


def load_weights(arrays, kept, after, **sides):
    count = len(arrays)

    def kernel(*refs):
        sources, rest = refs[: count + len(kept)], refs[count + len(kept) :]
        target, kept_here, semaphores = rest[0], rest[1:-1], rest[-1]
        copies = []
        for n, source in enumerate(sources):
            to = target.at[n] if n < count else kept_here[n - count]
            copies.append(pltpu.make_async_copy(source, to, semaphores.at[n]))
        for copy in copies:
            copy.start()
        for copy in copies:
            copy.wait()

    args = (*arrays, *kept)
    every = tuple(range(len(args)))
    outs = [struct((count,) + arrays[0].shape, BF16)] + [struct(k.shape, BF16) for k in kept]
    return run_whole(
        kernel, outs, args, 0, [pltpu.SemaphoreType.DMA((len(args),))],
        vmem=20, after=after, raw=every, far_in=every, **sides,
    )


def column_tiles(width, tile=512):
    return [(slice(None), slice(start, start + tile)) for start in range(0, width, tile)]


def feed_kernel(near, far, weights, scales, kept_out, hid_out, give, own, sent, rows):
    kept, hid = kept_out.buffer, hid_out.buffer
    part, depth = near.shape
    tile = 512
    width = hid.shape[1]
    rows[:part] = near[...]
    rows[part:] = far[...]
    for i in range(2):
        for n, start in enumerate(range(0, width, tile)):
            span = slice(start, start + tile)
            up = dot(rows[...], weights[3 * i, :, span])
            gate = dot(rows[...], weights[3 * i + 1, :, span])
            kept[i, :, span] = up.astype(BF16)
            kept[2 + i, :, span] = gate.astype(BF16)
            kept_out.send(2 * i + n, 4 + 2 * i + n)
            _, active = silu_parts(scales[2 * i + 1 : 2 * i + 2, span] * gate)
            hidden = (scales[2 * i : 2 * i + 1, span] * up * active).astype(BF16)
            if i == 0:
                hid[:, span] = hidden
                hid_out.send(n)
            else:
                give[:, span] = hidden
    total = dot(hid[...], weights[2]) + dot(give[...], weights[5])
    own[...] = total[:part]
    sent[...] = total[part:].astype(BF16)


def feed(near, far, weights, scales, after, **sides):
    part, depth = near.shape
    rows = 2 * part
    width = weights.shape[2]
    outs = [
        struct((4, rows, width), BF16), struct((rows, width), BF16),
        struct((rows, width), BF16), struct((part, depth), F32), struct((part, depth), BF16),
    ]
    tiles = column_tiles(width)
    return run_whole(
        feed_kernel, outs, (near, far, weights, scales), 12 * rows * depth * width,
        scratch=[pltpu.VMEM((rows, depth), BF16)], vmem=FEED_VMEM, after=after,
        store={0: [(i, *tile) for i in range(4) for tile in tiles], 1: tiles}, **sides,
    )


def feed_back_kernel(near, far, weights, scales, kept, d_up_out, d_gate_out, sums_out, give, own, sent, rows):
    d_up_all, d_gate_all = d_up_out.buffer, d_gate_out.buffer
    part, depth = near.shape
    tile = 512
    width = d_up_all.shape[1]
    rows[:part] = near[...]
    rows[part:] = far[...]
    for i in range(2):
        for n, start in enumerate(range(0, width, tile)):
            span = slice(start, start + tile)
            at = slice(i * width + start, i * width + start + tile)
            d_hidden = dot_nt(rows[...], weights[3 * i + 2, span])
            up_scale = scales[2 * i : 2 * i + 1, span]
            gate_scale = scales[2 * i + 1 : 2 * i + 2, span]
            up = kept[i, :, span].astype(F32)
            gate = kept[2 + i, :, span].astype(F32)
            scaled = gate_scale * gate
            sig, active = silu_parts(scaled)
            d_up_scaled = d_hidden * active
            d_gate_scaled = d_hidden * (up_scale * up) * (sig + active * (1.0 - sig))
            d_up = (d_up_scaled * up_scale).astype(BF16)
            d_gate = (d_gate_scaled * gate_scale).astype(BF16)
            sums_out[0:1, at] = jnp.sum(d_up_scaled * up, axis=0, keepdims=True)
            sums_out[1:2, at] = jnp.sum(d_gate_scaled * gate, axis=0, keepdims=True)
            if i == 0:
                d_up_all[:, span] = d_up
                d_gate_all[:, span] = d_gate
                d_up_out.send(n)
                d_gate_out.send(n)
            else:
                give[0, :, span] = d_up
                give[1, :, span] = d_gate
    total = dot_nt(d_up_all[...], weights[0]) + dot_nt(d_gate_all[...], weights[1])
    total += dot_nt(give[0], weights[3]) + dot_nt(give[1], weights[4])
    own[...] = total[:part]
    sent[...] = total[part:].astype(BF16)


def feed_back(near, far, weights, scales, kept, after, **sides):
    part, depth = near.shape
    rows = 2 * part
    width = weights.shape[2]
    outs = [
        struct((rows, width), BF16), struct((rows, width), BF16), struct((2, 2 * width), F32),
        struct((2, rows, depth), BF16), struct((part, depth), F32), struct((part, depth), BF16),
    ]
    tiles = column_tiles(width)
    return run_whole(
        feed_back_kernel, outs, (near, far, weights, scales, kept), 12 * rows * depth * width,
        scratch=[pltpu.VMEM((rows, depth), BF16)], vmem=FEED_VMEM, after=after, store={0: tiles, 1: tiles}, **sides,
    )


def view(ref, place):
    return ref.at[place] if place else ref


def piece_place(piece, bits):
    flags = [piece // bit % 2 for bit in bits]
    return flags[0], flags[1] + 2 * flags[2]


def weight_kernel(groups, orders, vectors, me, *refs):
    n_in = sum(len(left) + len(right) for left, right in groups) + vectors
    inputs = list(refs[:n_in])
    results = refs[n_in : n_in + 2 * len(orders)]
    targets = [r.buffer if isinstance(r, Stored) else r for r in results]
    turned = refs[-1]
    piece = 128
    count, half = turned.shape[0] // piece, turned.shape[0] // 2
    mine = me[0, 0]
    pieces = sorted(range(count), key=lambda j: (1 - piece_place(j, orders[0][0])[0], piece_place(j, orders[0][0])[1]))
    if vectors:
        lines = [inputs.pop(0) for _ in range(vectors)]
        for j in pieces:
            sent, position = piece_place(j, orders[0][0])
            target = targets[1 - sent]
            rows, width = target.shape[1] - piece, target.shape[2]
            owner = jnp.bitwise_xor(mine, j)
            row = iota((rows, width), 0)
            block = jnp.zeros((rows, width), F32)
            for n, line in enumerate(lines):
                values = line[pl.ds(owner, 1), :]
                if values.shape[1] < width:
                    values = jnp.concatenate([values, jnp.zeros((1, width - values.shape[1]), F32)], axis=1)
                block = jnp.where(row == n, values, block)
            target[position, piece:] = block.astype(BF16)
    base = 0
    for left_places, right_places in groups:
        left = [(inputs.pop(0), place) for place in left_places]
        right = [(inputs.pop(0), place) for place in right_places]
        start = 0
        for source, place in left:
            ref = view(source.get(), place)
            for n, j in enumerate(pieces):
                at = jnp.bitwise_xor(mine, j) * piece
                columns = ref[:, pl.ds(pl.multiple_of(at, piece), piece)]
                turned[n * piece : (n + 1) * piece, start : start + ref.shape[0]] = columns.T
            start += ref.shape[0]
        for side in range(2):
            start = 0
            product = None
            for source, place in right:
                ref = view(source.get(), place)
                rows = ref.shape[0]
                part = dot(turned[side * half : (side + 1) * half, start : start + rows], ref[...])
                product = part if product is None else product + part
                start += rows
            product = product.astype(BF16)
            width = product.shape[1]
            begin = 0
            for n, (bits, columns) in enumerate(orders):
                first, last = max(base, begin), min(base + width, begin + columns)
                if first < last:
                    for i, j in enumerate(pieces[side * count // 2 : (side + 1) * count // 2]):
                        sent, position = piece_place(j, bits)
                        targets[2 * n + 1 - sent][position, :piece, first - begin : last - begin] = product[
                            i * piece : (i + 1) * piece, first - base : last - base
                        ]
                begin += columns
            if side == 1 and len(orders) == 1 and len(groups) == 1 and isinstance(results[1], Stored):
                results[1].send()
            if side == 0 and len(orders) == 1 and len(groups) == 1 and isinstance(results[0], Stored):
                results[0].send()
        base += width


def weight_halves(me, groups, n_groups, orders, after=(), far_after=(), vectors=(), far_kept=True, far_sent=False, **sides):
    depth = shape_at(groups[0][0][0])[1]
    rows = sum(shape_at(entry)[0] for entry in groups[0][0])
    piece = depth // n_groups
    outs = [
        struct((n_groups // 2, piece + (VECTOR_ROWS if vectors and n == 0 else 0), columns), BF16)
        for n, (_, columns) in enumerate(orders) for _ in range(2)
    ]
    entries = [entry for left, right in groups for entry in (*left, *right)]
    args = (me, *vectors, *[a for a, _, _ in entries])
    places = [([p for _, p, _ in left], [p for _, p, _ in right]) for left, right in groups]
    total = sum(columns for _, columns in orders)
    skip = 1 + len(vectors)
    results = run_whole(
        functools.partial(weight_kernel, places, orders, len(vectors)), outs, args, 2 * rows * depth * total,
        [pltpu.VMEM((depth, rows), BF16)], vmem=40, smem=1, after=after,
        fetch={skip + i: [p] if p else None for i, (_, p, _) in enumerate(entries)},
        far_in=tuple(skip + i for i, (_, _, far) in enumerate(entries) if far), far_after=far_after,
        store={i: None for i in range(len(outs)) if (far_kept if i % 2 else far_sent)}, **sides,
    )
    return [*[results[2 * n : 2 * n + 2] for n in range(len(orders))], *results[len(outs) :]]


def merge_kernel(kept, got, *outs):
    for i in range(kept.shape[0] // 2):
        outs[0][i] = (kept[2 * i + 1].astype(F32) + got[2 * i + 1].astype(F32)).astype(BF16)
        outs[1][i] = (kept[2 * i].astype(F32) + got[2 * i].astype(F32)).astype(BF16)


def merge(kept, got, after=()):
    count, rows, columns = kept.shape
    outs = [struct((count // 2, rows, columns), BF16)] * 2
    return run_whole(merge_kernel, outs, (kept, got), kept.size, vmem=16, after=after)


def finish(kept, got, parts, after=()):
    def kernel(kept_ref, got_ref, *outs):
        total = kept_ref[0].astype(F32) + got_ref[0].astype(F32)
        for (row, rows, column, columns, turned), out in zip(parts, outs):
            piece = total[row : row + rows, column : column + columns]
            out[...] = piece.T if turned else piece

    outs = [struct((c, r) if turned else (r, c), F32) for _, r, _, c, turned in parts]
    return run_whole(kernel, outs, (kept, got), kept.size, vmem=16, after=after)


def block_of(entry):
    array, place, _ = entry
    return array[place] if place else array


def weight_halves_plain(me, groups, n_groups, orders, after=(), far_after=(), vectors=(), far_kept=True, far_sent=False, load=(), save=(), carry=(), pile=()
):
    products = [
        dot_tn(jnp.concatenate([block_of(e) for e in left], axis=0), jnp.concatenate([block_of(e) for e in right], axis=0))
        for left, right in groups
    ]
    product = jnp.concatenate(products, axis=1)
    parts = product.reshape(n_groups, product.shape[0] // n_groups, product.shape[1])
    order = jnp.bitwise_xor(me[0, 0], jnp.arange(n_groups, dtype=jnp.int32))
    parts = parts[order]
    results, start = [], 0
    for n, (_, columns) in enumerate(orders):
        chosen = parts[:, :, start : start + columns]
        if vectors and n == 0:
            lines = [jnp.pad(v[order], ((0, 0), (0, columns - v.shape[1])))[:, None] for v in vectors]
            chosen = jnp.concatenate([chosen, *lines], axis=1)
            chosen = jnp.pad(chosen, ((0, 0), (0, VECTOR_ROWS - len(lines)), (0, 0)))
        chosen = chosen.reshape((n_groups // 2, 2) + chosen.shape[1:]).astype(BF16)
        results.append((chosen[:, 1], chosen[:, 0]))
        start += columns
    loaded = [array[place] if place else array for array, place in load]
    return [*results, *loaded, *save, *carry, *([jnp.concatenate(pile)] if pile else [])]


def add(pair, after=()):
    kept, got = pair
    if kept.shape[1] >= 128:
        return merge(kept, got, after)
    total = kept.astype(F32) + got.astype(F32)
    parts = total.reshape((kept.shape[0] // 2, 2) + kept.shape[1:]).astype(BF16)
    return parts[:, 1], parts[:, 0]


def stage(pair, bit, after=()):
    sent, kept = add(pair, after)
    return kept, swap(sent, "dp", bit)


def combine_kernel(*refs):
    pairs, (sent, kept) = refs[:-2], refs[-2:]
    start = 0
    for a, b in zip(pairs[::2], pairs[1::2]):
        rows, columns = a.shape[1:]
        span = slice(start, start + columns)
        for piece, target in ((1, sent), (0, kept)):
            target[0, :rows, span] = (a[piece].astype(F32) + b[piece].astype(F32)).astype(BF16)
            if rows < target.shape[1]:
                target[0, rows:, span] = jnp.zeros((target.shape[1] - rows, columns), BF16)
        start += columns


def combine(pairs, after=()):
    count = pairs[0][0].shape[0]
    rows = max(kept.shape[1] for kept, _ in pairs)
    if count == 2 and rows >= 128:
        out = struct((1, rows, sum(kept.shape[2] for kept, _ in pairs)), BF16)
        return run_whole(combine_kernel, [out, out], [x for pair in pairs for x in pair], 0, vmem=16, after=after)
    totals = [kept.astype(F32) + got.astype(F32) for kept, got in pairs]
    total = jnp.concatenate([jnp.pad(t, ((0, 0), (0, rows - t.shape[1]), (0, 0))) for t in totals], axis=2)
    parts = total.reshape((count // 2, 2) + total.shape[1:]).astype(BF16)
    return parts[:, 1], parts[:, 0]


def last_stage(pair, bits, parts, after=()):
    for bit in bits:
        pair = stage(pair, bit)
    kept, got = pair
    if kept.shape[1] >= 128:
        return finish(kept, got, parts, after)
    total = (kept.astype(F32) + got.astype(F32))[0]
    pieces = [total[r : r + rows, c : c + columns] for r, rows, c, columns, _ in parts]
    return [piece.T if part[-1] else piece for piece, part in zip(pieces, parts)]


def shards(
    tokens,
    seq_lengths,
    w_query,
    w_key,
    w_value,
    w_out,
    qk_scale,
    attn_rate,
    w_up,
    w_gate,
    up_scale,
    gate_scale,
    w_down,
    mlp_rate,
    out_grad,
):
    local_rows, depth = tokens.shape
    n_mp = lax.axis_size("mp")
    n_dp = lax.axis_size("dp")
    assert n_mp == 4
    width = w_query.shape[1]
    hidden_width = w_up.shape[1]
    heads = width // HD
    part = local_rows // PARTS
    me = lax.axis_index("mp").astype(jnp.int32)
    me_ref = me.reshape(1, 1)
    group = lax.axis_index("dp").astype(jnp.int32)
    group_ref = group.reshape(1, 1)
    dp_bits = bits_of("dp")
    seq_count = seq_lengths.shape[1]

    far_tokens = swap(tokens, "mp", 2)
    core_tokens = swap(tokens, "mp", 1)
    ends = jnp.cumsum(seq_lengths[0])
    starts = jnp.concatenate([jnp.zeros((1,), jnp.int32), ends])
    owner = jnp.bitwise_xor(me, jnp.arange(n_mp, dtype=jnp.int32))
    row_ids = owner[:, None] * local_rows + jnp.arange(local_rows, dtype=jnp.int32)[None]
    segment = jnp.sum((row_ids[:, :, None] >= ends).astype(jnp.int32), axis=2)
    first = jnp.sum(
        jnp.where(segment[:, :, None] == jnp.arange(seq_count + 1, dtype=jnp.int32), starts, 0), axis=2
    )
    position = (row_ids - first).astype(F32)
    frequency = jnp.exp(jnp.arange(HALF, dtype=F32) * (-2.0 * math.log(10000.0) / HD))
    angles = position[:, :, None] * jnp.tile(frequency, heads)[None, None]
    cos, sin = jnp.cos(angles), jnp.sin(angles)
    seg_q = jnp.where(segment < seq_count, segment, -1).astype(F32)[:, None, :]
    seg_k = jnp.where(segment < seq_count, segment, -2).astype(F32)[:, None, :]
    gain = qk_scale.reshape(heads, 2, HALF).transpose(1, 0, 2).reshape(1, width)

    scale_rows = jnp.stack([up_scale, gate_scale * math.sqrt(depth)])
    core_out = swap(w_out, "mp", 1)
    core_rows = swap(scale_rows, "mp", 1)
    core_up = swap(w_up, "mp", 1)
    core_gate = swap(w_gate, "mp", 1)
    core_down = swap(w_down, "mp", 1)
    scales = jnp.concatenate([scale_rows, core_rows], axis=0)

    weights = (w_query, w_key, w_value)
    early = project(0, tokens, core_tokens, *weights, gain, cos, sin, save=[core_tokens])
    far_tokens, _ = hold([far_tokens], (early[0], seg_q, seg_k))
    cross_tokens = swap(far_tokens, "mp", 1)
    late = project(
        2, far_tokens, cross_tokens, *early[7:10], gain, cos, sin, save=[far_tokens, cross_tokens]
    )
    core_tokens, far_tokens, cross_tokens = early[10], late[10], late[11]
    qi, ki, cos_far, sin_far, q_far, k_far, v_far = zip(early[:7], late[:7])
    q, k, v = zip(early[4:7], late[7:10])
    head_out, inv, give, out_here = attend(
        me_ref, q, k, v, seg_q, seg_k, (core_up, core_gate, core_down, core_out, core_rows), load=[(w_out, ())]
    )
    attn_own, attn_far = out_project(head_out, swap(give, "mp", 1), out_here, core_out)
    feed_parts = [w_up, w_gate, w_down, core_up, core_gate, core_down]
    feed_weights, tokens_here = load_weights(feed_parts, (), (attn_own,), load=[(tokens, ())])
    attn_far = swap(attn_far, "mp", 2)

    attn_row = attn_rate.reshape(1, depth)
    mlp_row = mlp_rate.reshape(1, depth)
    full, lowered, vector = struct((part, depth), F32), struct((part, depth), BF16), struct((1, depth), F32)
    both = struct((2 * part, depth), BF16)

    def part_of(c):
        return (slice(c * part, (c + 1) * part),)

    def mix_attn(c, after, *before):
        outs = [lowered, both, both] if c else [lowered, lowered, struct((8, 128), BF16)]
        return run_whole(
            functools.partial(mix_attn_kernel, c), outs, (attn_own, attn_far, tokens_here, attn_row, *before),
            20 * part * depth, vmem=16, after=after,
        )

    def mix_mlp(c, own, far, h_one, cotangent, after, *before):
        return run_whole(
            functools.partial(mix_mlp_kernel, c),
            [full, lowered, lowered, vector, both if c else struct((8, 128), BF16)],
            (own, far, h_one, mlp_row, cotangent, *before), 30 * part * depth, vmem=16, after=after,
            store={} if c else {0: None, 2: None},
        )

    def mix_back(own, far, d_mix, attn_sum, h_one, rows, after):
        return run_whole(
            mix_back_kernel, [lowered, full, vector],
            (own, far, d_mix, attn_sum, h_one, rows, attn_row, mlp_row), 40 * part * depth, vmem=16, after=after,
        )

    fast = depth // n_dp == 128 and len(dp_bits) == 3
    later_bits = [dp_bits[1], dp_bits[0], dp_bits[2]] if fast else dp_bits

    def weight_grad(groups, orders, after=(), far_after=(), vectors=(), **sides):
        run = weight_halves if fast else weight_halves_plain
        return run(group_ref, groups, n_dp, orders, after, far_after, vectors, **sides)

    def whole(array, far=False):
        return (array, (), far)

    def layer(array, i, far=False):
        return (array, (i,), far)

    def rows_of(array, c, far=False):
        return (array, (slice(c * part, (c + 1) * part),), far)

    def over_dp(array, bit):
        return swap(array, "dp", bit)

    def cross(array):
        return swap(array, "mp", 2)

    def core(array):
        return swap(array, "mp", 1)

    near_a, sum_a, _ = mix_attn(0, (feed_weights,))
    far_a = cross(near_a)
    near_b, sums, near_rows = mix_attn(1, (near_a,), sum_a, near_a)

    near_b, token = hold([near_b], (far_a,))
    far_b = cross(near_b)
    core_near = core(near_rows)
    core_far_a = core(far_a)
    kept_a, hid_a, give_a, own_a, sent, sums, near_rows = feed(
        near_a, far_a, feed_weights, scales, (token,), save=[sums, near_rows]
    )
    core_hid_a = core(give_a)

    sent, token = hold([sent], (far_b,))
    got = cross(sent)
    core_far_b = core(far_b)
    kept_b, hid_b, give_b, own_b, sent, cotangent = feed(
        near_b, far_b, feed_weights, scales, (token,), load=[(out_grad, part_of(0))]
    )
    core_hid_b = core(give_b)

    sent, token = hold([sent], (got, core_near, core_far_a, core_far_b))
    got_b = cross(sent)
    out_a, d_near_a, d_mix_a, rate_a, _ = mix_mlp(0, own_a, got, near_a, cotangent, (token,))
    d_far_a = cross(d_near_a)
    back_weights, kept_a, kept_b, cotangent, own_b = load_weights(
        feed_parts, (kept_a, kept_b), (d_near_a,),
        load=[(out_grad, part_of(1))], carry=[own_b],
    )

    out_b, d_near_b, d_mix_b, rate_b, d_near_rows = mix_mlp(
        1, own_b, got_b, near_b, cotangent, (d_far_a, core_hid_a), d_near_a
    )
    d_far_b = cross(d_near_b)
    core_d_near = core(d_near_rows)
    core_d_far_a = core(d_far_a)
    d_up_a, d_gate_a, sums_a, give_a, own_a, sent, d_mix_b, d_near_rows, block_out = feed_back(
        d_near_a, d_far_a, back_weights, scales, kept_a, (d_near_b,),
        save=[d_mix_b, d_near_rows], pile=[out_a, out_b],
    )

    sent, give_a, token = hold([sent, give_a], (d_far_b, core_hid_b))
    got_a = cross(sent)
    core_give_a = core(give_a)
    core_d_far_b = core(d_far_b)
    d_up_b, d_gate_b, sums_b, give_b, own_b, sent = feed_back(
        d_near_b, d_far_b, back_weights, scales, kept_b, (token,)
    )
    down_a, down_b, d_mix_a, sum_a, rows_a, h_one_a, own_a = weight_grad(
        [(
            [rows_of(d_near_rows, 0, True), whole(d_far_a), rows_of(d_near_rows, 1, True), whole(d_far_b),
             rows_of(core_d_near, 0), whole(core_d_far_a, True), rows_of(core_d_near, 1), whole(core_d_far_b, True)],
            [whole(hid_a, True), whole(hid_b, True), whole(core_hid_a), whole(core_hid_b)],
        )],
        [(dp_bits, hidden_width // 2), (later_bits, hidden_width // 2)], (sums_b,), far_kept=False,
        load=[(d_mix_a, ()), (sums, part_of(0)), (tokens, part_of(0)), (near_rows, part_of(0))], carry=[own_a],
    )

    sent, give_b, sent_a, sent_b, token = hold([sent, give_b, down_a[0], down_b[0]], (got_a,))
    got_b = cross(sent)
    core_give_b = core(give_b)
    down_a = (down_a[1], over_dp(sent_a, dp_bits[0]))
    down_b = (down_b[1], over_dp(sent_b, later_bits[0]))
    a_near_a, rest_a, attn_rate_a = mix_back(own_a, got_a, d_mix_a, sum_a, h_one_a, rows_a, (token,))
    a_far_a = cross(a_near_a)
    rows_in = [
        rows_of(near_rows, 0, True), whole(far_a), rows_of(near_rows, 1, True), whole(far_b),
        rows_of(core_near, 0, True), whole(core_far_a, True), rows_of(core_near, 1, True), whole(core_far_b, True),
    ]
    grad_up, d_mix_b, sum_b, rows_b, h_one_b, out_here, rest_a, own_b = weight_grad(
        [(rows_in, [whole(d_up_a, True), whole(d_up_b, True), layer(core_give_a, 0), layer(core_give_b, 0)])],
        [(dp_bits, hidden_width)], (a_near_a,), far_sent=True,
        load=[(d_mix_b, ()), (sums, part_of(1)), (tokens, part_of(1)), (near_rows, part_of(1)), (w_out, ())],
        save=[rest_a], carry=[own_b],
    )

    sent_a, kept_a = add(down_a, (grad_up[0],))
    sent_b, kept_b = add(down_b, (sent_a,))
    sent_a, sent_b, token = hold([sent_a, sent_b], (got_b, a_far_a))
    down_a = (kept_a, over_dp(sent_a, dp_bits[1]))
    down_b = (kept_b, over_dp(sent_b, later_bits[1]))
    a_near_b, rest_b, attn_rate_b = mix_back(own_b, got_b, d_mix_b, sum_b, h_one_b, rows_b, (token,))
    a_far_b = cross(a_near_b)

    def pack_kernel(part_a, part_b, rate_a, rate_b, rate_c, rate_d, own_ref, core_ref):
        total = part_a[...] + part_b[...]
        own_ref[0:2] = total[:, :hidden_width]
        own_ref[2:3] = rate_a[...] + rate_b[...]
        own_ref[3:4] = rate_c[...] + rate_d[...]
        core_ref[0:2] = total[:, hidden_width:]
        core_ref[2:4] = own_ref[2:4]

    def pair_kernel(own_ref, got_ref, sum_ref, rate_ref):
        sum_ref[...] = own_ref[...] + got_ref[...]
        rate_ref[...] = own_ref[2:4] + got_ref[2:4]

    size = depth // n_dp

    def table_kernel(sum_ref, got_ref, scale_ref, rate_ref):
        rates = sum_ref[2:4] + got_ref[...]
        for target, lines in (
            (scale_ref, [sum_ref[0:1], sum_ref[1:2] * math.sqrt(depth)]),
            (rate_ref, [rates[0:1], rates[1:2]]),
        ):
            for n, line in enumerate(lines):
                for p in range(n_dp):
                    target[p : p + 1, n * size : (n + 1) * size] = line[:, p * size : (p + 1) * size]

    four = struct((4, depth), F32)
    assert hidden_width == depth
    own_sums, core_sums = run_whole(
        pack_kernel, [four, four], (sums_a, sums_b, attn_rate_a, attn_rate_b, rate_a, rate_b), 0, vmem=8
    )
    core_sums = core(core_sums)
    head_a = head_back(a_near_a, a_far_a, out_here, core_out, (a_near_b, own_sums))
    pair_sums, rates = run_whole(
        pair_kernel, [four, struct((2, depth), F32)], (own_sums, core_sums), 0, vmem=8, after=(head_a[0],)
    )
    rates = cross(rates)
    grad_gate, up_sent, rests = weight_grad(
        [(rows_in, [whole(d_gate_a, True), whole(d_gate_b, True), layer(core_give_a, 1), layer(core_give_b, 1)])],
        [(later_bits, hidden_width)], (pair_sums,), pile=[rest_a, rest_b], load=[(grad_up[0], ())],
    )

    if fast:
        lines = run_whole(
            table_kernel, [struct((n_dp, 2 * size), F32)] * 2, (pair_sums, rates), 0, vmem=8, after=(grad_gate[0],)
        )
    else:
        rates = pair_sums[2:4] + rates
        pairs = [(pair_sums[0], pair_sums[1] * math.sqrt(depth)), (rates[0], rates[1])]
        lines = [jnp.concatenate([x.reshape(n_dp, -1) for x in pair], axis=1) for pair in pairs]
    down_sent, down_kept = combine([down_a, down_b], (lines[0],))
    down_sent, up_sent, gate_sent, head_give, token = hold(
        [down_sent, up_sent, grad_gate[0], head_a[1]], (a_far_b,)
    )
    down = (down_kept, over_dp(down_sent, dp_bits[2]))
    up_got = over_dp(up_sent, dp_bits[0])
    gate_got = over_dp(gate_sent, later_bits[0])
    core_head_a = core(head_give)
    head_b = head_back(a_near_b, a_far_b, out_here, core_out, (token,))
    core_head_b = core(head_b[1])
    joined, qk_rows, up_kept, gate_kept = attend_back(
        me_ref, [head_a[0], head_b[0]], [core_head_a, core_head_b], q_far, k_far, v_far, head_out, inv, qi, ki,
        seg_k, seg_q, gain, cos_far, sin_far, load=[(grad_up[1], ()), (grad_gate[1], ())],
    )

    def attn_rows(array, half):
        return (array, (slice(half * part, (half + 1) * part), slice(0, depth)), False)

    if not fast:
        qk_rows = qk_rows[:, :HALF].reshape(n_dp, -1)
    give_far, far, give, own = input_grad(joined, *weights, (qk_rows,), ())
    up_sent, up_kept = add((up_kept, up_got), (own,))
    gate_sent, gate_kept = add((gate_kept, gate_got), (up_sent,))
    up_sent, gate_sent, give_far, token = hold([up_sent, gate_sent, give_far], ())
    grad_up = (up_kept, over_dp(up_sent, dp_bits[1]))
    grad_gate = (gate_kept, over_dp(gate_sent, later_bits[1]))
    far_got = core(give_far)
    token_rows = [whole(tokens, True), whole(core_tokens, True), whole(far_tokens, True), whole(cross_tokens, True)]
    first, second, own, give = weight_grad(
        [
            (
                [attn_rows(x, half) for pair in ((head_give, head_b[1]), (core_head_a, core_head_b))
                 for half in range(2) for x in pair],
                [layer(head_out, slot) for slot in (0, 2, 1, 3)],
            ),
            (token_rows, [layer(joined, slot) for slot in range(4)]),
        ],
        [(dp_bits, 2 * width + width // 2), (later_bits, 2 * width - width // 2)], vectors=(*lines, qk_rows), far_kept=False, after=(token,),
        carry=[own, give],
    )

    rest_bits = dp_bits[3:]
    feed_sent, feed_kept = combine([grad_up, grad_gate], (first[0],))
    (down,) = last_stage(down, rest_bits, [(0, size, 0, hidden_width, True)], (feed_sent,))
    far_sum = add_far(far, far_got, (down,))
    feed_sent, first_sent, second_sent, far_sum, token = hold([feed_sent, first[0], second[0], far_sum], ())
    feeds = (feed_kept, over_dp(feed_sent, dp_bits[2]))
    first = (first[1], over_dp(first_sent, dp_bits[0]))
    second = (second[1], over_dp(second_sent, later_bits[0]))
    far_grad = cross(far_sum)
    first_sent, first_kept = add(first, (token,))
    second_sent, second_kept = add(second, (first_sent,))
    first_sent, second_sent, give, token = hold([first_sent, second_sent, give], ())
    first = (first_kept, over_dp(first_sent, dp_bits[1]))
    second = (second_kept, over_dp(second_sent, later_bits[1]))
    got = core(give)

    attn_sent, attn_kept = combine([first, second], (token,))
    attn = (attn_kept, over_dp(attn_sent, dp_bits[2]))
    late = (attn_kept,)
    grad_up, grad_gate = last_stage(
        feeds, rest_bits,
        [(0, size, 0, hidden_width, False), (0, size, hidden_width, hidden_width, False)], late,
    )
    short = width // n_dp
    grad_out, grad_query, grad_key, grad_value, scale_up, scale_gate, rate_attn, rate_mlp, scale_qk = last_stage(
        attn, rest_bits,
        [
            (0, size, 0, width, True), (0, size, width, width, False),
            (0, size, 2 * width, width, False), (0, size, 3 * width, width, False),
            (size, 1, 0, size, False), (size, 1, size, size, False),
            (size + 1, 1, 0, size, False), (size + 1, 1, size, size, False), (size + 2, 1, 0, short, False),
        ],
        late,
    )
    token_grad = rests + (own + got.astype(F32) + far_grad.astype(F32))
    return (
        block_out,
        token_grad,
        grad_query,
        grad_key,
        grad_value,
        grad_out,
        scale_qk[0],
        rate_attn[0],
        grad_up,
        grad_gate,
        scale_up[0],
        scale_gate[0],
        down,
        rate_mlp[0],
    )


def solution(mesh):
    in_specs = (
        P(("dp", "mp"), None),
        P("dp", None),
        P(None, "mp"),
        P(None, "mp"),
        P(None, "mp"),
        P("mp", None),
        P("mp"),
        P(),
        P(None, "mp"),
        P(None, "mp"),
        P("mp"),
        P("mp"),
        P("mp", None),
        P(),
        P(("dp", "mp"), None),
    )
    out_specs = (
        P(("dp", "mp"), None),
        P(("dp", "mp"), None),
        P("dp", "mp"),
        P("dp", "mp"),
        P("dp", "mp"),
        P("mp", "dp"),
        P(("mp", "dp")),
        P("dp"),
        P("dp", "mp"),
        P("dp", "mp"),
        P(("mp", "dp")),
        P(("mp", "dp")),
        P("mp", "dp"),
        P("dp"),
    )
    return jax.shard_map(shards, mesh=mesh, in_specs=in_specs, out_specs=out_specs, check_vma=False)
```

```python
import functools
import math

import jax
import jax.numpy as jnp
from jax import lax
from jax.experimental import pallas as pl
from jax.experimental.pallas import tpu as pltpu
from jax.sharding import PartitionSpec as P

HD = 64
HALF = HD // 2
EPS = 1e-06
F32 = jnp.float32
BF16 = jnp.bfloat16
SCORE_ROOT = math.sqrt(HD)
EXP_SCALE = SCORE_ROOT * math.log2(math.e)
MIB = 1 << 20
PARTS = 2
LATER = 5e8
FEED_VMEM = 24
VECTOR_ROWS = 16


def dot(left, right):
    return lax.dot_general(left, right, (((1,), (0,)), ((), ())), preferred_element_type=F32)


def dot_nt(left, right):
    return lax.dot_general(left, right, (((1,), (1,)), ((), ())), preferred_element_type=F32)


def dot_tn(left, right):
    return lax.dot_general(left, right, (((0,), (0,)), ((), ())), preferred_element_type=F32)


def iota(shape, dim):
    return lax.broadcasted_iota(jnp.int32, shape, dim)


def struct(shape, dtype):
    return jax.ShapeDtypeStruct(shape, dtype)


def in_vmem():
    return pl.BlockSpec(memory_space=pltpu.VMEM)


def in_smem():
    return pl.BlockSpec(memory_space=pltpu.SMEM)


def cost(flops, args, outs, transcendentals=0):
    moved = sum(a.size * a.dtype.itemsize for a in args)
    moved += sum(math.prod(o.shape) * jnp.dtype(o.dtype).itemsize for o in outs)
    return pl.CostEstimate(flops=int(2 * flops), bytes_accessed=int(2 * moved), transcendentals=int(transcendentals))


class Fetched:
    def __init__(self, copies, buffer):
        self.copies = copies
        self.buffer = buffer
        self.shape = buffer.shape
        self.waited = set()

    def start(self):
        for copy in self.copies:
            copy.start()

    def get(self, *parts):
        for n in parts or range(len(self.copies)):
            if n not in self.waited:
                self.copies[n].wait()
                self.waited.add(n)
        return self.buffer


class Stored:
    def __init__(self, copies, buffer):
        self.copies = copies
        self.buffer = buffer
        self.shape = buffer.shape
        self.sent = set()

    def send(self, *parts):
        for n in parts or range(len(self.copies)):
            if n not in self.sent:
                self.copies[n].start()
                self.sent.add(n)


def run_whole(
    body, outs, args, flops, scratch=(), vmem=32, smem=0, transcendentals=0, after=(), fetch=None, store=None,
    far_in=(), far_out=(), far_after=(), raw=(), load=(), save=(), carry=(), pile=()
):
    fetch, store = fetch or {}, store or {}
    after = (*after, *[pltpu.with_memory_space_constraint(a, pltpu.HBM) for a in far_after])
    count, extra, n_out = len(args), len(after), len(outs)
    fetch = {i: [()] if places is None else places for i, places in fetch.items()}
    store = {i: [()] if places is None else places for i, places in store.items()}
    n_copies = sum(len(places) for places in (*fetch.values(), *store.values()))
    n_copies += len(load) + len(save) + len(pile)
    sides = len(load) + len(save) + len(carry)

    def kernel(*refs):
        ins, refs = list(refs[:count]), refs[count + extra :]
        side_in, refs = refs[:sides], refs[sides:]
        heap, refs = refs[: len(pile)], refs[len(pile) :]
        results, refs = list(refs[:n_out]), refs[n_out:]
        side_out, rest = refs[:sides], refs[sides:]
        if pile:
            heap_out, rest = rest[0], rest[1:]
        own, rest = rest[: len(scratch)], list(rest[len(scratch) :])
        semaphores = rest.pop() if n_copies else None
        used = 0
        for i, places in fetch.items():
            buffer = rest.pop(0)
            copies = []
            for place in places:
                source, target = (ins[i].at[place], buffer.at[place]) if place else (ins[i], buffer)
                copies.append(pltpu.make_async_copy(source, target, semaphores.at[used]))
                used += 1
            ins[i] = Fetched(copies, buffer)
            ins[i].start()
        for i, places in store.items():
            buffer = rest.pop(0)
            copies = []
            for place in places:
                source, target = (buffer.at[place], results[i].at[place]) if place else (buffer, results[i])
                copies.append(pltpu.make_async_copy(source, target, semaphores.at[used]))
                used += 1
            results[i] = Stored(copies, buffer)
        moves = []
        for n in range(len(load) + len(save)):
            source = side_in[n]
            if n < len(load) and load[n][1]:
                source = source.at[load[n][1]]
            moves.append(pltpu.make_async_copy(source, side_out[n], semaphores.at[used]))
            used += 1
        start = 0
        for ref in heap:
            target = heap_out.at[start : start + ref.shape[0]]
            moves.append(pltpu.make_async_copy(ref, target, semaphores.at[used]))
            start += ref.shape[0]
            used += 1
        for move in moves:
            move.start()
        for n in range(len(load) + len(save), sides):
            side_out[n][...] = side_in[n][...]
        body(*ins, *results, *own)
        for i in fetch:
            ins[i].get()
        for i in store:
            results[i].send()
        for i in store:
            for copy in results[i].copies:
                copy.wait()
        for move in moves:
            move.wait()

    def in_hbm(array):
        return pltpu.with_memory_space_constraint(array, pltpu.HBM)

    estimate = cost(flops, args, outs, transcendentals)
    buffers = [pltpu.VMEM(args[i].shape, args[i].dtype) for i in fetch]
    buffers += [pltpu.VMEM(outs[i].shape, outs[i].dtype) for i in store]
    if n_copies:
        buffers.append(pltpu.SemaphoreType.DMA((n_copies,)))
    args = [in_hbm(a) if i in far_in else a for i, a in enumerate(args)]
    outs = [pltpu.HBM(o.shape, o.dtype) if i in store or i in far_out else o for i, o in enumerate(outs)]
    anywhere = pl.BlockSpec(memory_space=pl.ANY)
    specs = [
        in_smem() if i < smem else anywhere if i in fetch or i in raw else in_vmem() for i in range(count)
    ]
    side_args = [in_hbm(a) for a, _ in load] + [*save, *carry]
    side_outs = [struct(shape_at(entry), entry[0].dtype) for entry in load]
    side_outs += [pltpu.HBM(a.shape, a.dtype) for a in save] + [struct(a.shape, a.dtype) for a in carry]
    heap_shape = [pltpu.HBM((sum(a.shape[0] for a in pile), *pile[0].shape[1:]), pile[0].dtype)] if pile else []
    return pl.pallas_call(
        kernel,
        out_shape=outs + side_outs + heap_shape,
        in_specs=specs
        + [anywhere] * (extra + len(load)) + [in_vmem()] * (len(save) + len(carry)) + [anywhere] * len(pile),
        out_specs=[anywhere if i in store else in_vmem() for i in range(n_out)]
        + [in_vmem()] * len(load) + [anywhere] * len(save) + [in_vmem()] * len(carry) + [anywhere] * len(heap_shape),
        scratch_shapes=list(scratch) + buffers,
        compiler_params=pltpu.CompilerParams(vmem_limit_bytes=vmem * MIB),
        cost_estimate=estimate,
    )(*args, *after, *side_args, *pile)


def shape_at(entry):
    array, place = entry[:2]
    return jax.eval_shape(lambda x: x[place], array).shape if place else array.shape


def hold(arrays, after):
    count = len(arrays)

    def kernel(*refs):
        for source, target in zip(refs[:count], refs[count + len(after) :]):
            target[...] = source[...]
        token = refs[-1]
        token[...] = jnp.zeros_like(token)

    anywhere = pl.BlockSpec(memory_space=pl.ANY)
    return pl.pallas_call(
        kernel,
        out_shape=[struct(a.shape, a.dtype) for a in arrays] + [struct((8, 128), F32)],
        in_specs=[in_vmem()] * count + [anywhere] * len(after),
        out_specs=[in_vmem()] * (count + 1),
        compiler_params=pltpu.CompilerParams(vmem_limit_bytes=16 * MIB),
        cost_estimate=pl.CostEstimate(flops=0, bytes_accessed=0, transcendentals=0),
    )(*arrays, *after)


def swap(values, axis, bit):
    size = lax.axis_size(axis)
    return lax.ppermute(values, axis, [(i, i ^ bit) for i in range(size)])


def bits_of(axis):
    size = lax.axis_size(axis)
    return [1 << i for i in range(size.bit_length() - 1)]


def head_order(width):
    half = width // 2
    source = iota((width, width), 0)
    target = iota((width, width), 1)
    wanted = (target % half) // HALF * HD + target // half * HALF + target % HALF
    return (source == wanted).astype(BF16)


def same_head(lanes):
    return (iota((lanes, lanes), 0) // HALF == iota((lanes, lanes), 1) // HALF).astype(BF16)


def head_total(values, ones):
    high = values.astype(BF16)
    low = (values - high.astype(F32)).astype(BF16)
    return dot(high, ones) + dot(low, ones)


def rope_head(lanes):
    half = lanes // 2
    return iota((1, lanes), 1) % half // HALF


def value_head(lanes):
    return iota((1, lanes), 1) // HD


def project_kernel(first, xa, xb, wq, wk, wv, gain, cos, sin, *refs):
    fars, more = refs[:7], refs[7:10]
    qi_out, ki_out, cos_far, sin_far = fars[:4]
    width = wq.shape[1]
    half = width // 2
    ones = same_head(half)
    if first == 0:
        order = head_order(width)
        more[0][...] = dot(wq.get()[...], order).astype(BF16)
        more[1][...] = dot(wk.get()[...], order).astype(BF16)
        wq, wk = more[0], more[1]
        wv = wv.get()
        more[2][...] = wv[...]
    cos_far.buffer[...] = cos[first : first + 2]
    sin_far.buffer[...] = sin[first : first + 2]
    cos_far.send()
    sin_far.send()
    for index, source in enumerate((xa, xb)):
        rows = source.get()[...] if isinstance(source, Fetched) else source[...]
        c, s = cos[first + index], sin[first + index]
        for weights, unit_out, inverse_out in ((wq, fars[4], qi_out), (wk, fars[5], ki_out)):
            full = dot(rows, weights[...])
            a, b = full[:, :half], full[:, half:]
            inverse = lax.rsqrt(head_total(a * a + b * b, ones) + EPS)
            inverse_out.buffer[index] = inverse
            unit_out.buffer[index, :, :half] = ((a * c - b * s) * inverse * gain[:, :half]).astype(BF16)
            unit_out.buffer[index, :, half:] = ((b * c + a * s) * inverse * gain[:, half:]).astype(BF16)
            inverse_out.send(index)
            unit_out.send(index)
        fars[6].buffer[index] = dot(rows, wv[...]).astype(BF16)
        fars[6].send(index)
    if first > 0:
        for near, far in zip(more, fars[4:]):
            near[...] = far.buffer[...]


def project(first, xa, xb, wq, wk, wv, gain, cos, sin, **sides):
    rows, depth = xa.shape
    width = wq.shape[1]
    low = [struct((2, rows, width), BF16)] * 3
    outs = [struct((2, rows, width // 2), F32)] * 4 + low
    args = (xa, xb, wq, wk, wv, gain, cos, sin)
    early = first == 0
    outs = outs + ([struct((depth, width), BF16)] * 3 if early else low)
    by_row = [(0,), (1,)]
    return run_whole(
        functools.partial(project_kernel, first), outs, args, 2 * 2 * rows * depth * width * 3, vmem=24,
        far_in=(0, 2, 3, 4) if early else (), fetch={2: None, 3: None, 0: None, 4: None} if early else {},
        store={0: by_row, 1: by_row, 2: None, 3: None, 4: by_row, 5: by_row, 6: by_row}, **sides,
    )


def pair_mask(seg_query, seg_key, query_block, key_block, query_dim, rows):
    allowed = seg_query == seg_key
    if query_block == key_block:
        query_id = iota((rows, rows), query_dim)
        key_id = iota((rows, rows), 1 - query_dim)
        allowed = (allowed & (key_id <= query_id)) | (key_id == query_id)
    return allowed


def column(row):
    return jnp.broadcast_to(row, (8, row.shape[1])).T[:, :1]


def join_pairs(buffer, first, second):
    buffer[0:2] = first[...]
    buffer[2:4] = second[...]


def attend_kernel(
    heads, me, q01, q23, k01, k23, v01, v23, seg_col, seg_row, head_out, inv_out, give_out, q, k, v, kbuf, vbuf
):
    blocks, rows, width = kbuf.shape
    join_pairs(q, q01, q23)
    join_pairs(k, k01, k23)
    join_pairs(v, v01, v23)
    mine = me[0, 0]
    q_head = rope_head(width)
    v_head = value_head(width)
    for block in range(blocks):
        slot = jnp.bitwise_xor(mine, block)
        kbuf[block] = k[slot]
        vbuf[block] = v[slot]
    for block in range(blocks):
        slot = jnp.bitwise_xor(mine, block)
        queries = q[slot]
        seg_q = column(seg_col[slot])
        count = block + 1
        allowed = jnp.concatenate(
            [
                pair_mask(seg_q, seg_row[jnp.bitwise_xor(mine, other)], block, other, 0, rows)
                for other in range(count)
            ],
            axis=1,
        )
        keys = kbuf[0:count].reshape(count * rows, width)
        values = vbuf[0:count].reshape(count * rows, width)
        inverse = jnp.zeros((rows, width), F32)
        mixed = jnp.zeros((rows, width), F32)
        for h in range(heads):
            scores = dot_nt(jnp.where(q_head == h, queries, jnp.zeros_like(queries)), keys)
            weight = jnp.where(allowed, jnp.exp2(scores * EXP_SCALE), 0.0)
            total = jnp.sum(weight, axis=1, keepdims=True)
            inverse = jnp.where(v_head == h, 1.0 / total, inverse)
            mixed = jnp.where(v_head == h, dot(weight.astype(BF16), values), mixed)
        inv_out[slot] = inverse
        head_out[slot] = (mixed * inverse).astype(BF16)
    give_out[0] = head_out[1]
    give_out[1] = head_out[3]


def attend(me, q, k, v, seg_col, seg_row, after, **sides):
    _, rows, width = q[0].shape
    blocks = 4
    heads = width // HD
    outs = [
        struct((blocks, rows, width), BF16),
        struct((blocks, rows, width), F32),
        struct((2, rows, width), BF16),
    ]
    args = (me, *q, *k, *v, seg_col, seg_row)
    scratch = [pltpu.VMEM((blocks, rows, width), BF16)] * 5
    return run_whole(
        functools.partial(attend_kernel, heads), outs, args,
        10 * heads * 2 * 2 * rows * rows * width, scratch, vmem=24, smem=1, after=after, far_out=(1,), far_in=(1, 3, 5), **sides,
    )


def out_project_kernel(heads, got, w_out, w_core, own, far):
    far[...] = (dot(heads[2], w_out[...]) + dot(got[1], w_core[...])).astype(BF16)
    own[...] = dot(heads[0], w_out[...]) + dot(got[0], w_core[...])


def out_project(heads, got, w_out, w_core):
    _, rows, width = heads.shape
    depth = w_out.shape[1]
    outs = [struct((rows, depth), F32), struct((rows, depth), BF16)]
    return run_whole(
        out_project_kernel, outs, (heads, got, w_out, w_core), 2 * 4 * rows * width * depth, vmem=16,
    )


def head_back_kernel(near, far, w_out, w_core, mine, give):
    part, depth = near.shape
    for i, source in enumerate((near, far)):
        span = slice(i * part, (i + 1) * part)
        rows = source[...]
        mine[span] = dot_nt(rows, w_out[...]).astype(BF16)
        give[span, :depth] = rows
        give[span, depth:] = dot_nt(rows, w_core[...]).astype(BF16)


def head_back(near, far, w_out, w_core, after):
    part, depth = near.shape
    width = w_out.shape[0]
    outs = [struct((2 * part, width), BF16), struct((2 * part, depth + width), BF16)]
    return run_whole(
        head_back_kernel, outs, (near, far, w_out, w_core), 2 * 4 * part * width * depth, vmem=16, after=after,
    )


def attend_back_kernel(
    heads, me, mine0, mine1, got0, got1, q01, q23, k01, k23, v01, v23, head_out, inv, qi01, qi23, ki01, ki23,
    seg_col, seg_row, gain, cos01, cos23, sin01, sin23, joined, scale_out, q, k, v, qm, km, dm, row_dot, dq, dk, dv,
):
    blocks, rows, width = q.shape
    inv = inv.get()
    join_pairs(q, q01.get(), q23.get())
    join_pairs(k, k01.get(), k23.get())
    join_pairs(v, v01.get(), v23.get())
    half = width // 2
    part = rows // PARTS
    depth = got0.shape[1] - width
    self_id = me[0, 0]
    q_head = rope_head(width)
    v_head = value_head(width)
    picks = (iota((8, width), 0) == iota((8, width), 1) // HD).astype(BF16)
    for slot in range(blocks):
        for c in range(PARTS):
            span = slice(c * part, (c + 1) * part)
            at = slice(slot // 2 * part, (slot // 2 + 1) * part)
            grads = (mine0, mine1)[c][at] if slot % 2 == 0 else (got0, got1)[c][at, depth:]
            scaled = (grads.astype(F32) * inv[slot, span]).astype(BF16)
            product = scaled.astype(F32) * head_out[slot, span].astype(F32)
            high = product.astype(BF16)
            low = (product - high.astype(F32)).astype(BF16)
            dots = dot_nt(picks, high) + dot_nt(picks, low)
            for h in range(heads):
                start = h * rows + c * part
                dm[slot, start : start + part] = jnp.where(v_head == h, scaled, jnp.zeros_like(scaled))
                row_dot[slot, :, start : start + part] = dots[h : h + 1]
        queries, keys = q[slot], k[slot]
        for h in range(heads):
            at = slice(h * rows, (h + 1) * rows)
            qm[slot, at] = jnp.where(q_head == h, queries, jnp.zeros_like(queries))
            km[slot, at] = jnp.where(q_head == h, keys, jnp.zeros_like(keys))
    for block in range(blocks):
        slot = jnp.bitwise_xor(self_id, block)
        for other in range(block + 1):
            there = jnp.bitwise_xor(self_id, other)
            allowed = pair_mask(seg_row[slot], column(seg_col[there]), block, other, 1, rows)
            allowed = jnp.concatenate([allowed] * heads, axis=1)
            scores = dot_nt(k[there], qm[slot])
            weight = jnp.where(allowed, jnp.exp2(scores * EXP_SCALE), 0.0)
            grad = (weight * (dot_nt(v[there], dm[slot]) - row_dot[slot])).astype(BF16)
            d_value = dot(weight.astype(BF16), dm[slot])
            d_key = dot(grad, qm[slot])
            stacked = jnp.concatenate([grad[:, h * rows : (h + 1) * rows] for h in range(heads)], axis=0)
            d_query = dot_tn(stacked, km[there])
            if other == block:
                dv[there] = d_value
                dk[there] = d_key
            else:
                dv[there] += d_value
                dk[there] += d_key
            if other == 0:
                dq[slot] = d_query
            else:
                dq[slot] += d_query
    order = head_order(width)
    ones = same_head(half)
    scale_sum = jnp.zeros((1, width), F32)
    for slot in range(blocks):
        c, s = [pair[slot // 2].get()[slot % 2] for pair in ((cos01, cos23), (sin01, sin23))]
        for place, (grad_ref, unit_ref, inv_ref) in enumerate(
            ((dq, q, (qi01, qi23)), (dk, k, (ki01, ki23)))
        ):
            inverse = inv_ref[slot // 2].get()[slot % 2]
            grads = grad_ref[slot] * SCORE_ROOT
            normed = unit_ref[slot].astype(F32) / gain[...]
            scale_sum = scale_sum + jnp.sum(normed * grads, axis=0, keepdims=True)
            grads = grads * gain[...]
            product = normed * grads
            along = head_total(product[:, :half] + product[:, half:], ones)
            a = (grads[:, :half] - normed[:, :half] * along) * inverse
            b = (grads[:, half:] - normed[:, half:] * along) * inverse
            turned = jnp.concatenate([(a * c + b * s).astype(BF16), (b * c - a * s).astype(BF16)], axis=1)
            joined[slot, :, place * width : (place + 1) * width] = dot_nt(turned, order).astype(BF16)
        joined[slot, :, 2 * width : 3 * width] = dv[slot].astype(BF16)
    scale_out[...] = jnp.zeros_like(scale_out)
    for h in range(heads):
        for side in range(2):
            at = side * half + h * HALF
            scale_out[2 * h + side : 2 * h + side + 1, :HALF] = scale_sum[:, at : at + HALF]


def attend_back(me, mine, got, q, k, v, head_out, inv, qi, ki, seg_col, seg_row, gain, cos, sin, **sides):
    blocks = 4
    _, rows, width = q[0].shape
    heads = width // HD
    outs = [struct((blocks, rows, 3 * width), BF16), struct((2 * heads, 128), F32)]
    args = (me, *mine, *got, *q, *k, *v, head_out, inv, *qi, *ki, seg_col, seg_row, gain, *cos, *sin)
    scratch = (
        [pltpu.VMEM((blocks, rows, width), BF16)] * 3
        + [pltpu.VMEM((blocks, heads * rows, width), BF16)] * 3
        + [pltpu.VMEM((blocks, 1, heads * rows), F32)]
        + [pltpu.VMEM((blocks, rows, width), F32)] * 3
    )
    return run_whole(
        functools.partial(attend_back_kernel, heads), outs, args,
        10 * heads * 5 * 2 * rows * rows * width, scratch, vmem=40, smem=1,
        fetch={i: None for i in (12, 5, 6, 7, 8, 9, 10, 13, 14, 15, 16, 20, 21, 22, 23)},
        far_in=(5, 6, 7, 8, 9, 10, 12, 13, 14, 15, 16, 20, 21, 22, 23), **sides,
    )


def input_grad_kernel(joined, wq, wk, wv, give_far, far, give, own):
    width = wq.shape[1]

    def rows_of(slot):
        out = dot_nt(joined[slot, :, :width], wq[...])
        out += dot_nt(joined[slot, :, width : 2 * width], wk[...])
        return out + dot_nt(joined[slot, :, 2 * width :], wv[...])

    give_far[...] = rows_of(3).astype(BF16)
    far[...] = rows_of(2)
    give[...] = rows_of(1).astype(BF16)
    own[...] = rows_of(0)


def input_grad(joined, wq, wk, wv, after, far_after):
    rows = joined.shape[1]
    depth, width = wq.shape
    outs = [struct((rows, depth), BF16), struct((rows, depth), F32)] * 2
    return run_whole(
        input_grad_kernel, outs, (joined, wq, wk, wv), 2 * 4 * rows * depth * width * 3, vmem=24, after=after, far_after=far_after, far_in=(1, 2, 3),
    )


def add_far_kernel(far, got, sum_out):
    sum_out[...] = (far[...] + got[...].astype(F32)).astype(BF16)


def add_far(far, got, after):
    return run_whole(add_far_kernel, [struct(far.shape, BF16)], (far, got), far.size, vmem=16, after=after)[0]


def unit_rows(values):
    inverse = lax.rsqrt(jnp.sum(values * values, axis=-1, keepdims=True) + EPS)
    return values * inverse, inverse


def unit_back(grad_in, normed, inverse):
    return (grad_in - normed * jnp.sum(normed * grad_in, axis=-1, keepdims=True)) * inverse


def mix_attn_kernel(c, own, far, tokens, rate, *refs):
    part = refs[-3].shape[0]
    span = slice(c * part, (c + 1) * part)
    total = own[span] + far[span].astype(F32)
    h_attn, _ = unit_rows(total)
    residual = tokens[span].astype(F32)
    h_one, _ = unit_rows(residual + rate[...] * (h_attn - residual))
    low = h_one.astype(BF16)
    low_out, sum_out, both_out = refs[-3:]
    low_out[...] = low
    if c > 0:
        sum_out[: c * part] = refs[0][...]
        both_out[: c * part] = refs[1][...]
        sum_out[span] = total.astype(BF16)
        both_out[span] = low
    else:
        sum_out[...] = total.astype(BF16)
        both_out[...] = jnp.zeros_like(both_out)


def mix_mlp_kernel(c, own, far, h_one, rate, cotangent, *refs):
    out, low_out, mix_out, rate_out, both_out = refs[-5:]
    part = far.shape[0]
    total = own[...] + far[...].astype(F32)
    h_mlp, mlp_inverse = unit_rows(total)
    first = h_one[...].astype(F32)
    away = h_mlp - first
    block_out, out_inverse = unit_rows(first + rate[...] * away)
    (out if c > 0 else out.buffer)[...] = block_out
    d_mix = unit_back(cotangent[...].astype(F32), block_out, out_inverse)
    (mix_out if c > 0 else mix_out.buffer)[...] = d_mix.astype(BF16)
    if c == 0:
        out.send()
        mix_out.send()
    rate_out[...] = jnp.sum(d_mix * away, axis=0, keepdims=True)
    low = unit_back(rate[...] * d_mix, h_mlp, mlp_inverse).astype(BF16)
    low_out[...] = low
    if c > 0:
        both_out[: c * part] = refs[0][...]
        both_out[c * part :] = low
    else:
        both_out[...] = jnp.zeros_like(both_out)


def mix_back_kernel(own, far, d_mix_two, attn_sum, h_one, tokens, rate, mlp_rate, low_out, rest_out, rate_out):
    h_attn, attn_inverse = unit_rows(attn_sum[...].astype(F32))
    residual = tokens[...].astype(F32)
    away = h_attn - residual
    _, one_inverse = unit_rows(residual + rate[...] * away)
    d_one = own[...] + far[...].astype(F32)
    d_one = d_one + (1.0 - mlp_rate[...]) * d_mix_two[...].astype(F32)
    d_mix = unit_back(d_one, h_one[...].astype(F32), one_inverse)
    rest_out[...] = (1.0 - rate[...]) * d_mix
    rate_out[...] = jnp.sum(d_mix * away, axis=0, keepdims=True)
    low_out[...] = unit_back(rate[...] * d_mix, h_attn, attn_inverse).astype(BF16)


def silu_parts(gate):
    sig = 0.5 * jnp.tanh(0.5 * gate) + 0.5
    return sig, gate * sig


def load_weights(arrays, kept, after, **sides):
    count = len(arrays)

    def kernel(*refs):
        sources, rest = refs[: count + len(kept)], refs[count + len(kept) :]
        target, kept_here, semaphores = rest[0], rest[1:-1], rest[-1]
        copies = []
        for n, source in enumerate(sources):
            to = target.at[n] if n < count else kept_here[n - count]
            copies.append(pltpu.make_async_copy(source, to, semaphores.at[n]))
        for copy in copies:
            copy.start()
        for copy in copies:
            copy.wait()

    args = (*arrays, *kept)
    every = tuple(range(len(args)))
    outs = [struct((count,) + arrays[0].shape, BF16)] + [struct(k.shape, BF16) for k in kept]
    return run_whole(
        kernel, outs, args, 0, [pltpu.SemaphoreType.DMA((len(args),))],
        vmem=20, after=after, raw=every, far_in=every, **sides,
    )


def column_tiles(width, tile=512):
    return [(slice(None), slice(start, start + tile)) for start in range(0, width, tile)]


def feed_kernel(near, far, weights, scales, kept_out, hid_out, give, own, sent, rows):
    kept, hid = kept_out.buffer, hid_out.buffer
    part, depth = near.shape
    tile = 512
    width = hid.shape[1]
    rows[:part] = near[...]
    rows[part:] = far[...]
    for i in range(2):
        for n, start in enumerate(range(0, width, tile)):
            span = slice(start, start + tile)
            up = dot(rows[...], weights[3 * i, :, span])
            gate = dot(rows[...], weights[3 * i + 1, :, span])
            kept[i, :, span] = up.astype(BF16)
            kept[2 + i, :, span] = gate.astype(BF16)
            kept_out.send(2 * i + n, 4 + 2 * i + n)
            _, active = silu_parts(scales[2 * i + 1 : 2 * i + 2, span] * gate)
            hidden = (scales[2 * i : 2 * i + 1, span] * up * active).astype(BF16)
            if i == 0:
                hid[:, span] = hidden
                hid_out.send(n)
            else:
                give[:, span] = hidden
    total = dot(hid[...], weights[2]) + dot(give[...], weights[5])
    own[...] = total[:part]
    sent[...] = total[part:].astype(BF16)


def feed(near, far, weights, scales, after, **sides):
    part, depth = near.shape
    rows = 2 * part
    width = weights.shape[2]
    outs = [
        struct((4, rows, width), BF16), struct((rows, width), BF16),
        struct((rows, width), BF16), struct((part, depth), F32), struct((part, depth), BF16),
    ]
    tiles = column_tiles(width)
    return run_whole(
        feed_kernel, outs, (near, far, weights, scales), 12 * rows * depth * width,
        scratch=[pltpu.VMEM((rows, depth), BF16)], vmem=FEED_VMEM, after=after,
        store={0: [(i, *tile) for i in range(4) for tile in tiles], 1: tiles}, **sides,
    )


def feed_back_kernel(near, far, weights, scales, kept, d_up_out, d_gate_out, sums_out, give, own, sent, rows):
    d_up_all, d_gate_all = d_up_out.buffer, d_gate_out.buffer
    part, depth = near.shape
    tile = 512
    width = d_up_all.shape[1]
    rows[:part] = near[...]
    rows[part:] = far[...]
    for i in range(2):
        for n, start in enumerate(range(0, width, tile)):
            span = slice(start, start + tile)
            at = slice(i * width + start, i * width + start + tile)
            d_hidden = dot_nt(rows[...], weights[3 * i + 2, span])
            up_scale = scales[2 * i : 2 * i + 1, span]
            gate_scale = scales[2 * i + 1 : 2 * i + 2, span]
            up = kept[i, :, span].astype(F32)
            gate = kept[2 + i, :, span].astype(F32)
            scaled = gate_scale * gate
            sig, active = silu_parts(scaled)
            d_up_scaled = d_hidden * active
            d_gate_scaled = d_hidden * (up_scale * up) * (sig + active * (1.0 - sig))
            d_up = (d_up_scaled * up_scale).astype(BF16)
            d_gate = (d_gate_scaled * gate_scale).astype(BF16)
            sums_out[0:1, at] = jnp.sum(d_up_scaled * up, axis=0, keepdims=True)
            sums_out[1:2, at] = jnp.sum(d_gate_scaled * gate, axis=0, keepdims=True)
            if i == 0:
                d_up_all[:, span] = d_up
                d_gate_all[:, span] = d_gate
                d_up_out.send(n)
                d_gate_out.send(n)
            else:
                give[0, :, span] = d_up
                give[1, :, span] = d_gate
    total = dot_nt(d_up_all[...], weights[0]) + dot_nt(d_gate_all[...], weights[1])
    total += dot_nt(give[0], weights[3]) + dot_nt(give[1], weights[4])
    own[...] = total[:part]
    sent[...] = total[part:].astype(BF16)


def feed_back(near, far, weights, scales, kept, after, **sides):
    part, depth = near.shape
    rows = 2 * part
    width = weights.shape[2]
    outs = [
        struct((rows, width), BF16), struct((rows, width), BF16), struct((2, 2 * width), F32),
        struct((2, rows, depth), BF16), struct((part, depth), F32), struct((part, depth), BF16),
    ]
    tiles = column_tiles(width)
    return run_whole(
        feed_back_kernel, outs, (near, far, weights, scales, kept), 12 * rows * depth * width,
        scratch=[pltpu.VMEM((rows, depth), BF16)], vmem=FEED_VMEM, after=after, store={0: tiles, 1: tiles}, **sides,
    )


def view(ref, place):
    return ref.at[place] if place else ref


def piece_place(piece, bits):
    flags = [piece // bit % 2 for bit in bits]
    return flags[0], flags[1] + 2 * flags[2]


def weight_kernel(groups, orders, vectors, me, *refs):
    n_in = sum(len(left) + len(right) for left, right in groups) + vectors
    inputs = list(refs[:n_in])
    results = refs[n_in : n_in + 2 * len(orders)]
    targets = [r.buffer if isinstance(r, Stored) else r for r in results]
    turned = refs[-1]
    piece = 128
    count, half = turned.shape[0] // piece, turned.shape[0] // 2
    mine = me[0, 0]
    pieces = sorted(range(count), key=lambda j: (1 - piece_place(j, orders[0][0])[0], piece_place(j, orders[0][0])[1]))
    if vectors:
        lines = [inputs.pop(0) for _ in range(vectors)]
        for j in pieces:
            sent, position = piece_place(j, orders[0][0])
            target = targets[1 - sent]
            rows, width = target.shape[1] - piece, target.shape[2]
            owner = jnp.bitwise_xor(mine, j)
            row = iota((rows, width), 0)
            block = jnp.zeros((rows, width), F32)
            for n, line in enumerate(lines):
                values = line[pl.ds(owner, 1), :]
                if values.shape[1] < width:
                    values = jnp.concatenate([values, jnp.zeros((1, width - values.shape[1]), F32)], axis=1)
                block = jnp.where(row == n, values, block)
            target[position, piece:] = block.astype(BF16)
    base = 0
    for left_places, right_places in groups:
        left = [(inputs.pop(0), place) for place in left_places]
        right = [(inputs.pop(0), place) for place in right_places]
        start = 0
        for source, place in left:
            ref = view(source.get(), place)
            for n, j in enumerate(pieces):
                at = jnp.bitwise_xor(mine, j) * piece
                columns = ref[:, pl.ds(pl.multiple_of(at, piece), piece)]
                turned[n * piece : (n + 1) * piece, start : start + ref.shape[0]] = columns.T
            start += ref.shape[0]
        for side in range(2):
            start = 0
            product = None
            for source, place in right:
                ref = view(source.get(), place)
                rows = ref.shape[0]
                part = dot(turned[side * half : (side + 1) * half, start : start + rows], ref[...])
                product = part if product is None else product + part
                start += rows
            product = product.astype(BF16)
            width = product.shape[1]
            begin = 0
            for n, (bits, columns) in enumerate(orders):
                first, last = max(base, begin), min(base + width, begin + columns)
                if first < last:
                    for i, j in enumerate(pieces[side * count // 2 : (side + 1) * count // 2]):
                        sent, position = piece_place(j, bits)
                        targets[2 * n + 1 - sent][position, :piece, first - begin : last - begin] = product[
                            i * piece : (i + 1) * piece, first - base : last - base
                        ]
                begin += columns
            if side == 1 and len(orders) == 1 and len(groups) == 1 and isinstance(results[1], Stored):
                results[1].send()
            if side == 0 and len(orders) == 1 and len(groups) == 1 and isinstance(results[0], Stored):
                results[0].send()
        base += width


def weight_halves(me, groups, n_groups, orders, after=(), far_after=(), vectors=(), far_kept=True, far_sent=False, **sides):
    depth = shape_at(groups[0][0][0])[1]
    rows = sum(shape_at(entry)[0] for entry in groups[0][0])
    piece = depth // n_groups
    outs = [
        struct((n_groups // 2, piece + (VECTOR_ROWS if vectors and n == 0 else 0), columns), BF16)
        for n, (_, columns) in enumerate(orders) for _ in range(2)
    ]
    entries = [entry for left, right in groups for entry in (*left, *right)]
    args = (me, *vectors, *[a for a, _, _ in entries])
    places = [([p for _, p, _ in left], [p for _, p, _ in right]) for left, right in groups]
    total = sum(columns for _, columns in orders)
    skip = 1 + len(vectors)
    results = run_whole(
        functools.partial(weight_kernel, places, orders, len(vectors)), outs, args, 2 * rows * depth * total,
        [pltpu.VMEM((depth, rows), BF16)], vmem=24, smem=1, after=after,
        fetch={skip + i: [p] if p else None for i, (_, p, _) in enumerate(entries)},
        far_in=tuple(skip + i for i, (_, _, far) in enumerate(entries) if far), far_after=far_after,
        store={i: None for i in range(len(outs)) if (far_kept if i % 2 else far_sent)}, **sides,
    )
    return [*[results[2 * n : 2 * n + 2] for n in range(len(orders))], *results[len(outs) :]]


def merge_kernel(kept, got, *outs):
    for i in range(kept.shape[0] // 2):
        outs[0][i] = (kept[2 * i + 1].astype(F32) + got[2 * i + 1].astype(F32)).astype(BF16)
        outs[1][i] = (kept[2 * i].astype(F32) + got[2 * i].astype(F32)).astype(BF16)


def merge(kept, got, after=()):
    count, rows, columns = kept.shape
    outs = [struct((count // 2, rows, columns), BF16)] * 2
    return run_whole(merge_kernel, outs, (kept, got), kept.size, vmem=16, after=after)


def finish(kept, got, parts, after=()):
    def kernel(kept_ref, got_ref, *outs):
        total = kept_ref[0].astype(F32) + got_ref[0].astype(F32)
        for (row, rows, column, columns, turned), out in zip(parts, outs):
            piece = total[row : row + rows, column : column + columns]
            out[...] = piece.T if turned else piece

    outs = [struct((c, r) if turned else (r, c), F32) for _, r, _, c, turned in parts]
    return run_whole(
        kernel, outs, (kept, got), kept.size, vmem=16, after=after, far_out=tuple(range(len(outs)))
    )


def block_of(entry):
    array, place, _ = entry
    return array[place] if place else array


def weight_halves_plain(me, groups, n_groups, orders, after=(), far_after=(), vectors=(), far_kept=True, far_sent=False, load=(), save=(), carry=(), pile=()
):
    products = [
        dot_tn(jnp.concatenate([block_of(e) for e in left], axis=0), jnp.concatenate([block_of(e) for e in right], axis=0))
        for left, right in groups
    ]
    product = jnp.concatenate(products, axis=1)
    parts = product.reshape(n_groups, product.shape[0] // n_groups, product.shape[1])
    order = jnp.bitwise_xor(me[0, 0], jnp.arange(n_groups, dtype=jnp.int32))
    parts = parts[order]
    results, start = [], 0
    for n, (_, columns) in enumerate(orders):
        chosen = parts[:, :, start : start + columns]
        if vectors and n == 0:
            lines = [jnp.pad(v[order], ((0, 0), (0, columns - v.shape[1])))[:, None] for v in vectors]
            chosen = jnp.concatenate([chosen, *lines], axis=1)
            chosen = jnp.pad(chosen, ((0, 0), (0, VECTOR_ROWS - len(lines)), (0, 0)))
        chosen = chosen.reshape((n_groups // 2, 2) + chosen.shape[1:]).astype(BF16)
        results.append((chosen[:, 1], chosen[:, 0]))
        start += columns
    loaded = [array[place] if place else array for array, place in load]
    return [*results, *loaded, *save, *carry, *([jnp.concatenate(pile)] if pile else [])]


def add(pair, after=()):
    kept, got = pair
    if kept.shape[1] >= 128:
        return merge(kept, got, after)
    total = kept.astype(F32) + got.astype(F32)
    parts = total.reshape((kept.shape[0] // 2, 2) + kept.shape[1:]).astype(BF16)
    return parts[:, 1], parts[:, 0]


def stage(pair, bit, after=()):
    sent, kept = add(pair, after)
    return kept, swap(sent, "dp", bit)


def combine_kernel(*refs):
    pairs, (sent, kept) = refs[:-2], refs[-2:]
    start = 0
    for a, b in zip(pairs[::2], pairs[1::2]):
        rows, columns = a.shape[1:]
        span = slice(start, start + columns)
        for piece, target in ((1, sent), (0, kept)):
            target[0, :rows, span] = (a[piece].astype(F32) + b[piece].astype(F32)).astype(BF16)
            if rows < target.shape[1]:
                target[0, rows:, span] = jnp.zeros((target.shape[1] - rows, columns), BF16)
        start += columns


def combine(pairs, after=()):
    count = pairs[0][0].shape[0]
    rows = max(kept.shape[1] for kept, _ in pairs)
    if count == 2 and rows >= 128:
        out = struct((1, rows, sum(kept.shape[2] for kept, _ in pairs)), BF16)
        return run_whole(combine_kernel, [out, out], [x for pair in pairs for x in pair], 0, vmem=16, after=after)
    totals = [kept.astype(F32) + got.astype(F32) for kept, got in pairs]
    total = jnp.concatenate([jnp.pad(t, ((0, 0), (0, rows - t.shape[1]), (0, 0))) for t in totals], axis=2)
    parts = total.reshape((count // 2, 2) + total.shape[1:]).astype(BF16)
    return parts[:, 1], parts[:, 0]


def last_stage(pair, bits, parts, after=()):
    for bit in bits:
        pair = stage(pair, bit)
    kept, got = pair
    if kept.shape[1] >= 128:
        return finish(kept, got, parts, after)
    total = (kept.astype(F32) + got.astype(F32))[0]
    pieces = [total[r : r + rows, c : c + columns] for r, rows, c, columns, _ in parts]
    return [piece.T if part[-1] else piece for piece, part in zip(pieces, parts)]


def shards(
    tokens,
    seq_lengths,
    w_query,
    w_key,
    w_value,
    w_out,
    qk_scale,
    attn_rate,
    w_up,
    w_gate,
    up_scale,
    gate_scale,
    w_down,
    mlp_rate,
    out_grad,
):
    local_rows, depth = tokens.shape
    n_mp = lax.axis_size("mp")
    n_dp = lax.axis_size("dp")
    assert n_mp == 4
    width = w_query.shape[1]
    hidden_width = w_up.shape[1]
    heads = width // HD
    part = local_rows // PARTS
    me = lax.axis_index("mp").astype(jnp.int32)
    me_ref = me.reshape(1, 1)
    group = lax.axis_index("dp").astype(jnp.int32)
    group_ref = group.reshape(1, 1)
    dp_bits = bits_of("dp")
    seq_count = seq_lengths.shape[1]

    far_tokens = swap(tokens, "mp", 2)
    core_tokens = swap(tokens, "mp", 1)
    ends = jnp.cumsum(seq_lengths[0])
    starts = jnp.concatenate([jnp.zeros((1,), jnp.int32), ends])
    owner = jnp.bitwise_xor(me, jnp.arange(n_mp, dtype=jnp.int32))
    row_ids = owner[:, None] * local_rows + jnp.arange(local_rows, dtype=jnp.int32)[None]
    segment = jnp.sum((row_ids[:, :, None] >= ends).astype(jnp.int32), axis=2)
    first = jnp.sum(
        jnp.where(segment[:, :, None] == jnp.arange(seq_count + 1, dtype=jnp.int32), starts, 0), axis=2
    )
    position = (row_ids - first).astype(F32)
    frequency = jnp.exp(jnp.arange(HALF, dtype=F32) * (-2.0 * math.log(10000.0) / HD))
    angles = position[:, :, None] * jnp.tile(frequency, heads)[None, None]
    cos, sin = jnp.cos(angles), jnp.sin(angles)
    seg_q = jnp.where(segment < seq_count, segment, -1).astype(F32)[:, None, :]
    seg_k = jnp.where(segment < seq_count, segment, -2).astype(F32)[:, None, :]
    gain = qk_scale.reshape(heads, 2, HALF).transpose(1, 0, 2).reshape(1, width)

    scale_rows = jnp.stack([up_scale, gate_scale * math.sqrt(depth)])
    core_out = swap(w_out, "mp", 1)
    core_rows = swap(scale_rows, "mp", 1)
    core_up = swap(w_up, "mp", 1)
    core_gate = swap(w_gate, "mp", 1)
    core_down = swap(w_down, "mp", 1)
    scales = jnp.concatenate([scale_rows, core_rows], axis=0)

    weights = (w_query, w_key, w_value)
    early = project(0, tokens, core_tokens, *weights, gain, cos, sin, save=[core_tokens])
    far_tokens, _ = hold([far_tokens], (early[9],))
    cross_tokens = swap(far_tokens, "mp", 1)
    late = project(
        2, far_tokens, cross_tokens, *early[7:10], gain, cos, sin, save=[far_tokens, cross_tokens]
    )
    core_tokens, far_tokens, cross_tokens = early[10], late[10], late[11]
    qi, ki, cos_far, sin_far, q_far, k_far, v_far = zip(early[:7], late[:7])
    q, k, v = zip(early[4:7], late[7:10])
    head_out, inv, give, out_here = attend(
        me_ref, q, k, v, seg_q, seg_k, (core_up, core_gate, core_down, core_out, core_rows), load=[(w_out, ())]
    )
    attn_own, attn_far = out_project(head_out, swap(give, "mp", 1), out_here, core_out)
    feed_parts = [w_up, w_gate, w_down, core_up, core_gate, core_down]
    feed_weights, tokens_here = load_weights(feed_parts, (), (attn_own,), load=[(tokens, ())])
    attn_far = swap(attn_far, "mp", 2)

    attn_row = attn_rate.reshape(1, depth)
    mlp_row = mlp_rate.reshape(1, depth)
    full, lowered, vector = struct((part, depth), F32), struct((part, depth), BF16), struct((1, depth), F32)
    both = struct((2 * part, depth), BF16)

    def part_of(c):
        return (slice(c * part, (c + 1) * part),)

    def mix_attn(c, after, *before):
        outs = [lowered, both, both] if c else [lowered, lowered, struct((8, 128), BF16)]
        return run_whole(
            functools.partial(mix_attn_kernel, c), outs, (attn_own, attn_far, tokens_here, attn_row, *before),
            20 * part * depth, vmem=16, after=after,
        )

    def mix_mlp(c, own, far, h_one, cotangent, after, *before):
        return run_whole(
            functools.partial(mix_mlp_kernel, c),
            [full, lowered, lowered, vector, both if c else struct((8, 128), BF16)],
            (own, far, h_one, mlp_row, cotangent, *before), LATER if c else 0, vmem=16, after=after,
            store={} if c else {0: None, 2: None},
        )

    def mix_back(own, far, d_mix, attn_sum, h_one, rows, after, flops=0):
        return run_whole(
            mix_back_kernel, [lowered, full, vector],
            (own, far, d_mix, attn_sum, h_one, rows, attn_row, mlp_row), flops, vmem=16, after=after,
        )

    fast = depth // n_dp == 128 and len(dp_bits) == 3
    later_bits = [dp_bits[1], dp_bits[0], dp_bits[2]] if fast else dp_bits

    def weight_grad(groups, orders, after=(), far_after=(), vectors=(), **sides):
        run = weight_halves if fast else weight_halves_plain
        return run(group_ref, groups, n_dp, orders, after, far_after, vectors, **sides)

    def whole(array, far=False):
        return (array, (), far)

    def layer(array, i, far=False):
        return (array, (i,), far)

    def rows_of(array, c, far=False):
        return (array, (slice(c * part, (c + 1) * part),), far)

    def over_dp(array, bit):
        return swap(array, "dp", bit)

    def cross(array):
        return swap(array, "mp", 2)

    def core(array):
        return swap(array, "mp", 1)

    near_a, sum_a, _ = mix_attn(0, (feed_weights,))
    far_a = cross(near_a)
    near_b, sums, near_rows = mix_attn(1, (near_a,), sum_a, near_a)

    near_b, token = hold([near_b], (far_a,))
    far_b = cross(near_b)
    core_near = core(near_rows)
    core_far_a = core(far_a)
    kept_a, hid_a, give_a, own_a, sent, sums, near_rows = feed(
        near_a, far_a, feed_weights, scales, (token,), save=[sums, near_rows]
    )
    core_hid_a = core(give_a)

    sent, token = hold([sent], (far_b,))
    got = cross(sent)
    core_far_b = core(far_b)
    kept_b, hid_b, give_b, own_b, sent, cotangent = feed(
        near_b, far_b, feed_weights, scales, (token,), load=[(out_grad, part_of(0))]
    )
    core_hid_b = core(give_b)

    sent, token = hold([sent], (got, core_near, core_far_a, core_far_b))
    got_b = cross(sent)
    out_a, d_near_a, d_mix_a, rate_a, _ = mix_mlp(0, own_a, got, near_a, cotangent, (token,))
    d_far_a = cross(d_near_a)
    back_weights, kept_a, kept_b, cotangent, own_b = load_weights(
        feed_parts, (kept_a, kept_b), (d_near_a,),
        load=[(out_grad, part_of(1))], carry=[own_b],
    )

    out_b, d_near_b, d_mix_b, rate_b, d_near_rows = mix_mlp(
        1, own_b, got_b, near_b, cotangent, (core_hid_a,), d_near_a
    )
    d_far_b = cross(d_near_b)
    core_d_near = core(d_near_rows)
    core_d_far_a = core(d_far_a)
    d_up_a, d_gate_a, sums_a, give_a, own_a, sent, d_mix_b, d_near_rows, block_out = feed_back(
        d_near_a, d_far_a, back_weights, scales, kept_a, (d_near_b,),
        save=[d_mix_b, d_near_rows], pile=[out_a, out_b],
    )

    sent, give_a, token = hold([sent, give_a], (d_far_b, core_hid_b))
    got_a = cross(sent)
    core_give_a = core(give_a)
    core_d_far_b = core(d_far_b)
    d_up_b, d_gate_b, sums_b, give_b, own_b, sent = feed_back(
        d_near_b, d_far_b, back_weights, scales, kept_b, (token,)
    )
    down_a, down_b, d_mix_a, sum_a, rows_a, h_one_a, own_a = weight_grad(
        [(
            [rows_of(d_near_rows, 0, True), whole(d_far_a), rows_of(d_near_rows, 1, True), whole(d_far_b),
             rows_of(core_d_near, 0), whole(core_d_far_a, True), rows_of(core_d_near, 1), whole(core_d_far_b, True)],
            [whole(hid_a, True), whole(hid_b, True), whole(core_hid_a), whole(core_hid_b)],
        )],
        [(dp_bits, hidden_width // 2), (later_bits, hidden_width // 2)], (sums_b,), far_kept=False,
        load=[(d_mix_a, ()), (sums, part_of(0)), (tokens, part_of(0)), (near_rows, part_of(0))], carry=[own_a],
    )

    sent, give_b, sent_a, sent_b, token = hold([sent, give_b, down_a[0], down_b[0]], (got_a,))
    got_b = cross(sent)
    core_give_b = core(give_b)
    down_a = (down_a[1], over_dp(sent_a, dp_bits[0]))
    down_b = (down_b[1], over_dp(sent_b, later_bits[0]))
    a_near_a, rest_a, attn_rate_a = mix_back(own_a, got_a, d_mix_a, sum_a, h_one_a, rows_a, (token,))
    a_far_a = cross(a_near_a)
    rows_in = [
        rows_of(near_rows, 0, True), whole(far_a), rows_of(near_rows, 1, True), whole(far_b),
        rows_of(core_near, 0, True), whole(core_far_a, True), rows_of(core_near, 1, True), whole(core_far_b, True),
    ]
    grad_up, d_mix_b, sum_b, rows_b, h_one_b, out_here, rest_a, own_b = weight_grad(
        [(rows_in, [whole(d_up_a, True), whole(d_up_b, True), layer(core_give_a, 0), layer(core_give_b, 0)])],
        [(dp_bits, hidden_width)], (a_near_a,), far_sent=True,
        load=[(d_mix_b, ()), (sums, part_of(1)), (tokens, part_of(1)), (near_rows, part_of(1)), (w_out, ())],
        save=[rest_a], carry=[own_b],
    )

    a_near_b, rest_b, attn_rate_b = mix_back(own_b, got_b, d_mix_b, sum_b, h_one_b, rows_b, (), LATER)
    a_far_b = cross(a_near_b)
    sent_a, kept_a = add(down_a, (a_near_b,))
    sent_b, kept_b = add(down_b, (sent_a,))
    sent_a, sent_b, token = hold([sent_a, sent_b], ())
    down_a = (kept_a, over_dp(sent_a, dp_bits[1]))
    down_b = (kept_b, over_dp(sent_b, later_bits[1]))

    def pack_kernel(part_a, part_b, rate_a, rate_b, rate_c, rate_d, own_ref, core_ref):
        total = part_a[...] + part_b[...]
        own_ref[0:2] = total[:, :hidden_width]
        own_ref[2:3] = rate_a[...] + rate_b[...]
        own_ref[3:4] = rate_c[...] + rate_d[...]
        core_ref[0:2] = total[:, hidden_width:]
        core_ref[2:4] = own_ref[2:4]

    def pair_kernel(own_ref, got_ref, sum_ref, rate_ref):
        sum_ref[...] = own_ref[...] + got_ref[...]
        rate_ref[...] = own_ref[2:4] + got_ref[2:4]

    size = depth // n_dp

    def table_kernel(sum_ref, got_ref, scale_ref, rate_ref):
        rates = sum_ref[2:4] + got_ref[...]
        for target, lines in (
            (scale_ref, [sum_ref[0:1], sum_ref[1:2] * math.sqrt(depth)]),
            (rate_ref, [rates[0:1], rates[1:2]]),
        ):
            for n, line in enumerate(lines):
                for p in range(n_dp):
                    target[p : p + 1, n * size : (n + 1) * size] = line[:, p * size : (p + 1) * size]

    four = struct((4, depth), F32)
    assert hidden_width == depth
    own_sums, core_sums = run_whole(
        pack_kernel, [four, four], (sums_a, sums_b, attn_rate_a, attn_rate_b, rate_a, rate_b), 0, vmem=8,
        after=(token,),
    )
    core_sums = core(core_sums)
    head_a = head_back(a_near_a, a_far_a, out_here, core_out, (a_near_b, own_sums))
    pair_sums, rates = run_whole(
        pair_kernel, [four, struct((2, depth), F32)], (own_sums, core_sums), 0, vmem=8, after=(head_a[0],)
    )
    rates = cross(rates)
    grad_gate, up_sent, rests = weight_grad(
        [(rows_in, [whole(d_gate_a, True), whole(d_gate_b, True), layer(core_give_a, 1), layer(core_give_b, 1)])],
        [(later_bits, hidden_width)], (pair_sums,), pile=[rest_a, rest_b], load=[(grad_up[0], ())],
    )

    if fast:
        lines = run_whole(
            table_kernel, [struct((n_dp, 2 * size), F32)] * 2, (pair_sums, rates), 0, vmem=8, after=(grad_gate[0],)
        )
    else:
        rates = pair_sums[2:4] + rates
        pairs = [(pair_sums[0], pair_sums[1] * math.sqrt(depth)), (rates[0], rates[1])]
        lines = [jnp.concatenate([x.reshape(n_dp, -1) for x in pair], axis=1) for pair in pairs]
    down_sent, down_kept = combine([down_a, down_b], (lines[0],))
    down_sent, up_sent, gate_sent, head_give, token = hold(
        [down_sent, up_sent, grad_gate[0], head_a[1]], (a_far_b,)
    )
    down = (down_kept, over_dp(down_sent, dp_bits[2]))
    up_got = over_dp(up_sent, dp_bits[0])
    gate_got = over_dp(gate_sent, later_bits[0])
    core_head_a = core(head_give)
    head_b = head_back(a_near_b, a_far_b, out_here, core_out, (token,))
    core_head_b = core(head_b[1])
    joined, qk_rows, up_kept, gate_kept = attend_back(
        me_ref, [head_a[0], head_b[0]], [core_head_a, core_head_b], q_far, k_far, v_far, head_out, inv, qi, ki,
        seg_k, seg_q, gain, cos_far, sin_far, load=[(grad_up[1], ()), (grad_gate[1], ())],
    )

    def attn_rows(array, half):
        return (array, (slice(half * part, (half + 1) * part), slice(0, depth)), False)

    if not fast:
        qk_rows = qk_rows[:, :HALF].reshape(n_dp, -1)
    give_far, far, give, own = input_grad(joined, *weights, (qk_rows,), ())
    up_sent, up_kept = add((up_kept, up_got), (own,))
    gate_sent, gate_kept = add((gate_kept, gate_got), (up_sent,))
    up_sent, gate_sent, give_far, token = hold([up_sent, gate_sent, give_far], ())
    grad_up = (up_kept, over_dp(up_sent, dp_bits[1]))
    grad_gate = (gate_kept, over_dp(gate_sent, later_bits[1]))
    far_got = core(give_far)
    token_rows = [whole(tokens, True), whole(core_tokens, True), whole(far_tokens, True), whole(cross_tokens, True)]
    first, second, own, give = weight_grad(
        [
            (
                [attn_rows(x, half) for pair in ((head_give, head_b[1]), (core_head_a, core_head_b))
                 for half in range(2) for x in pair],
                [layer(head_out, slot) for slot in (0, 2, 1, 3)],
            ),
            (token_rows, [layer(joined, slot) for slot in range(4)]),
        ],
        [(dp_bits, 2 * width + width // 2), (later_bits, 2 * width - width // 2)], vectors=(*lines, qk_rows), far_kept=False, after=(token,),
        carry=[own, give],
    )

    rest_bits = dp_bits[3:]
    feed_sent, feed_kept = combine([grad_up, grad_gate], (first[0],))
    far_sum = add_far(far, far_got, (feed_sent,))
    feed_sent, first_sent, second_sent, far_sum, down_got, token = hold(
        [feed_sent, first[0], second[0], far_sum, down[1]], ()
    )
    feeds = (feed_kept, over_dp(feed_sent, dp_bits[2]))
    first = (first[1], over_dp(first_sent, dp_bits[0]))
    second = (second[1], over_dp(second_sent, later_bits[0]))
    far_grad = cross(far_sum)
    (down,) = last_stage((down[0], down_got), rest_bits, [(0, size, 0, hidden_width, True)], (token,))

    first_sent, first_kept = add(first, (token,))
    second_sent, second_kept = add(second, (first_sent,))
    first_sent, second_sent, give, token = hold([first_sent, second_sent, give], ())
    first = (first_kept, over_dp(first_sent, dp_bits[1]))
    second = (second_kept, over_dp(second_sent, later_bits[1]))
    got = core(give)

    attn_sent, attn_kept = combine([first, second], (token,))
    attn = (attn_kept, over_dp(attn_sent, dp_bits[2]))
    late = (attn_kept,)
    grad_up, grad_gate = last_stage(
        feeds, rest_bits,
        [(0, size, 0, hidden_width, False), (0, size, hidden_width, hidden_width, False)], late,
    )
    short = width // n_dp
    grad_out, grad_query, grad_key, grad_value, scale_up, scale_gate, rate_attn, rate_mlp, scale_qk = last_stage(
        attn, rest_bits,
        [
            (0, size, 0, width, True), (0, size, width, width, False),
            (0, size, 2 * width, width, False), (0, size, 3 * width, width, False),
            (size, 1, 0, size, False), (size, 1, size, size, False),
            (size + 1, 1, 0, size, False), (size + 1, 1, size, size, False), (size + 2, 1, 0, short, False),
        ],
        late,
    )
    token_grad = rests + (own + got.astype(F32) + far_grad.astype(F32))
    return (
        block_out,
        token_grad,
        grad_query,
        grad_key,
        grad_value,
        grad_out,
        scale_qk[0],
        rate_attn[0],
        grad_up,
        grad_gate,
        scale_up[0],
        scale_gate[0],
        down,
        rate_mlp[0],
    )


def solution(mesh):
    in_specs = (
        P(("dp", "mp"), None),
        P("dp", None),
        P(None, "mp"),
        P(None, "mp"),
        P(None, "mp"),
        P("mp", None),
        P("mp"),
        P(),
        P(None, "mp"),
        P(None, "mp"),
        P("mp"),
        P("mp"),
        P("mp", None),
        P(),
        P(("dp", "mp"), None),
    )
    out_specs = (
        P(("dp", "mp"), None),
        P(("dp", "mp"), None),
        P("dp", "mp"),
        P("dp", "mp"),
        P("dp", "mp"),
        P("mp", "dp"),
        P(("mp", "dp")),
        P("dp"),
        P("dp", "mp"),
        P("dp", "mp"),
        P(("mp", "dp")),
        P(("mp", "dp")),
        P("mp", "dp"),
        P("dp"),
    )
    return jax.shard_map(shards, mesh=mesh, in_specs=in_specs, out_specs=out_specs, check_vma=False)
```

```python
import functools
import math

import jax
import jax.numpy as jnp
from jax import lax
from jax.experimental import pallas as pl
from jax.experimental.pallas import tpu as pltpu
from jax.sharding import PartitionSpec as P

HD = 64
HALF = HD // 2
EPS = 1e-06
F32 = jnp.float32
BF16 = jnp.bfloat16
SCORE_ROOT = math.sqrt(HD)
EXP_SCALE = SCORE_ROOT * math.log2(math.e)
MIB = 1 << 20
PARTS = 2
LATER = 5e8
FEED_VMEM = 24
VECTOR_ROWS = 16


def dot(left, right):
    return lax.dot_general(left, right, (((1,), (0,)), ((), ())), preferred_element_type=F32)


def dot_nt(left, right):
    return lax.dot_general(left, right, (((1,), (1,)), ((), ())), preferred_element_type=F32)


def dot_tn(left, right):
    return lax.dot_general(left, right, (((0,), (0,)), ((), ())), preferred_element_type=F32)


def iota(shape, dim):
    return lax.broadcasted_iota(jnp.int32, shape, dim)


def struct(shape, dtype):
    return jax.ShapeDtypeStruct(shape, dtype)


def in_vmem():
    return pl.BlockSpec(memory_space=pltpu.VMEM)


def in_smem():
    return pl.BlockSpec(memory_space=pltpu.SMEM)


def cost(flops, args, outs, transcendentals=0):
    moved = sum(a.size * a.dtype.itemsize for a in args)
    moved += sum(math.prod(o.shape) * jnp.dtype(o.dtype).itemsize for o in outs)
    return pl.CostEstimate(flops=int(2 * flops), bytes_accessed=int(2 * moved), transcendentals=int(transcendentals))


class Fetched:
    def __init__(self, copies, buffer):
        self.copies = copies
        self.buffer = buffer
        self.shape = buffer.shape
        self.waited = set()

    def start(self):
        for copy in self.copies:
            copy.start()

    def get(self, *parts):
        for n in parts or range(len(self.copies)):
            if n not in self.waited:
                self.copies[n].wait()
                self.waited.add(n)
        return self.buffer


class Stored:
    def __init__(self, copies, buffer):
        self.copies = copies
        self.buffer = buffer
        self.shape = buffer.shape
        self.sent = set()

    def send(self, *parts):
        for n in parts or range(len(self.copies)):
            if n not in self.sent:
                self.copies[n].start()
                self.sent.add(n)


def run_whole(
    body, outs, args, flops, scratch=(), vmem=32, smem=0, transcendentals=0, after=(), fetch=None, store=None,
    far_in=(), far_out=(), far_after=(), raw=(), load=(), save=(), carry=(), pile=()
):
    fetch, store = fetch or {}, store or {}
    after = (*after, *[pltpu.with_memory_space_constraint(a, pltpu.HBM) for a in far_after])
    count, extra, n_out = len(args), len(after), len(outs)
    fetch = {i: [()] if places is None else places for i, places in fetch.items()}
    store = {i: [()] if places is None else places for i, places in store.items()}
    n_copies = sum(len(places) for places in (*fetch.values(), *store.values()))
    n_copies += len(load) + len(save) + len(pile)
    sides = len(load) + len(save) + len(carry)

    def kernel(*refs):
        ins, refs = list(refs[:count]), refs[count + extra :]
        side_in, refs = refs[:sides], refs[sides:]
        heap, refs = refs[: len(pile)], refs[len(pile) :]
        results, refs = list(refs[:n_out]), refs[n_out:]
        side_out, rest = refs[:sides], refs[sides:]
        if pile:
            heap_out, rest = rest[0], rest[1:]
        own, rest = rest[: len(scratch)], list(rest[len(scratch) :])
        semaphores = rest.pop() if n_copies else None
        used = 0
        for i, places in fetch.items():
            buffer = rest.pop(0)
            copies = []
            for place in places:
                source, target = (ins[i].at[place], buffer.at[place]) if place else (ins[i], buffer)
                copies.append(pltpu.make_async_copy(source, target, semaphores.at[used]))
                used += 1
            ins[i] = Fetched(copies, buffer)
            ins[i].start()
        for i, places in store.items():
            buffer = rest.pop(0)
            copies = []
            for place in places:
                source, target = (buffer.at[place], results[i].at[place]) if place else (buffer, results[i])
                copies.append(pltpu.make_async_copy(source, target, semaphores.at[used]))
                used += 1
            results[i] = Stored(copies, buffer)
        moves = []
        for n in range(len(load) + len(save)):
            source = side_in[n]
            if n < len(load) and load[n][1]:
                source = source.at[load[n][1]]
            moves.append(pltpu.make_async_copy(source, side_out[n], semaphores.at[used]))
            used += 1
        start = 0
        for ref in heap:
            target = heap_out.at[start : start + ref.shape[0]]
            moves.append(pltpu.make_async_copy(ref, target, semaphores.at[used]))
            start += ref.shape[0]
            used += 1
        for move in moves:
            move.start()
        for n in range(len(load) + len(save), sides):
            side_out[n][...] = side_in[n][...]
        body(*ins, *results, *own)
        for i in fetch:
            ins[i].get()
        for i in store:
            results[i].send()
        for i in store:
            for copy in results[i].copies:
                copy.wait()
        for move in moves:
            move.wait()

    def in_hbm(array):
        return pltpu.with_memory_space_constraint(array, pltpu.HBM)

    estimate = cost(flops, args, outs, transcendentals)
    buffers = [pltpu.VMEM(args[i].shape, args[i].dtype) for i in fetch]
    buffers += [pltpu.VMEM(outs[i].shape, outs[i].dtype) for i in store]
    if n_copies:
        buffers.append(pltpu.SemaphoreType.DMA((n_copies,)))
    args = [in_hbm(a) if i in far_in else a for i, a in enumerate(args)]
    outs = [pltpu.HBM(o.shape, o.dtype) if i in store or i in far_out else o for i, o in enumerate(outs)]
    anywhere = pl.BlockSpec(memory_space=pl.ANY)
    specs = [
        in_smem() if i < smem else anywhere if i in fetch or i in raw else in_vmem() for i in range(count)
    ]
    side_args = [in_hbm(a) for a, _ in load] + [*save, *carry]
    side_outs = [struct(shape_at(entry), entry[0].dtype) for entry in load]
    side_outs += [pltpu.HBM(a.shape, a.dtype) for a in save] + [struct(a.shape, a.dtype) for a in carry]
    heap_shape = [pltpu.HBM((sum(a.shape[0] for a in pile), *pile[0].shape[1:]), pile[0].dtype)] if pile else []
    return pl.pallas_call(
        kernel,
        out_shape=outs + side_outs + heap_shape,
        in_specs=specs
        + [anywhere] * (extra + len(load)) + [in_vmem()] * (len(save) + len(carry)) + [anywhere] * len(pile),
        out_specs=[anywhere if i in store else in_vmem() for i in range(n_out)]
        + [in_vmem()] * len(load) + [anywhere] * len(save) + [in_vmem()] * len(carry) + [anywhere] * len(heap_shape),
        scratch_shapes=list(scratch) + buffers,
        compiler_params=pltpu.CompilerParams(vmem_limit_bytes=vmem * MIB),
        cost_estimate=estimate,
    )(*args, *after, *side_args, *pile)


def shape_at(entry):
    array, place = entry[:2]
    return jax.eval_shape(lambda x: x[place], array).shape if place else array.shape


def hold(arrays, after):
    count = len(arrays)

    def kernel(*refs):
        for source, target in zip(refs[:count], refs[count + len(after) :]):
            target[...] = source[...]
        token = refs[-1]
        token[...] = jnp.zeros_like(token)

    anywhere = pl.BlockSpec(memory_space=pl.ANY)
    return pl.pallas_call(
        kernel,
        out_shape=[struct(a.shape, a.dtype) for a in arrays] + [struct((8, 128), F32)],
        in_specs=[in_vmem()] * count + [anywhere] * len(after),
        out_specs=[in_vmem()] * (count + 1),
        compiler_params=pltpu.CompilerParams(vmem_limit_bytes=16 * MIB),
        cost_estimate=pl.CostEstimate(flops=0, bytes_accessed=0, transcendentals=0),
    )(*arrays, *after)


def swap(values, axis, bit):
    size = lax.axis_size(axis)
    return lax.ppermute(values, axis, [(i, i ^ bit) for i in range(size)])


def bits_of(axis):
    size = lax.axis_size(axis)
    return [1 << i for i in range(size.bit_length() - 1)]


def head_order(width):
    half = width // 2
    source = iota((width, width), 0)
    target = iota((width, width), 1)
    wanted = (target % half) // HALF * HD + target // half * HALF + target % HALF
    return (source == wanted).astype(BF16)


def same_head(lanes):
    return (iota((lanes, lanes), 0) // HALF == iota((lanes, lanes), 1) // HALF).astype(BF16)


def head_total(values, ones):
    high = values.astype(BF16)
    low = (values - high.astype(F32)).astype(BF16)
    return dot(high, ones) + dot(low, ones)


def rope_head(lanes):
    half = lanes // 2
    return iota((1, lanes), 1) % half // HALF


def value_head(lanes):
    return iota((1, lanes), 1) // HD


def project_kernel(first, xa, xb, wq, wk, wv, gain, cos, sin, *refs):
    fars, more = refs[:7], refs[7:10]
    qi_out, ki_out, cos_far, sin_far = fars[:4]
    width = wq.shape[1]
    half = width // 2
    ones = same_head(half)
    if first == 0:
        order = head_order(width)
        more[0][...] = dot(wq.get()[...], order).astype(BF16)
        more[1][...] = dot(wk.get()[...], order).astype(BF16)
        wq, wk = more[0], more[1]
        wv = wv.get()
        more[2][...] = wv[...]
    cos_far.buffer[...] = cos[first : first + 2]
    sin_far.buffer[...] = sin[first : first + 2]
    cos_far.send()
    sin_far.send()
    for index, source in enumerate((xa, xb)):
        rows = source.get()[...] if isinstance(source, Fetched) else source[...]
        c, s = cos[first + index], sin[first + index]
        for weights, unit_out, inverse_out in ((wq, fars[4], qi_out), (wk, fars[5], ki_out)):
            full = dot(rows, weights[...])
            a, b = full[:, :half], full[:, half:]
            inverse = lax.rsqrt(head_total(a * a + b * b, ones) + EPS)
            inverse_out.buffer[index] = inverse
            unit_out.buffer[index, :, :half] = ((a * c - b * s) * inverse * gain[:, :half]).astype(BF16)
            unit_out.buffer[index, :, half:] = ((b * c + a * s) * inverse * gain[:, half:]).astype(BF16)
            inverse_out.send(index)
            unit_out.send(index)
        fars[6].buffer[index] = dot(rows, wv[...]).astype(BF16)
        fars[6].send(index)
    if first > 0:
        for near, far in zip(more, fars[4:]):
            near[...] = far.buffer[...]


def project(first, xa, xb, wq, wk, wv, gain, cos, sin, **sides):
    rows, depth = xa.shape
    width = wq.shape[1]
    low = [struct((2, rows, width), BF16)] * 3
    outs = [struct((2, rows, width // 2), F32)] * 4 + low
    args = (xa, xb, wq, wk, wv, gain, cos, sin)
    early = first == 0
    outs = outs + ([struct((depth, width), BF16)] * 3 if early else low)
    by_row = [(0,), (1,)]
    return run_whole(
        functools.partial(project_kernel, first), outs, args, 2 * 2 * rows * depth * width * 3, vmem=24,
        far_in=(0, 2, 3, 4) if early else (), fetch={2: None, 3: None, 0: None, 4: None} if early else {},
        store={0: by_row, 1: by_row, 2: None, 3: None, 4: by_row, 5: by_row, 6: by_row}, **sides,
    )


def pair_mask(seg_query, seg_key, query_block, key_block, query_dim, rows):
    allowed = seg_query == seg_key
    if query_block == key_block:
        query_id = iota((rows, rows), query_dim)
        key_id = iota((rows, rows), 1 - query_dim)
        allowed = (allowed & (key_id <= query_id)) | (key_id == query_id)
    return allowed


def column(row):
    return jnp.broadcast_to(row, (8, row.shape[1])).T[:, :1]


def join_pairs(buffer, first, second):
    buffer[0:2] = first[...]
    buffer[2:4] = second[...]


def attend_kernel(
    heads, me, q01, q23, k01, k23, v01, v23, seg_col, seg_row, head_out, inv_out, give_out, q, k, v, kbuf, vbuf
):
    blocks, rows, width = kbuf.shape
    join_pairs(q, q01, q23)
    join_pairs(k, k01, k23)
    join_pairs(v, v01, v23)
    mine = me[0, 0]
    q_head = rope_head(width)
    v_head = value_head(width)
    for block in range(blocks):
        slot = jnp.bitwise_xor(mine, block)
        kbuf[block] = k[slot]
        vbuf[block] = v[slot]
    for block in range(blocks):
        slot = jnp.bitwise_xor(mine, block)
        queries = q[slot]
        seg_q = column(seg_col[slot])
        count = block + 1
        allowed = jnp.concatenate(
            [
                pair_mask(seg_q, seg_row[jnp.bitwise_xor(mine, other)], block, other, 0, rows)
                for other in range(count)
            ],
            axis=1,
        )
        keys = kbuf[0:count].reshape(count * rows, width)
        values = vbuf[0:count].reshape(count * rows, width)
        inverse = jnp.zeros((rows, width), F32)
        mixed = jnp.zeros((rows, width), F32)
        for h in range(heads):
            scores = dot_nt(jnp.where(q_head == h, queries, jnp.zeros_like(queries)), keys)
            weight = jnp.where(allowed, jnp.exp2(scores * EXP_SCALE), 0.0)
            total = jnp.sum(weight, axis=1, keepdims=True)
            inverse = jnp.where(v_head == h, 1.0 / total, inverse)
            mixed = jnp.where(v_head == h, dot(weight.astype(BF16), values), mixed)
        inv_out[slot] = inverse
        head_out[slot] = (mixed * inverse).astype(BF16)
    give_out[0] = head_out[1]
    give_out[1] = head_out[3]


def attend(me, q, k, v, seg_col, seg_row, after, **sides):
    _, rows, width = q[0].shape
    blocks = 4
    heads = width // HD
    outs = [
        struct((blocks, rows, width), BF16),
        struct((blocks, rows, width), F32),
        struct((2, rows, width), BF16),
    ]
    args = (me, *q, *k, *v, seg_col, seg_row)
    scratch = [pltpu.VMEM((blocks, rows, width), BF16)] * 5
    return run_whole(
        functools.partial(attend_kernel, heads), outs, args,
        10 * heads * 2 * 2 * rows * rows * width, scratch, vmem=24, smem=1, after=after, far_out=(1,), far_in=(1, 3, 5), **sides,
    )


def out_project_kernel(heads, got, w_out, w_core, own, far):
    far[...] = (dot(heads[2], w_out[...]) + dot(got[1], w_core[...])).astype(BF16)
    own[...] = dot(heads[0], w_out[...]) + dot(got[0], w_core[...])


def out_project(heads, got, w_out, w_core):
    _, rows, width = heads.shape
    depth = w_out.shape[1]
    outs = [struct((rows, depth), F32), struct((rows, depth), BF16)]
    return run_whole(
        out_project_kernel, outs, (heads, got, w_out, w_core), 2 * 4 * rows * width * depth, vmem=16,
    )


def head_back_kernel(near, far, w_out, w_core, mine, give):
    part, depth = near.shape
    for i, source in enumerate((near, far)):
        span = slice(i * part, (i + 1) * part)
        rows = source[...]
        mine[span] = dot_nt(rows, w_out[...]).astype(BF16)
        give[span, :depth] = rows
        give[span, depth:] = dot_nt(rows, w_core[...]).astype(BF16)


def head_back(near, far, w_out, w_core, after):
    part, depth = near.shape
    width = w_out.shape[0]
    outs = [struct((2 * part, width), BF16), struct((2 * part, depth + width), BF16)]
    return run_whole(
        head_back_kernel, outs, (near, far, w_out, w_core), 2 * 4 * part * width * depth, vmem=16, after=after,
    )


def attend_back_kernel(
    heads, me, mine0, mine1, got0, got1, q01, q23, k01, k23, v01, v23, head_out, inv, qi01, qi23, ki01, ki23,
    seg_col, seg_row, gain, cos01, cos23, sin01, sin23, joined, scale_out, q, k, v, qm, km, dm, row_dot, dq, dk, dv,
):
    blocks, rows, width = q.shape
    inv = inv.get()
    join_pairs(q, q01.get(), q23.get())
    join_pairs(k, k01.get(), k23.get())
    join_pairs(v, v01.get(), v23.get())
    half = width // 2
    part = rows // PARTS
    depth = got0.shape[1] - width
    self_id = me[0, 0]
    q_head = rope_head(width)
    v_head = value_head(width)
    picks = (iota((8, width), 0) == iota((8, width), 1) // HD).astype(BF16)
    for slot in range(blocks):
        for c in range(PARTS):
            span = slice(c * part, (c + 1) * part)
            at = slice(slot // 2 * part, (slot // 2 + 1) * part)
            grads = (mine0, mine1)[c][at] if slot % 2 == 0 else (got0, got1)[c][at, depth:]
            scaled = (grads.astype(F32) * inv[slot, span]).astype(BF16)
            product = scaled.astype(F32) * head_out[slot, span].astype(F32)
            high = product.astype(BF16)
            low = (product - high.astype(F32)).astype(BF16)
            dots = dot_nt(picks, high) + dot_nt(picks, low)
            for h in range(heads):
                start = h * rows + c * part
                dm[slot, start : start + part] = jnp.where(v_head == h, scaled, jnp.zeros_like(scaled))
                row_dot[slot, :, start : start + part] = dots[h : h + 1]
        queries, keys = q[slot], k[slot]
        for h in range(heads):
            at = slice(h * rows, (h + 1) * rows)
            qm[slot, at] = jnp.where(q_head == h, queries, jnp.zeros_like(queries))
            km[slot, at] = jnp.where(q_head == h, keys, jnp.zeros_like(keys))
    for block in range(blocks):
        slot = jnp.bitwise_xor(self_id, block)
        for other in range(block + 1):
            there = jnp.bitwise_xor(self_id, other)
            allowed = pair_mask(seg_row[slot], column(seg_col[there]), block, other, 1, rows)
            allowed = jnp.concatenate([allowed] * heads, axis=1)
            scores = dot_nt(k[there], qm[slot])
            weight = jnp.where(allowed, jnp.exp2(scores * EXP_SCALE), 0.0)
            grad = (weight * (dot_nt(v[there], dm[slot]) - row_dot[slot])).astype(BF16)
            d_value = dot(weight.astype(BF16), dm[slot])
            d_key = dot(grad, qm[slot])
            stacked = jnp.concatenate([grad[:, h * rows : (h + 1) * rows] for h in range(heads)], axis=0)
            d_query = dot_tn(stacked, km[there])
            if other == block:
                dv[there] = d_value
                dk[there] = d_key
            else:
                dv[there] += d_value
                dk[there] += d_key
            if other == 0:
                dq[slot] = d_query
            else:
                dq[slot] += d_query
    order = head_order(width)
    ones = same_head(half)
    scale_sum = jnp.zeros((1, width), F32)
    for slot in range(blocks):
        c, s = [pair[slot // 2].get()[slot % 2] for pair in ((cos01, cos23), (sin01, sin23))]
        for place, (grad_ref, unit_ref, inv_ref) in enumerate(
            ((dq, q, (qi01, qi23)), (dk, k, (ki01, ki23)))
        ):
            inverse = inv_ref[slot // 2].get()[slot % 2]
            grads = grad_ref[slot] * SCORE_ROOT
            normed = unit_ref[slot].astype(F32) / gain[...]
            scale_sum = scale_sum + jnp.sum(normed * grads, axis=0, keepdims=True)
            grads = grads * gain[...]
            product = normed * grads
            along = head_total(product[:, :half] + product[:, half:], ones)
            a = (grads[:, :half] - normed[:, :half] * along) * inverse
            b = (grads[:, half:] - normed[:, half:] * along) * inverse
            turned = jnp.concatenate([(a * c + b * s).astype(BF16), (b * c - a * s).astype(BF16)], axis=1)
            joined[slot, :, place * width : (place + 1) * width] = dot_nt(turned, order).astype(BF16)
        joined[slot, :, 2 * width : 3 * width] = dv[slot].astype(BF16)
    scale_out[...] = jnp.zeros_like(scale_out)
    for h in range(heads):
        for side in range(2):
            at = side * half + h * HALF
            scale_out[2 * h + side : 2 * h + side + 1, :HALF] = scale_sum[:, at : at + HALF]


def attend_back(me, mine, got, q, k, v, head_out, inv, qi, ki, seg_col, seg_row, gain, cos, sin, **sides):
    blocks = 4
    _, rows, width = q[0].shape
    heads = width // HD
    outs = [struct((blocks, rows, 3 * width), BF16), struct((2 * heads, 128), F32)]
    args = (me, *mine, *got, *q, *k, *v, head_out, inv, *qi, *ki, seg_col, seg_row, gain, *cos, *sin)
    scratch = (
        [pltpu.VMEM((blocks, rows, width), BF16)] * 3
        + [pltpu.VMEM((blocks, heads * rows, width), BF16)] * 3
        + [pltpu.VMEM((blocks, 1, heads * rows), F32)]
        + [pltpu.VMEM((blocks, rows, width), F32)] * 3
    )
    return run_whole(
        functools.partial(attend_back_kernel, heads), outs, args,
        10 * heads * 5 * 2 * rows * rows * width, scratch, vmem=40, smem=1,
        fetch={i: None for i in (12, 5, 6, 7, 8, 9, 10, 13, 14, 15, 16, 20, 21, 22, 23)},
        far_in=(5, 6, 7, 8, 9, 10, 12, 13, 14, 15, 16, 20, 21, 22, 23), **sides,
    )


def input_grad_kernel(joined, wq, wk, wv, give_far, far, give, own):
    width = wq.shape[1]

    def rows_of(slot):
        out = dot_nt(joined[slot, :, :width], wq[...])
        out += dot_nt(joined[slot, :, width : 2 * width], wk[...])
        return out + dot_nt(joined[slot, :, 2 * width :], wv[...])

    give_far[...] = rows_of(3).astype(BF16)
    far[...] = rows_of(2)
    give[...] = rows_of(1).astype(BF16)
    own[...] = rows_of(0)


def input_grad(joined, wq, wk, wv, after, far_after):
    rows = joined.shape[1]
    depth, width = wq.shape
    outs = [struct((rows, depth), BF16), struct((rows, depth), F32)] * 2
    return run_whole(
        input_grad_kernel, outs, (joined, wq, wk, wv), 2 * 4 * rows * depth * width * 3, vmem=24, after=after, far_after=far_after, far_in=(1, 2, 3),
    )


def add_far_kernel(far, got, sum_out):
    sum_out[...] = (far[...] + got[...].astype(F32)).astype(BF16)


def add_far(far, got, after):
    return run_whole(add_far_kernel, [struct(far.shape, BF16)], (far, got), far.size, vmem=16, after=after)[0]


def unit_rows(values):
    inverse = lax.rsqrt(jnp.sum(values * values, axis=-1, keepdims=True) + EPS)
    return values * inverse, inverse


def unit_back(grad_in, normed, inverse):
    return (grad_in - normed * jnp.sum(normed * grad_in, axis=-1, keepdims=True)) * inverse


def mix_attn_kernel(c, own, far, tokens, rate, *refs):
    part = refs[-3].shape[0]
    span = slice(c * part, (c + 1) * part)
    total = own[span] + far[span].astype(F32)
    h_attn, _ = unit_rows(total)
    residual = tokens[span].astype(F32)
    h_one, _ = unit_rows(residual + rate[...] * (h_attn - residual))
    low = h_one.astype(BF16)
    low_out, sum_out, both_out = refs[-3:]
    low_out[...] = low
    if c > 0:
        sum_out[: c * part] = refs[0][...]
        both_out[: c * part] = refs[1][...]
        sum_out[span] = total.astype(BF16)
        both_out[span] = low
    else:
        sum_out[...] = total.astype(BF16)
        both_out[...] = jnp.zeros_like(both_out)


def mix_mlp_kernel(c, own, far, h_one, rate, cotangent, *refs):
    out, low_out, mix_out, rate_out, both_out = refs[-5:]
    part = far.shape[0]
    total = own[...] + far[...].astype(F32)
    h_mlp, mlp_inverse = unit_rows(total)
    first = h_one[...].astype(F32)
    away = h_mlp - first
    block_out, out_inverse = unit_rows(first + rate[...] * away)
    (out if c > 0 else out.buffer)[...] = block_out
    d_mix = unit_back(cotangent[...].astype(F32), block_out, out_inverse)
    (mix_out if c > 0 else mix_out.buffer)[...] = d_mix.astype(BF16)
    if c == 0:
        out.send()
        mix_out.send()
    rate_out[...] = jnp.sum(d_mix * away, axis=0, keepdims=True)
    low = unit_back(rate[...] * d_mix, h_mlp, mlp_inverse).astype(BF16)
    low_out[...] = low
    if c > 0:
        both_out[: c * part] = refs[0][...]
        both_out[c * part :] = low
    else:
        both_out[...] = jnp.zeros_like(both_out)


def mix_back_kernel(own, far, d_mix_two, attn_sum, h_one, tokens, rate, mlp_rate, low_out, rest_out, rate_out):
    h_attn, attn_inverse = unit_rows(attn_sum[...].astype(F32))
    residual = tokens[...].astype(F32)
    away = h_attn - residual
    _, one_inverse = unit_rows(residual + rate[...] * away)
    d_one = own[...] + far[...].astype(F32)
    d_one = d_one + (1.0 - mlp_rate[...]) * d_mix_two[...].astype(F32)
    d_mix = unit_back(d_one, h_one[...].astype(F32), one_inverse)
    rest_out[...] = (1.0 - rate[...]) * d_mix
    rate_out[...] = jnp.sum(d_mix * away, axis=0, keepdims=True)
    low_out[...] = unit_back(rate[...] * d_mix, h_attn, attn_inverse).astype(BF16)


def silu_parts(gate):
    sig = 0.5 * jnp.tanh(0.5 * gate) + 0.5
    return sig, gate * sig


def load_weights(arrays, kept, after, **sides):
    count = len(arrays)

    def kernel(*refs):
        sources, rest = refs[: count + len(kept)], refs[count + len(kept) :]
        target, kept_here, semaphores = rest[0], rest[1:-1], rest[-1]
        copies = []
        for n, source in enumerate(sources):
            to = target.at[n] if n < count else kept_here[n - count]
            copies.append(pltpu.make_async_copy(source, to, semaphores.at[n]))
        for copy in copies:
            copy.start()
        for copy in copies:
            copy.wait()

    args = (*arrays, *kept)
    every = tuple(range(len(args)))
    outs = [struct((count,) + arrays[0].shape, BF16)] + [struct(k.shape, BF16) for k in kept]
    return run_whole(
        kernel, outs, args, 0, [pltpu.SemaphoreType.DMA((len(args),))],
        vmem=20, after=after, raw=every, far_in=every, **sides,
    )


def column_tiles(width, tile=512):
    return [(slice(None), slice(start, start + tile)) for start in range(0, width, tile)]


def feed_kernel(near, far, weights, scales, kept_out, hid_out, give, own, sent, rows):
    kept, hid = kept_out.buffer, hid_out.buffer
    part, depth = near.shape
    tile = 512
    width = hid.shape[1]
    rows[:part] = near[...]
    rows[part:] = far[...]
    for i in range(2):
        for n, start in enumerate(range(0, width, tile)):
            span = slice(start, start + tile)
            up = dot(rows[...], weights[3 * i, :, span])
            gate = dot(rows[...], weights[3 * i + 1, :, span])
            kept[i, :, span] = up.astype(BF16)
            kept[2 + i, :, span] = gate.astype(BF16)
            kept_out.send(2 * i + n, 4 + 2 * i + n)
            _, active = silu_parts(scales[2 * i + 1 : 2 * i + 2, span] * gate)
            hidden = (scales[2 * i : 2 * i + 1, span] * up * active).astype(BF16)
            if i == 0:
                hid[:, span] = hidden
                hid_out.send(n)
            else:
                give[:, span] = hidden
    total = dot(hid[...], weights[2]) + dot(give[...], weights[5])
    own[...] = total[:part]
    sent[...] = total[part:].astype(BF16)


def feed(near, far, weights, scales, after, **sides):
    part, depth = near.shape
    rows = 2 * part
    width = weights.shape[2]
    outs = [
        struct((4, rows, width), BF16), struct((rows, width), BF16),
        struct((rows, width), BF16), struct((part, depth), F32), struct((part, depth), BF16),
    ]
    tiles = column_tiles(width)
    return run_whole(
        feed_kernel, outs, (near, far, weights, scales), 12 * rows * depth * width,
        scratch=[pltpu.VMEM((rows, depth), BF16)], vmem=FEED_VMEM, after=after,
        store={0: [(i, *tile) for i in range(4) for tile in tiles], 1: tiles}, **sides,
    )


def feed_back_kernel(near, far, weights, scales, kept, d_up_out, d_gate_out, sums_out, give, own, sent, rows):
    d_up_all, d_gate_all = d_up_out.buffer, d_gate_out.buffer
    part, depth = near.shape
    tile = 512
    width = d_up_all.shape[1]
    rows[:part] = near[...]
    rows[part:] = far[...]
    for i in range(2):
        for n, start in enumerate(range(0, width, tile)):
            span = slice(start, start + tile)
            at = slice(i * width + start, i * width + start + tile)
            d_hidden = dot_nt(rows[...], weights[3 * i + 2, span])
            up_scale = scales[2 * i : 2 * i + 1, span]
            gate_scale = scales[2 * i + 1 : 2 * i + 2, span]
            up = kept[i, :, span].astype(F32)
            gate = kept[2 + i, :, span].astype(F32)
            scaled = gate_scale * gate
            sig, active = silu_parts(scaled)
            d_up_scaled = d_hidden * active
            d_gate_scaled = d_hidden * (up_scale * up) * (sig + active * (1.0 - sig))
            d_up = (d_up_scaled * up_scale).astype(BF16)
            d_gate = (d_gate_scaled * gate_scale).astype(BF16)
            sums_out[0:1, at] = jnp.sum(d_up_scaled * up, axis=0, keepdims=True)
            sums_out[1:2, at] = jnp.sum(d_gate_scaled * gate, axis=0, keepdims=True)
            if i == 0:
                d_up_all[:, span] = d_up
                d_gate_all[:, span] = d_gate
                d_up_out.send(n)
                d_gate_out.send(n)
            else:
                give[0, :, span] = d_up
                give[1, :, span] = d_gate
    total = dot_nt(d_up_all[...], weights[0]) + dot_nt(d_gate_all[...], weights[1])
    total += dot_nt(give[0], weights[3]) + dot_nt(give[1], weights[4])
    own[...] = total[:part]
    sent[...] = total[part:].astype(BF16)


def feed_back(near, far, weights, scales, kept, after, **sides):
    part, depth = near.shape
    rows = 2 * part
    width = weights.shape[2]
    outs = [
        struct((rows, width), BF16), struct((rows, width), BF16), struct((2, 2 * width), F32),
        struct((2, rows, depth), BF16), struct((part, depth), F32), struct((part, depth), BF16),
    ]
    tiles = column_tiles(width)
    return run_whole(
        feed_back_kernel, outs, (near, far, weights, scales, kept), 12 * rows * depth * width,
        scratch=[pltpu.VMEM((rows, depth), BF16)], vmem=FEED_VMEM, after=after, store={0: tiles, 1: tiles}, **sides,
    )


def view(ref, place):
    return ref.at[place] if place else ref


def piece_place(piece, bits):
    flags = [piece // bit % 2 for bit in bits]
    return flags[0], flags[1] + 2 * flags[2]


def weight_kernel(groups, orders, vectors, me, *refs):
    n_in = sum(len(left) + len(right) for left, right in groups) + vectors
    inputs = list(refs[:n_in])
    results = refs[n_in : n_in + 2 * len(orders)]
    targets = [r.buffer if isinstance(r, Stored) else r for r in results]
    turned = refs[-1]
    piece = 128
    count, half = turned.shape[0] // piece, turned.shape[0] // 2
    mine = me[0, 0]
    pieces = sorted(range(count), key=lambda j: (1 - piece_place(j, orders[0][0])[0], piece_place(j, orders[0][0])[1]))
    if vectors:
        lines = [inputs.pop(0) for _ in range(vectors)]
        for j in pieces:
            sent, position = piece_place(j, orders[0][0])
            target = targets[1 - sent]
            rows, width = target.shape[1] - piece, target.shape[2]
            owner = jnp.bitwise_xor(mine, j)
            row = iota((rows, width), 0)
            block = jnp.zeros((rows, width), F32)
            for n, line in enumerate(lines):
                values = line[pl.ds(owner, 1), :]
                if values.shape[1] < width:
                    values = jnp.concatenate([values, jnp.zeros((1, width - values.shape[1]), F32)], axis=1)
                block = jnp.where(row == n, values, block)
            target[position, piece:] = block.astype(BF16)
    base = 0
    for left_places, right_places in groups:
        left = [(inputs.pop(0), place) for place in left_places]
        right = [(inputs.pop(0), place) for place in right_places]
        start = 0
        for source, place in left:
            ref = view(source.get(), place)
            for n, j in enumerate(pieces):
                at = jnp.bitwise_xor(mine, j) * piece
                columns = ref[:, pl.ds(pl.multiple_of(at, piece), piece)]
                turned[n * piece : (n + 1) * piece, start : start + ref.shape[0]] = columns.T
            start += ref.shape[0]
        for side in range(2):
            start = 0
            product = None
            for source, place in right:
                ref = view(source.get(), place)
                rows = ref.shape[0]
                part = dot(turned[side * half : (side + 1) * half, start : start + rows], ref[...])
                product = part if product is None else product + part
                start += rows
            product = product.astype(BF16)
            width = product.shape[1]
            begin = 0
            for n, (bits, columns) in enumerate(orders):
                first, last = max(base, begin), min(base + width, begin + columns)
                if first < last:
                    for i, j in enumerate(pieces[side * count // 2 : (side + 1) * count // 2]):
                        sent, position = piece_place(j, bits)
                        targets[2 * n + 1 - sent][position, :piece, first - begin : last - begin] = product[
                            i * piece : (i + 1) * piece, first - base : last - base
                        ]
                begin += columns
            if side == 1 and len(orders) == 1 and len(groups) == 1 and isinstance(results[1], Stored):
                results[1].send()
            if side == 0 and len(orders) == 1 and len(groups) == 1 and isinstance(results[0], Stored):
                results[0].send()
        base += width


def weight_halves(me, groups, n_groups, orders, after=(), far_after=(), vectors=(), far_kept=True, far_sent=False, **sides):
    depth = shape_at(groups[0][0][0])[1]
    rows = sum(shape_at(entry)[0] for entry in groups[0][0])
    piece = depth // n_groups
    outs = [
        struct((n_groups // 2, piece + (VECTOR_ROWS if vectors and n == 0 else 0), columns), BF16)
        for n, (_, columns) in enumerate(orders) for _ in range(2)
    ]
    entries = [entry for left, right in groups for entry in (*left, *right)]
    args = (me, *vectors, *[a for a, _, _ in entries])
    places = [([p for _, p, _ in left], [p for _, p, _ in right]) for left, right in groups]
    total = sum(columns for _, columns in orders)
    skip = 1 + len(vectors)
    results = run_whole(
        functools.partial(weight_kernel, places, orders, len(vectors)), outs, args, 2 * rows * depth * total,
        [pltpu.VMEM((depth, rows), BF16)], vmem=24, smem=1, after=after,
        fetch={skip + i: [p] if p else None for i, (_, p, _) in enumerate(entries)},
        far_in=tuple(skip + i for i, (_, _, far) in enumerate(entries) if far), far_after=far_after,
        store={i: None for i in range(len(outs)) if (far_kept if i % 2 else far_sent)}, **sides,
    )
    return [*[results[2 * n : 2 * n + 2] for n in range(len(orders))], *results[len(outs) :]]


def merge_kernel(kept, got, *outs):
    for i in range(kept.shape[0] // 2):
        outs[0][i] = (kept[2 * i + 1].astype(F32) + got[2 * i + 1].astype(F32)).astype(BF16)
        outs[1][i] = (kept[2 * i].astype(F32) + got[2 * i].astype(F32)).astype(BF16)


def merge(kept, got, after=()):
    count, rows, columns = kept.shape
    outs = [struct((count // 2, rows, columns), BF16)] * 2
    return run_whole(merge_kernel, outs, (kept, got), kept.size, vmem=16, after=after)


def finish(kept, got, parts, after=()):
    def kernel(kept_ref, got_ref, *outs):
        total = kept_ref[0].astype(F32) + got_ref[0].astype(F32)
        for (row, rows, column, columns, turned), out in zip(parts, outs):
            piece = total[row : row + rows, column : column + columns]
            out[...] = piece.T if turned else piece

    outs = [struct((c, r) if turned else (r, c), F32) for _, r, _, c, turned in parts]
    return run_whole(
        kernel, outs, (kept, got), kept.size, vmem=16, after=after, far_out=tuple(range(len(outs)))
    )


def block_of(entry):
    array, place, _ = entry
    return array[place] if place else array


def weight_halves_plain(me, groups, n_groups, orders, after=(), far_after=(), vectors=(), far_kept=True, far_sent=False, load=(), save=(), carry=(), pile=()
):
    products = [
        dot_tn(jnp.concatenate([block_of(e) for e in left], axis=0), jnp.concatenate([block_of(e) for e in right], axis=0))
        for left, right in groups
    ]
    product = jnp.concatenate(products, axis=1)
    parts = product.reshape(n_groups, product.shape[0] // n_groups, product.shape[1])
    order = jnp.bitwise_xor(me[0, 0], jnp.arange(n_groups, dtype=jnp.int32))
    parts = parts[order]
    results, start = [], 0
    for n, (_, columns) in enumerate(orders):
        chosen = parts[:, :, start : start + columns]
        if vectors and n == 0:
            lines = [jnp.pad(v[order], ((0, 0), (0, columns - v.shape[1])))[:, None] for v in vectors]
            chosen = jnp.concatenate([chosen, *lines], axis=1)
            chosen = jnp.pad(chosen, ((0, 0), (0, VECTOR_ROWS - len(lines)), (0, 0)))
        chosen = chosen.reshape((n_groups // 2, 2) + chosen.shape[1:]).astype(BF16)
        results.append((chosen[:, 1], chosen[:, 0]))
        start += columns
    loaded = [array[place] if place else array for array, place in load]
    return [*results, *loaded, *save, *carry, *([jnp.concatenate(pile)] if pile else [])]


def add(pair, after=()):
    kept, got = pair
    if kept.shape[1] >= 128:
        return merge(kept, got, after)
    total = kept.astype(F32) + got.astype(F32)
    parts = total.reshape((kept.shape[0] // 2, 2) + kept.shape[1:]).astype(BF16)
    return parts[:, 1], parts[:, 0]


def stage(pair, bit, after=()):
    sent, kept = add(pair, after)
    return kept, swap(sent, "dp", bit)


def combine_kernel(*refs):
    pairs, (sent, kept) = refs[:-2], refs[-2:]
    start = 0
    for a, b in zip(pairs[::2], pairs[1::2]):
        rows, columns = a.shape[1:]
        span = slice(start, start + columns)
        for piece, target in ((1, sent), (0, kept)):
            target[0, :rows, span] = (a[piece].astype(F32) + b[piece].astype(F32)).astype(BF16)
            if rows < target.shape[1]:
                target[0, rows:, span] = jnp.zeros((target.shape[1] - rows, columns), BF16)
        start += columns


def combine(pairs, after=()):
    count = pairs[0][0].shape[0]
    rows = max(kept.shape[1] for kept, _ in pairs)
    if count == 2 and rows >= 128:
        out = struct((1, rows, sum(kept.shape[2] for kept, _ in pairs)), BF16)
        return run_whole(combine_kernel, [out, out], [x for pair in pairs for x in pair], 0, vmem=16, after=after)
    totals = [kept.astype(F32) + got.astype(F32) for kept, got in pairs]
    total = jnp.concatenate([jnp.pad(t, ((0, 0), (0, rows - t.shape[1]), (0, 0))) for t in totals], axis=2)
    parts = total.reshape((count // 2, 2) + total.shape[1:]).astype(BF16)
    return parts[:, 1], parts[:, 0]


def last_stage(pair, bits, parts, after=()):
    for bit in bits:
        pair = stage(pair, bit)
    kept, got = pair
    if kept.shape[1] >= 128:
        return finish(kept, got, parts, after)
    total = (kept.astype(F32) + got.astype(F32))[0]
    pieces = [total[r : r + rows, c : c + columns] for r, rows, c, columns, _ in parts]
    return [piece.T if part[-1] else piece for piece, part in zip(pieces, parts)]


def shards(
    tokens,
    seq_lengths,
    w_query,
    w_key,
    w_value,
    w_out,
    qk_scale,
    attn_rate,
    w_up,
    w_gate,
    up_scale,
    gate_scale,
    w_down,
    mlp_rate,
    out_grad,
):
    local_rows, depth = tokens.shape
    n_mp = lax.axis_size("mp")
    n_dp = lax.axis_size("dp")
    assert n_mp == 4
    width = w_query.shape[1]
    hidden_width = w_up.shape[1]
    heads = width // HD
    part = local_rows // PARTS
    me = lax.axis_index("mp").astype(jnp.int32)
    me_ref = me.reshape(1, 1)
    group = lax.axis_index("dp").astype(jnp.int32)
    group_ref = group.reshape(1, 1)
    dp_bits = bits_of("dp")
    seq_count = seq_lengths.shape[1]

    far_tokens = swap(tokens, "mp", 2)
    core_tokens = swap(tokens, "mp", 1)
    ends = jnp.cumsum(seq_lengths[0])
    starts = jnp.concatenate([jnp.zeros((1,), jnp.int32), ends])
    owner = jnp.bitwise_xor(me, jnp.arange(n_mp, dtype=jnp.int32))
    row_ids = owner[:, None] * local_rows + jnp.arange(local_rows, dtype=jnp.int32)[None]
    segment = jnp.sum((row_ids[:, :, None] >= ends).astype(jnp.int32), axis=2)
    first = jnp.sum(
        jnp.where(segment[:, :, None] == jnp.arange(seq_count + 1, dtype=jnp.int32), starts, 0), axis=2
    )
    position = (row_ids - first).astype(F32)
    frequency = jnp.exp(jnp.arange(HALF, dtype=F32) * (-2.0 * math.log(10000.0) / HD))
    angles = position[:, :, None] * jnp.tile(frequency, heads)[None, None]
    cos, sin = jnp.cos(angles), jnp.sin(angles)
    seg_q = jnp.where(segment < seq_count, segment, -1).astype(F32)[:, None, :]
    seg_k = jnp.where(segment < seq_count, segment, -2).astype(F32)[:, None, :]
    gain = qk_scale.reshape(heads, 2, HALF).transpose(1, 0, 2).reshape(1, width)

    scale_rows = jnp.stack([up_scale, gate_scale * math.sqrt(depth)])
    core_out = swap(w_out, "mp", 1)
    core_rows = swap(scale_rows, "mp", 1)
    core_up = swap(w_up, "mp", 1)
    core_gate = swap(w_gate, "mp", 1)
    core_down = swap(w_down, "mp", 1)
    scales = jnp.concatenate([scale_rows, core_rows], axis=0)

    weights = (w_query, w_key, w_value)
    early = project(0, tokens, core_tokens, *weights, gain, cos, sin, save=[core_tokens])
    far_tokens, _ = hold([far_tokens], (early[9],))
    cross_tokens = swap(far_tokens, "mp", 1)
    late = project(
        2, far_tokens, cross_tokens, *early[7:10], gain, cos, sin, save=[far_tokens, cross_tokens]
    )
    core_tokens, far_tokens, cross_tokens = early[10], late[10], late[11]
    qi, ki, cos_far, sin_far, q_far, k_far, v_far = zip(early[:7], late[:7])
    q, k, v = zip(early[4:7], late[7:10])
    head_out, inv, give, out_here = attend(
        me_ref, q, k, v, seg_q, seg_k, (core_up, core_gate, core_down, core_out, core_rows), load=[(w_out, ())]
    )
    attn_own, attn_far = out_project(head_out, swap(give, "mp", 1), out_here, core_out)
    feed_parts = [w_up, w_gate, w_down, core_up, core_gate, core_down]
    feed_weights, tokens_here = load_weights(feed_parts, (), (attn_own,), load=[(tokens, ())])
    attn_far = swap(attn_far, "mp", 2)

    attn_row = attn_rate.reshape(1, depth)
    mlp_row = mlp_rate.reshape(1, depth)
    full, lowered, vector = struct((part, depth), F32), struct((part, depth), BF16), struct((1, depth), F32)
    both = struct((2 * part, depth), BF16)

    def part_of(c):
        return (slice(c * part, (c + 1) * part),)

    def mix_attn(c, after, *before):
        outs = [lowered, both, both] if c else [lowered, lowered, struct((8, 128), BF16)]
        return run_whole(
            functools.partial(mix_attn_kernel, c), outs, (attn_own, attn_far, tokens_here, attn_row, *before),
            20 * part * depth, vmem=16, after=after,
        )

    def mix_mlp(c, own, far, h_one, cotangent, after, *before):
        return run_whole(
            functools.partial(mix_mlp_kernel, c),
            [full, lowered, lowered, vector, both if c else struct((8, 128), BF16)],
            (own, far, h_one, mlp_row, cotangent, *before), LATER if c else 0, vmem=16, after=after,
            store={} if c else {0: None, 2: None},
        )

    def mix_back(own, far, d_mix, attn_sum, h_one, rows, after, flops=0):
        return run_whole(
            mix_back_kernel, [lowered, full, vector],
            (own, far, d_mix, attn_sum, h_one, rows, attn_row, mlp_row), flops, vmem=16, after=after,
        )

    fast = depth // n_dp == 128 and len(dp_bits) == 3
    later_bits = [dp_bits[1], dp_bits[0], dp_bits[2]] if fast else dp_bits

    def weight_grad(groups, orders, after=(), far_after=(), vectors=(), **sides):
        run = weight_halves if fast else weight_halves_plain
        return run(group_ref, groups, n_dp, orders, after, far_after, vectors, **sides)

    def whole(array, far=False):
        return (array, (), far)

    def layer(array, i, far=False):
        return (array, (i,), far)

    def rows_of(array, c, far=False):
        return (array, (slice(c * part, (c + 1) * part),), far)

    def over_dp(array, bit):
        return swap(array, "dp", bit)

    def cross(array):
        return swap(array, "mp", 2)

    def core(array):
        return swap(array, "mp", 1)

    near_a, sum_a, _ = mix_attn(0, (feed_weights,))
    far_a = cross(near_a)
    near_b, sums, near_rows = mix_attn(1, (near_a,), sum_a, near_a)

    near_b, token = hold([near_b], (far_a,))
    far_b = cross(near_b)
    core_near = core(near_rows)
    core_far_a = core(far_a)
    kept_a, hid_a, give_a, own_a, sent, sums, near_rows = feed(
        near_a, far_a, feed_weights, scales, (token,), save=[sums, near_rows]
    )
    core_hid_a = core(give_a)

    sent, token = hold([sent], (far_b,))
    got = cross(sent)
    core_far_b = core(far_b)
    kept_b, hid_b, give_b, own_b, sent, cotangent = feed(
        near_b, far_b, feed_weights, scales, (token,), load=[(out_grad, part_of(0))]
    )
    core_hid_b = core(give_b)

    sent, token = hold([sent], (got, core_near, core_far_a, core_far_b))
    got_b = cross(sent)
    out_a, d_near_a, d_mix_a, rate_a, _ = mix_mlp(0, own_a, got, near_a, cotangent, (token,))
    d_far_a = cross(d_near_a)
    back_weights, kept_a, kept_b, cotangent, own_b = load_weights(
        feed_parts, (kept_a, kept_b), (d_near_a,),
        load=[(out_grad, part_of(1))], carry=[own_b],
    )

    out_b, d_near_b, d_mix_b, rate_b, d_near_rows = mix_mlp(
        1, own_b, got_b, near_b, cotangent, (core_hid_a,), d_near_a
    )
    d_far_b = cross(d_near_b)
    core_d_near = core(d_near_rows)
    core_d_far_a = core(d_far_a)
    d_up_a, d_gate_a, sums_a, give_a, own_a, sent, d_mix_b, d_near_rows, block_out = feed_back(
        d_near_a, d_far_a, back_weights, scales, kept_a, (d_near_b,),
        save=[d_mix_b, d_near_rows], pile=[out_a, out_b],
    )

    sent, give_a, token = hold([sent, give_a], (d_far_b, core_hid_b))
    got_a = cross(sent)
    core_give_a = core(give_a)
    core_d_far_b = core(d_far_b)
    d_up_b, d_gate_b, sums_b, give_b, own_b, sent = feed_back(
        d_near_b, d_far_b, back_weights, scales, kept_b, (token,)
    )
    down_a, down_b, d_mix_a, sum_a, rows_a, h_one_a, own_a = weight_grad(
        [(
            [rows_of(d_near_rows, 0, True), whole(d_far_a), rows_of(d_near_rows, 1, True), whole(d_far_b),
             rows_of(core_d_near, 0), whole(core_d_far_a, True), rows_of(core_d_near, 1), whole(core_d_far_b, True)],
            [whole(hid_a, True), whole(hid_b, True), whole(core_hid_a), whole(core_hid_b)],
        )],
        [(dp_bits, hidden_width // 2), (later_bits, hidden_width // 2)], (sums_b,), far_kept=False,
        load=[(d_mix_a, ()), (sums, part_of(0)), (tokens, part_of(0)), (near_rows, part_of(0))], carry=[own_a],
    )

    sent, give_b, sent_a, sent_b, token = hold([sent, give_b, down_a[0], down_b[0]], (got_a,))
    got_b = cross(sent)
    core_give_b = core(give_b)
    down_a = (down_a[1], over_dp(sent_a, dp_bits[0]))
    down_b = (down_b[1], over_dp(sent_b, later_bits[0]))
    a_near_a, rest_a, attn_rate_a = mix_back(own_a, got_a, d_mix_a, sum_a, h_one_a, rows_a, (token,))
    a_far_a = cross(a_near_a)
    rows_in = [
        rows_of(near_rows, 0, True), whole(far_a), rows_of(near_rows, 1, True), whole(far_b),
        rows_of(core_near, 0, True), whole(core_far_a, True), rows_of(core_near, 1, True), whole(core_far_b, True),
    ]
    grad_up, d_mix_b, sum_b, rows_b, h_one_b, out_here, rest_a, own_b = weight_grad(
        [(rows_in, [whole(d_up_a, True), whole(d_up_b, True), layer(core_give_a, 0), layer(core_give_b, 0)])],
        [(dp_bits, hidden_width)], (a_near_a,), far_sent=True,
        load=[(d_mix_b, ()), (sums, part_of(1)), (tokens, part_of(1)), (near_rows, part_of(1)), (w_out, ())],
        save=[rest_a], carry=[own_b],
    )

    a_near_b, rest_b, attn_rate_b = mix_back(own_b, got_b, d_mix_b, sum_b, h_one_b, rows_b, (), LATER)
    a_far_b = cross(a_near_b)
    sent_a, kept_a = add(down_a, (a_near_b,))
    sent_b, kept_b = add(down_b, (sent_a,))
    sent_a, sent_b, token = hold([sent_a, sent_b], ())
    down_a = (kept_a, over_dp(sent_a, dp_bits[1]))
    down_b = (kept_b, over_dp(sent_b, later_bits[1]))

    def pack_kernel(part_a, part_b, rate_a, rate_b, rate_c, rate_d, own_ref, core_ref):
        total = part_a[...] + part_b[...]
        own_ref[0:2] = total[:, :hidden_width]
        own_ref[2:3] = rate_a[...] + rate_b[...]
        own_ref[3:4] = rate_c[...] + rate_d[...]
        core_ref[0:2] = total[:, hidden_width:]
        core_ref[2:4] = own_ref[2:4]

    def pair_kernel(own_ref, got_ref, sum_ref, rate_ref):
        sum_ref[...] = own_ref[...] + got_ref[...]
        rate_ref[...] = own_ref[2:4] + got_ref[2:4]

    size = depth // n_dp

    def table_kernel(sum_ref, got_ref, scale_ref, rate_ref):
        rates = sum_ref[2:4] + got_ref[...]
        for target, lines in (
            (scale_ref, [sum_ref[0:1], sum_ref[1:2] * math.sqrt(depth)]),
            (rate_ref, [rates[0:1], rates[1:2]]),
        ):
            for n, line in enumerate(lines):
                for p in range(n_dp):
                    target[p : p + 1, n * size : (n + 1) * size] = line[:, p * size : (p + 1) * size]

    four = struct((4, depth), F32)
    assert hidden_width == depth
    own_sums, core_sums = run_whole(
        pack_kernel, [four, four], (sums_a, sums_b, attn_rate_a, attn_rate_b, rate_a, rate_b), 0, vmem=8,
        after=(token,),
    )
    core_sums = core(core_sums)
    grad_gate, up_sent, rests = weight_grad(
        [(rows_in, [whole(d_gate_a, True), whole(d_gate_b, True), layer(core_give_a, 1), layer(core_give_b, 1)])],
        [(later_bits, hidden_width)], (own_sums,), pile=[rest_a, rest_b], load=[(grad_up[0], ())],
    )

    down_sent, down_kept = combine([down_a, down_b], (grad_gate[0],))
    down_sent, up_sent, gate_sent, token = hold([down_sent, up_sent, grad_gate[0]], (a_far_b, a_far_a))
    down = (down_kept, over_dp(down_sent, dp_bits[2]))
    up_got = over_dp(up_sent, dp_bits[0])
    gate_got = over_dp(gate_sent, later_bits[0])
    head_a = head_back(a_near_a, a_far_a, out_here, core_out, (token,))
    head_give = head_a[1]
    core_head_a = core(head_give)
    head_b = head_back(a_near_b, a_far_b, out_here, core_out, (head_a[0],))
    core_head_b = core(head_b[1])
    pair_sums, rates = run_whole(
        pair_kernel, [four, struct((2, depth), F32)], (own_sums, core_sums), 0, vmem=8, after=(head_b[0],)
    )
    rates = cross(rates)
    joined, qk_rows, up_kept, gate_kept = attend_back(
        me_ref, [head_a[0], head_b[0]], [core_head_a, core_head_b], q_far, k_far, v_far, head_out, inv, qi, ki,
        seg_k, seg_q, gain, cos_far, sin_far, load=[(grad_up[1], ()), (grad_gate[1], ())],
        after=(pair_sums,),
    )

    def attn_rows(array, half):
        return (array, (slice(half * part, (half + 1) * part), slice(0, depth)), False)

    if fast:
        lines = run_whole(
            table_kernel, [struct((n_dp, 2 * size), F32)] * 2, (pair_sums, rates), 0, vmem=8, after=(qk_rows,)
        )
    else:
        rates = pair_sums[2:4] + rates
        pairs = [(pair_sums[0], pair_sums[1] * math.sqrt(depth)), (rates[0], rates[1])]
        lines = [jnp.concatenate([x.reshape(n_dp, -1) for x in pair], axis=1) for pair in pairs]
    if not fast:
        qk_rows = qk_rows[:, :HALF].reshape(n_dp, -1)
    give_far, far, give, own = input_grad(joined, *weights, (qk_rows,), ())
    up_sent, up_kept = add((up_kept, up_got), (own,))
    gate_sent, gate_kept = add((gate_kept, gate_got), (up_sent,))
    up_sent, gate_sent, give_far, token = hold([up_sent, gate_sent, give_far], ())
    grad_up = (up_kept, over_dp(up_sent, dp_bits[1]))
    grad_gate = (gate_kept, over_dp(gate_sent, later_bits[1]))
    far_got = core(give_far)
    token_rows = [whole(tokens, True), whole(core_tokens, True), whole(far_tokens, True), whole(cross_tokens, True)]
    first, second, own, give = weight_grad(
        [
            (
                [attn_rows(x, half) for pair in ((head_give, head_b[1]), (core_head_a, core_head_b))
                 for half in range(2) for x in pair],
                [layer(head_out, slot) for slot in (0, 2, 1, 3)],
            ),
            (token_rows, [layer(joined, slot) for slot in range(4)]),
        ],
        [(dp_bits, 2 * width + width // 2), (later_bits, 2 * width - width // 2)], vectors=(*lines, qk_rows), far_kept=False, after=(token,),
        carry=[own, give],
    )

    rest_bits = dp_bits[3:]
    feed_sent, feed_kept = combine([grad_up, grad_gate], (first[0],))
    far_sum = add_far(far, far_got, (feed_sent,))
    feed_sent, first_sent, second_sent, far_sum, down_got, token = hold(
        [feed_sent, first[0], second[0], far_sum, down[1]], ()
    )
    feeds = (feed_kept, over_dp(feed_sent, dp_bits[2]))
    first = (first[1], over_dp(first_sent, dp_bits[0]))
    second = (second[1], over_dp(second_sent, later_bits[0]))
    far_grad = cross(far_sum)
    (down,) = last_stage((down[0], down_got), rest_bits, [(0, size, 0, hidden_width, True)], (token,))

    first_sent, first_kept = add(first, (token,))
    second_sent, second_kept = add(second, (first_sent,))
    first_sent, second_sent, give, token = hold([first_sent, second_sent, give], ())
    first = (first_kept, over_dp(first_sent, dp_bits[1]))
    second = (second_kept, over_dp(second_sent, later_bits[1]))
    got = core(give)

    attn_sent, attn_kept = combine([first, second], (token,))
    attn = (attn_kept, over_dp(attn_sent, dp_bits[2]))
    late = (attn_kept,)
    grad_up, grad_gate = last_stage(
        feeds, rest_bits,
        [(0, size, 0, hidden_width, False), (0, size, hidden_width, hidden_width, False)], late,
    )
    short = width // n_dp
    grad_out, grad_query, grad_key, grad_value, scale_up, scale_gate, rate_attn, rate_mlp, scale_qk = last_stage(
        attn, rest_bits,
        [
            (0, size, 0, width, True), (0, size, width, width, False),
            (0, size, 2 * width, width, False), (0, size, 3 * width, width, False),
            (size, 1, 0, size, False), (size, 1, size, size, False),
            (size + 1, 1, 0, size, False), (size + 1, 1, size, size, False), (size + 2, 1, 0, short, False),
        ],
        late,
    )
    token_grad = rests + (own + got.astype(F32) + far_grad.astype(F32))
    return (
        block_out,
        token_grad,
        grad_query,
        grad_key,
        grad_value,
        grad_out,
        scale_qk[0],
        rate_attn[0],
        grad_up,
        grad_gate,
        scale_up[0],
        scale_gate[0],
        down,
        rate_mlp[0],
    )


def solution(mesh):
    in_specs = (
        P(("dp", "mp"), None),
        P("dp", None),
        P(None, "mp"),
        P(None, "mp"),
        P(None, "mp"),
        P("mp", None),
        P("mp"),
        P(),
        P(None, "mp"),
        P(None, "mp"),
        P("mp"),
        P("mp"),
        P("mp", None),
        P(),
        P(("dp", "mp"), None),
    )
    out_specs = (
        P(("dp", "mp"), None),
        P(("dp", "mp"), None),
        P("dp", "mp"),
        P("dp", "mp"),
        P("dp", "mp"),
        P("mp", "dp"),
        P(("mp", "dp")),
        P("dp"),
        P("dp", "mp"),
        P("dp", "mp"),
        P(("mp", "dp")),
        P(("mp", "dp")),
        P("mp", "dp"),
        P("dp"),
    )
    return jax.shard_map(shards, mesh=mesh, in_specs=in_specs, out_specs=out_specs, check_vma=False)
```
